32 devices in a mesh: dp: 16 (over z, y, core), tensor: 2 (over x).
Axes of the slice: x: 2, y: 2, z: 4, core: 2. Of those that a mesh axis runs over, the one named last changes fastest.
Arguments:
- inputs: bfloat16 [16384, 768], P(('dp', 'tensor')), may hold values from -6 to 6
- upstream: bfloat16 [16384, 768], P(('dp', 'tensor')), may hold values from -6 to 6
- lengths: int32 [16, 8], P('dp'), may hold values from 1 to 512, 1024 in all within a row
- query_weight: bfloat16 [768, 768], P(None, 'tensor'), may hold values from -0.21875 to 0.21875
- key_weight: bfloat16 [768, 768], P(None, 'tensor'), may hold values from -0.21875 to 0.21875
- value_weight: bfloat16 [768, 768], P(None, 'tensor'), may hold values from -0.21875 to 0.21875
- query_bias: bfloat16 [768], P('tensor'), may hold values from -3 to 3
- value_bias: bfloat16 [768], P('tensor'), may hold values from -3 to 3
- mix_weight: bfloat16 [768, 768], P('tensor'), may hold values from -0.875 to 0.875
- mix_bias: bfloat16 [768], replicated, may hold values from -3 to 3
- mid_gain: bfloat16 [768], replicated, may hold values from 0.5 to 1.5
- mid_shift: bfloat16 [768], replicated, may hold values from -3 to 3
- up_weight: bfloat16 [768, 3072], P(None, 'tensor'), may hold values from -0.21875 to 0.21875
- up_bias: bfloat16 [3072], P('tensor'), may hold values from -3 to 3
- down_weight: bfloat16 [3072, 768], P('tensor'), may hold values from -0.109375 to 0.109375
- down_bias: bfloat16 [768], replicated, may hold values from -3 to 3
- end_gain: bfloat16 [768], replicated, may hold values from 0.5 to 1.5
- end_shift: bfloat16 [768], replicated, may hold values from -3 to 3
Outputs:
- outputs: bfloat16 [16384, 768], P(('dp', 'tensor'))
- input_grad: bfloat16 [16384, 768], P(('dp', 'tensor'))
- query_weight_grad: float32 [768, 768], P(None, 'tensor')
- key_weight_grad: float32 [768, 768], P(None, 'tensor')
- value_weight_grad: float32 [768, 768], P(None, 'tensor')
- query_bias_grad: float32 [768], P('tensor')
- value_bias_grad: float32 [768], P('tensor')
- mix_weight_grad: float32 [768, 768], P('tensor')
- mix_bias_grad: float32 [768], replicated
- mid_gain_grad: float32 [768], replicated
- mid_shift_grad: float32 [768], replicated
- up_weight_grad: float32 [768, 3072], P(None, 'tensor')
- up_bias_grad: float32 [3072], P('tensor')
- down_weight_grad: float32 [3072, 768], P('tensor')
- down_bias_grad: float32 [768], replicated
- end_gain_grad: float32 [768], replicated
- end_shift_grad: float32 [768], replicated
The draws below stay inside these ranges and needn't reach their ends.
Inputs may be any that keep to these rules, and one draw needn't show every extreme that they name: The 8 lengths of a row sum to 1024, and the longest is 512.
All inputs are finite; a program needn't handle non-finite values.
Results may differ from the reference program's by a relative error of at most 0.017.
Values may be sent and summed in bfloat16 or wider, within the bound.
No kernel may reach another device: no remote copies, remote signals or barrier semaphores. Data moves between devices by JAX's collectives and lax.ppermute only.
A program may use at most 192 MiB of HBM per device.

```python
import math
import jax
import jax.numpy as jnp
import numpy as np
from jax import lax

D = 768
HEADS = 12
HEAD_DIM = 64
FF = 3072
SEQ = 1024
PASS = 8
ROWS = 16
TOKENS = 16384


def level_of(rng, shape, shards, least, top_value):
    factor_of, own = 1.0, jax.random.fold_in(rng, 6)
    for position, shards_of in shards:
        heights = jnp.exp(jax.random.uniform(jax.random.fold_in(own, position), (shards_of,), jnp.float32, least / len(shards), top_value / len(shards)))
        factor_of = factor_of * jnp.repeat(heights, shape[position] // shards_of).reshape([-1 if axis == position else 1 for axis in range(len(shape))])
    return factor_of


def split_up(count, total, reach, slope):
    loads = [(1 << 20) // math.isqrt(rank ** slope) + 1 for rank in range(2, count + 1)]
    spare, holding = total - reach - (count - 1), [1] * (count - 1)
    while spare > 0:
        candidates = [i for i in range(count - 1) if holding[i] < reach]
        pool, budget = sum([loads[i] for i in candidates]), spare
        for i in candidates:
            extra = min(reach - holding[i], max(1, budget * loads[i] // pool), spare)
            holding[i] = holding[i] + extra
            spare = spare - extra
    return np.array([reach] + holding)


def uneven(key, count, total, limit, skew):
    if count == 2:
        one = jax.random.randint(key, (), max(1, total - limit), min(limit, total - 1) + 1)
        return jnp.stack([one, total - one])
    tallies = jnp.asarray(split_up(count, total, limit, skew), jnp.int32)
    couples = (count - 1) // 2
    source_of, sink = tallies[1:1 + 2 * couples:2], tallies[2:2 + 2 * couples:2]
    room = jnp.minimum(source_of - 1, limit - sink)
    moved = jax.random.randint(jax.random.fold_in(key, 1), (couples,), 0, 1 << 20) % (room + 1)
    tallies = tallies.at[1:1 + 2 * couples:2].set(source_of - moved).at[2:2 + 2 * couples:2].set(sink + moved)
    return tallies[jax.random.permutation(jax.random.fold_in(key, 2), count)]


def gaussian(rng, shape, scale, bound, split=(), held_as=jnp.bfloat16):
    level = level_of(rng, shape, split, -0.22, 0.18) if split else 1.0
    entries = jax.random.normal(rng, shape, jnp.float32) * scale * level
    return jnp.minimum(jnp.maximum(entries, -bound), bound).astype(held_as)


def setup_inputs(seed: int = 0) -> dict:
    splits = jax.random.split(jax.random.key(seed), 19)
    return {
        "inputs": gaussian(splits[0], (TOKENS, D), 1.0, 6.0, ((0, 32),)),
        "upstream": gaussian(splits[1], (TOKENS, D), 1.0, 6.0, ((0, 32),)),
        "lengths": jax.vmap(lambda own: uneven(own, PASS, SEQ, SEQ // 2, 2))(jax.random.split(splits[2], ROWS)).reshape((ROWS, PASS)).astype(jnp.int32),
        "query_weight": gaussian(splits[3], (D, D), D ** -0.5, 0.21875, ((1, 2),)),
        "key_weight": gaussian(splits[4], (D, D), D ** -0.5, 0.21875, ((1, 2),)),
        "value_weight": gaussian(splits[5], (D, D), D ** -0.5, 0.21875, ((1, 2),)),
        "query_bias": gaussian(splits[6], (D,), 0.5, 3.0, ((0, 2),)),
        "value_bias": gaussian(splits[7], (D,), 0.5, 3.0, ((0, 2),)),
        "mix_weight": gaussian(splits[8], (D, D), (D // 16) ** -0.5, 0.875, ((0, 2),)),
        "mix_bias": gaussian(splits[9], (D,), 0.5, 3.0),
        "mid_gain": jnp.clip(1.0 + 0.1 * jax.random.normal(splits[10], (D,), jnp.float32), 0.5, 1.5).astype(jnp.bfloat16),
        "mid_shift": gaussian(splits[11], (D,), 0.5, 3.0),
        "up_weight": gaussian(splits[12], (D, FF), D ** -0.5, 0.21875, ((1, 2),)),
        "up_bias": gaussian(splits[13], (FF,), 0.5, 3.0, ((0, 2),)),
        "down_weight": gaussian(splits[14], (FF, D), FF ** -0.5, 0.109375, ((0, 2),)),
        "down_bias": gaussian(splits[15], (D,), 0.5, 3.0),
        "end_gain": jnp.clip(1.0 + 0.1 * jax.random.normal(splits[16], (D,), jnp.float32), 0.5, 1.5).astype(jnp.bfloat16),
        "end_shift": gaussian(splits[17], (D,), 0.5, 3.0),
    }


@jax.custom_vjp
def low(v):
    return lax.optimization_barrier(v.astype(jnp.bfloat16)).astype(jnp.float32)

@jax.custom_vjp
def low_back(v):
    return v

def low_keep(v):
    return (low(v), None)

def low_pass(kept, grad):
    return (grad,)

def back_keep(v):
    return (v, None)

def back_low(kept, grad):
    return (low(grad),)
low.defvjp(low_keep, low_pass)
low_back.defvjp(back_keep, back_low)
highest = lax.Precision.HIGHEST

def project(left, right):
    return jnp.einsum('gsd,de->gse', left, right, precision=highest)

def normalize(resid, gain, shift):
    middle = lax.optimization_barrier(jnp.mean(resid, axis=-1, keepdims=True))
    centered = resid - middle
    spread = lax.optimization_barrier(jnp.mean(centered * centered, axis=-1, keepdims=True))
    return centered * lax.rsqrt(spread + 1e-06) * gain + shift

def segment_ids(lengths):
    positions = jnp.arange(SEQ, dtype=jnp.int32)
    ends = jnp.cumsum(lengths, axis=-1).astype(jnp.int32)
    hits = (positions[None, :, None] >= ends[:, None, :]).astype(jnp.int32)
    return lax.optimization_barrier(jnp.sum(hits, axis=-1)).astype(jnp.int32)

def attend_row(pieces):
    query, keys, values, segs = pieces
    scores = jnp.einsum('qhd,khd->hqk', query, keys, precision=highest) * 0.125
    scores = low_back(scores)
    same = segs[:, None] == segs[None, :]
    scores = jnp.where(same[None], scores, -1e+30)
    probs = low(jax.nn.softmax(scores, axis=-1))
    return jnp.einsum('hqk,khd->qhd', probs, values, precision=highest)

def layer(params, inputs, segs):
    query_weight, key_weight, value_weight, query_bias, value_bias, mix_weight, mix_bias, mid_gain, mid_shift, up_weight, up_bias, down_weight, down_bias, end_gain, end_shift = params
    group = inputs.shape[0]
    inputs_low = low(inputs)
    query = low(low_back(project(inputs_low, query_weight)) + query_bias)
    keys = low(low_back(project(inputs_low, key_weight)))
    values = low(low_back(project(inputs_low, value_weight)) + value_bias)
    shape = (group, SEQ, HEADS, HEAD_DIM)
    heads_out = lax.map(jax.checkpoint(attend_row), (query.reshape(shape), keys.reshape(shape), values.reshape(shape), segs))
    context = low(low_back(heads_out)).reshape(group, SEQ, D)
    attended = low_back(project(context, mix_weight)) + mix_bias
    normed = normalize(inputs + attended, mid_gain, mid_shift)
    pre = low_back(project(low(normed), up_weight)) + up_bias
    active = low(jax.nn.gelu(pre, approximate=False))
    branch = low_back(project(active, down_weight)) + down_bias
    return normalize(normed + branch, end_gain, end_shift)

def reference(inputs, upstream, lengths, query_weight, key_weight, value_weight, query_bias, value_bias, mix_weight, mix_bias, mid_gain, mid_shift, up_weight, up_bias, down_weight, down_bias, end_gain, end_shift):
    params = tuple((w.astype(jnp.float32) for w in (query_weight, key_weight, value_weight, query_bias, value_bias, mix_weight, mix_bias, mid_gain, mid_shift, up_weight, up_bias, down_weight, down_bias, end_gain, end_shift)))
    group = math.gcd(ROWS, max(1, 4096 // SEQ))
    steps_count = ROWS // group
    xs = inputs.astype(jnp.float32).reshape(steps_count, group, SEQ, D)
    gs = upstream.astype(jnp.float32).reshape(steps_count, group, SEQ, D)
    ls = lengths.reshape(steps_count, group, PASS)

    def step(totals, batch):
        xrows, grows, lrows = batch
        segs = segment_ids(lrows)
        result, pull = jax.vjp(lambda p, v: layer(p, v, segs), params, xrows)
        grads, xgrad = pull(grows)
        totals = jax.tree.map(lambda a, b: a + b, totals, grads)
        return (totals, (result, xgrad))
    start = jax.tree.map(jnp.zeros_like, params)
    grads, (results, xgrads) = lax.scan(step, start, (xs, gs, ls))
    outputs = results.reshape(TOKENS, D).astype(jnp.bfloat16)
    input_grad = xgrads.reshape(TOKENS, D).astype(jnp.bfloat16)
    return (outputs, input_grad, grads[0], grads[1], grads[2], grads[3], grads[4], grads[5], grads[6], grads[7], grads[8], grads[9], grads[10], grads[11], grads[12], grads[13], grads[14])
```

```python
from functools import partial

import jax
import jax.numpy as jnp
from jax import lax
from jax.experimental import pallas as pl
from jax.experimental.pallas import tpu as pltpu
from jax.sharding import PartitionSpec as P

HEAD_DIM = 64
PAIR = 128
SEQ = 1024
LOW = jnp.bfloat16
F32 = jnp.float32
FAR = -1e30


def nt(a, b):
    return lax.dot_general(a, b, (((1,), (1,)), ((), ())), preferred_element_type=F32)


def tn(a, b):
    return lax.dot_general(a, b, (((0,), (0,)), ((), ())), preferred_element_type=F32)


def nn(a, b):
    return lax.dot_general(a, b, (((1,), (0,)), ((), ())), preferred_element_type=F32)


def seg_ends(len_ref):
    ends, total = [], jnp.int32(0)
    for j in range(len_ref.shape[1]):
        total = total + len_ref[0, j]
        ends.append(total)
    return ends


def seg_marks(ends, shift):
    pos = (lax.broadcasted_iota(jnp.int32, (SEQ, PAIR), 0) + shift) & (SEQ - 1)
    lane = lax.broadcasted_iota(jnp.int32, (SEQ, PAIR), 1) & (HEAD_DIM - 1)
    seg = jnp.zeros((SEQ, PAIR), jnp.int32)
    for e in ends:
        seg = seg + (pos >= e).astype(jnp.int32)
    own = seg == lane
    used = lane < len(ends)
    key_mark = jnp.where(own, 1.0, 0.0)
    query_mark = jnp.where(used & jnp.logical_not(own), FAR, 0.0)
    return key_mark, query_mark


def key_range(ends, first, size, step):
    begin, stop = jnp.int32(0), jnp.int32(SEQ)
    for e in ends:
        begin = jnp.where(e <= first, e, begin)
    for e in reversed(ends):
        stop = jnp.where(e >= first + size, e, stop)
    return (begin // step) * step, stop


def head_mask(h):
    lane = lax.broadcasted_iota(jnp.int32, (1, PAIR), 1)
    return (lane >= h * HEAD_DIM) & (lane < (h + 1) * HEAD_DIM)


def over_queries(ends, shift, bq, bk, step, body):
    most = -(-SEQ // bk)

    def one(t, _):
        q_at = pl.multiple_of(t * bq, bq)
        q_pos = (q_at + shift) & (SEQ - 1)
        begin, stop = key_range(ends, q_pos, bq, step)
        count = (stop - begin + bk - 1) // bk
        begin = jnp.minimum(begin, SEQ - count * bk)
        begin = pl.multiple_of(begin, step)
        for n in range(1, most + 1):

            @pl.when(count == n)
            def _():
                body(q_at, begin, n)

        return 0

    lax.fori_loop(0, SEQ // bq, one, 0)


def true_order(dst, src, shift):
    half = SEQ // 2
    dst[pl.ds(pl.multiple_of(shift, half), half), :] = src[:half]
    dst[pl.ds(pl.multiple_of(half - shift, half), half), :] = src[half:]


def both(own_ref, got_ref, at, pair):
    cols = slice(at + pair * PAIR, at + (pair + 1) * PAIR)
    return jnp.concatenate([own_ref[:, cols], got_ref[:, cols]], axis=0)


def attend_kernel(bq, bk, step, ahead, len_ref, side_ref, own_ref, got_ref, ctx_ref, lse_ref, qh, kh, vt, acc, tot):
    shift = side_ref[0] * (SEQ // 2)
    half = SEQ // 2
    ends = seg_ends(len_ref)
    key_mark, query_mark = seg_marks(ends, shift)
    width = own_ref.shape[1] // 3
    heads = width // HEAD_DIM
    for p in range(heads // 2):
        cols = slice(p * PAIR, (p + 1) * PAIR)
        q = both(own_ref, got_ref, 0, p).astype(F32) * 0.125
        k = both(own_ref, got_ref, width, p).astype(F32)
        for h in range(2):
            qh[2 * p + h] = jnp.where(head_mask(h), q, query_mark).astype(LOW)
            true_order(kh.at[2 * p + h], jnp.where(head_mask(h), k, key_mark).astype(LOW), shift)
        vals = jnp.transpose(both(own_ref, got_ref, 2 * width, p).astype(F32)).astype(LOW)
        vt[cols, pl.ds(pl.multiple_of(shift, half), half)] = vals[:, :half]
        vt[cols, pl.ds(pl.multiple_of(half - shift, half), half)] = vals[:, half:]

    def body(q_at, begin, n):
        qs = pl.ds(q_at, bq)
        at = [pl.ds(pl.multiple_of(begin + i * bk, step), bk) for i in range(n)]

        def score(h):
            query = qh[h, qs, :]
            return [nt(kh[h, at[i], :], query) for i in range(n)]

        ready = [score(h) for h in range(ahead)]
        for h in range(heads):
            dims = slice(h * HEAD_DIM, (h + 1) * HEAD_DIM)
            if h + ahead < heads:
                ready.append(score(h + ahead))
            parts = ready[h]
            top = jnp.max(parts[0], axis=0, keepdims=True)
            for s in parts[1:]:
                top = jnp.maximum(top, jnp.max(s, axis=0, keepdims=True))
            total, out = 0.0, 0.0
            for i, s in enumerate(parts):
                p = jnp.exp(s - top)
                total = total + jnp.sum(p, axis=0, keepdims=True)
                out = out + nn(vt[dims, at[i]], p.astype(LOW))
            acc[dims, qs] = out * (1.0 / total)
            tot[h : h + 1, qs] = top + jnp.log(total)

    over_queries(ends, shift, bq, bk, step, body)
    ctx_ref[...] = jnp.transpose(acc[...]).astype(LOW)
    lse_ref[...] = tot[...]


def attend(lengths, side, own, got, bq=256, bk=256, step=128, ahead=2):
    width = own.shape[1] // 3
    heads = width // HEAD_DIM
    assert heads <= 8
    smem = pl.BlockSpec(memory_space=pltpu.SMEM)
    vmem = pl.BlockSpec(memory_space=pltpu.VMEM)
    return pl.pallas_call(
        partial(attend_kernel, bq, bk, step, ahead),
        in_specs=[smem, smem, vmem, vmem],
        out_specs=[vmem, vmem],
        out_shape=[
            jax.ShapeDtypeStruct((SEQ, width), LOW),
            jax.ShapeDtypeStruct((8, SEQ), F32),
        ],
        scratch_shapes=[
            pltpu.VMEM((heads, SEQ, PAIR), LOW),
            pltpu.VMEM((heads, SEQ, PAIR), LOW),
            pltpu.VMEM((width, SEQ), LOW),
            pltpu.VMEM((width, SEQ), F32),
            pltpu.VMEM((8, SEQ), F32),
        ],
        compiler_params=pltpu.CompilerParams(vmem_limit_bytes=32 * 1024 * 1024),
        name="attend",
    )(lengths, side, own, got)


def attend_back_kernel(
    bq, bk, step, ahead, len_ref, side_ref, own_ref, got_ref, do_own_ref, do_got_ref, ctx_ref, lse_ref,
    g_ref, bias_ref, qh, qz, dom, kh, vals, kt, inner, dqt, dk, dv,
):
    shift = side_ref[0] * (SEQ // 2)
    half = SEQ // 2
    ends = seg_ends(len_ref)
    key_mark, query_mark = seg_marks(ends, shift)
    width = own_ref.shape[1] // 3
    heads = width // HEAD_DIM
    first = pl.ds(pl.multiple_of(shift, half), half)
    second = pl.ds(pl.multiple_of(half - shift, half), half)
    for p in range(heads // 2):
        cols = slice(p * PAIR, (p + 1) * PAIR)
        q = both(own_ref, got_ref, 0, p).astype(F32) * 0.125
        k = both(own_ref, got_ref, width, p).astype(F32)
        do = both(do_own_ref, do_got_ref, 0, p).astype(F32)
        for h in range(2):
            mask = head_mask(h)
            at = 2 * p + h
            qh[at] = jnp.where(mask, q, query_mark).astype(LOW)
            qz[at] = jnp.where(mask, q, 0.0).astype(LOW)
            dom[at] = jnp.where(mask, do, 0.0).astype(LOW)
            true_order(kh.at[at], jnp.where(mask, k, key_mark).astype(LOW), shift)
        true_order(vals.at[p], both(own_ref, got_ref, 2 * width, p), shift)
        turned = jnp.transpose(k).astype(LOW)
        kt[cols, first] = turned[:, :half]
        kt[cols, second] = turned[:, half:]
        prod = jnp.transpose(do * ctx_ref[:, cols].astype(F32))
        for h in range(2):
            inner[2 * p + h : 2 * p + h + 1, :] = jnp.sum(
                prod[h * HEAD_DIM : (h + 1) * HEAD_DIM], axis=0, keepdims=True
            )
    dk[...] = jnp.zeros_like(dk)
    dv[...] = jnp.zeros_like(dv)

    def body(q_at, begin, n):
        qs = pl.ds(q_at, bq)
        at = [pl.ds(pl.multiple_of(begin + i * bk, step), bk) for i in range(n)]

        def score(h):
            query, grad = qh[h, qs, :], dom[h, qs, :]
            return [(nt(kh[h, at[i], :], query), nt(vals[h // 2, at[i], :], grad)) for i in range(n)]

        ready = [score(h) for h in range(ahead)]
        for h in range(heads):
            if h + ahead < heads:
                ready.append(score(h + ahead))
            dims = slice(h * HEAD_DIM, (h + 1) * HEAD_DIM)
            plain, grad = qz[h, qs, :], dom[h, qs, :]
            lse, mean = lse_ref[h : h + 1, qs], inner[h : h + 1, qs]
            out = 0.0
            for i, (s, gp) in enumerate(ready[h]):
                p = jnp.exp(s - lse)
                ds = (p * (gp - mean)).astype(LOW)
                dv[h // 2, at[i], :] += nn(p.astype(LOW), grad)
                dk[h // 2, at[i], :] += nn(ds, plain)
                out = out + nn(kt[dims, at[i]], ds)
            dqt[dims, qs] = out

    over_queries(ends, shift, bq, bk, step, body)
    gq = jnp.transpose(dqt[...]) * 0.125
    g_ref[:, :width] = gq.astype(LOW)
    bias_ref[0:1, :] = jnp.sum(gq, axis=0, keepdims=True)
    for p in range(heads // 2):
        cols = slice(p * PAIR, (p + 1) * PAIR)
        for at, src in ((width + p * PAIR, dk), (2 * width + p * PAIR, dv)):
            g_ref[:half, at : at + PAIR] = src[p, first, :].astype(LOW)
            g_ref[half:, at : at + PAIR] = src[p, second, :].astype(LOW)
        bias_ref[1:2, cols] = jnp.sum(dv[p], axis=0, keepdims=True)


def attend_back(lengths, side, own, got, g_own, g_got, context, lse, bq=256, bk=256, step=128, ahead=1):
    width = own.shape[1] // 3
    heads = width // HEAD_DIM
    smem = pl.BlockSpec(memory_space=pltpu.SMEM)
    vmem = pl.BlockSpec(memory_space=pltpu.VMEM)
    return pl.pallas_call(
        partial(attend_back_kernel, bq, bk, step, ahead),
        in_specs=[smem, smem] + [vmem] * 6,
        out_specs=[vmem] * 2,
        out_shape=[
            jax.ShapeDtypeStruct((SEQ, 3 * width), LOW),
            jax.ShapeDtypeStruct((8, width), F32),
        ],
        scratch_shapes=[
            pltpu.VMEM((heads, SEQ, PAIR), LOW),
            pltpu.VMEM((heads, SEQ, PAIR), LOW),
            pltpu.VMEM((heads, SEQ, PAIR), LOW),
            pltpu.VMEM((heads, SEQ, PAIR), LOW),
            pltpu.VMEM((heads // 2, SEQ, PAIR), LOW),
            pltpu.VMEM((width, SEQ), LOW),
            pltpu.VMEM((8, SEQ), F32),
            pltpu.VMEM((width, SEQ), F32),
            pltpu.VMEM((heads // 2, SEQ, PAIR), F32),
            pltpu.VMEM((heads // 2, SEQ, PAIR), F32),
        ],
        compiler_params=pltpu.CompilerParams(vmem_limit_bytes=48 * 1024 * 1024),
        name="attend_back",
    )(lengths, side, own, got, g_own, g_got, context, lse)


MIB = 1024 * 1024
VEC = ("mix_bias", "mid_gain", "mid_shift", "down_bias", "end_gain", "end_shift")


def unit_norm(resid):
    middle = jnp.mean(resid, axis=-1, keepdims=True)
    centered = resid - middle
    spread = jnp.mean(centered * centered, axis=-1, keepdims=True)
    scaled = lax.rsqrt(spread + 1e-06)
    return centered * scaled, scaled


def norm_back(grad, unit, scaled, gain):
    weighted = grad * gain
    first_mean = jnp.mean(weighted, axis=-1, keepdims=True)
    second_mean = jnp.mean(weighted * unit, axis=-1, keepdims=True)
    return scaled * (weighted - first_mean - unit * second_mean)


def gelu_pair(v):
    t = 1.0 / (1.0 + (0.3275911 * 0.7071067811865476) * jnp.abs(v))
    bell = jnp.exp(-0.5 * v * v)
    poly = t * (0.5 * 1.061405429)
    poly = t * (poly - 0.5 * 1.453152027)
    poly = t * (poly + 0.5 * 1.421413741)
    poly = t * (poly - 0.5 * 0.284496736)
    poly = t * (poly + 0.5 * 0.254829592)
    tail = poly * bell
    cdf = jnp.where(v >= 0, 1.0 - tail, tail)
    return v * cdf, cdf + (v * 0.3989422804014327) * bell


def rows_sum(v):
    return jnp.sum(v, axis=0, keepdims=True)


def token_kernel(
    tile, ctx_a, ctx_b, x_ref, e_ref, vec_ref, mix_a, mix_b, up_a, up_b0, up_b1, up_bias, down_a, down_b0, down_b1,
    out_ref, g_first_ref, g_ctx_a, g_ctx_b, act_ref, g_pre_ref, normed_ref, g_branch_ref, g_att_ref, sum_ref,
    slope,
):
    hidden = up_b0.shape[1]
    ups = [up_a.at[:, :hidden], up_a.at[:, hidden:], up_b0, up_b1]
    downs = [down_a.at[:hidden], down_a.at[hidden:], down_b0, down_b1]
    count = len(ups)
    mix_bias, mid_gain, mid_shift, down_bias, end_gain, end_shift = (vec_ref[i : i + 1, :] for i in range(6))
    sum_ref[...] = jnp.zeros_like(sum_ref)

    def add(row, value):
        sum_ref[row : row + 1, :] += rows_sum(value)

    def one(r, _):
        rows = pl.ds(pl.multiple_of(r * tile, tile), tile)
        context_a, context_b = ctx_a[rows, :], ctx_b[rows, :]
        attended = nn(context_a, mix_a[...]) + nn(context_b, mix_b[...])
        unit_one, scaled_one = unit_norm(x_ref[rows, :].astype(F32) + attended + mix_bias)
        normed = unit_one * mid_gain + mid_shift
        low = normed.astype(LOW)
        normed_ref[rows, :] = low

        def pre(j):
            return nn(low, ups[j][...]) + up_bias[j : j + 1, :]

        branch = normed + down_bias
        ahead = pre(0)
        for j in range(count):
            value, ahead = ahead, (pre(j + 1) if j + 1 < count else None)
            active, incline = gelu_pair(value)
            active = active.astype(LOW)
            act_ref[j, rows, :] = active
            slope[j] = incline.astype(LOW)
            branch = branch + nn(active, downs[j][...])
        unit_two, scaled_two = unit_norm(branch)
        out_ref[rows, :] = (unit_two * end_gain + end_shift).astype(LOW)
        e = e_ref[rows, :].astype(F32)
        add(4, e * unit_two)
        add(5, e)
        g_second = norm_back(e, unit_two, scaled_two, end_gain)
        add(3, g_second)
        g_branch = g_second.astype(LOW)
        g_branch_ref[rows, :] = g_branch

        def g_active(j):
            return nt(g_branch, downs[j][...])

        g_normed = g_second
        ahead = g_active(0)
        for j in range(count):
            value, ahead = ahead, (g_active(j + 1) if j + 1 < count else None)
            g_pre = value * slope[j].astype(F32)
            add(6 + j, g_pre)
            g_pre = g_pre.astype(LOW)
            g_pre_ref[j, rows, :] = g_pre
            g_normed = g_normed + nt(g_pre, ups[j][...])
        add(1, g_normed * unit_one)
        add(2, g_normed)
        g_first = norm_back(g_normed, unit_one, scaled_one, mid_gain)
        add(0, g_first)
        g_first_ref[rows, :] = g_first
        g_att = g_first.astype(LOW)
        g_att_ref[rows, :] = g_att
        g_ctx_a[rows, :] = nt(g_att, mix_a[...]).astype(LOW)
        g_ctx_b[rows, :] = nt(g_att, mix_b[...]).astype(LOW)
        return 0

    lax.fori_loop(0, x_ref.shape[0] // tile, one, 0)


def token_part(ctx_a, ctx_b, x, e, vec, mix_a, mix_b, up_a, up_b, up_bias, down_a, down_b, tile=256):
    tokens, width = x.shape
    part = ctx_a.shape[1]
    hidden = up_b[0].shape[1]
    vmem = pl.BlockSpec(memory_space=pltpu.VMEM)
    sds = jax.ShapeDtypeStruct
    full, half = sds((tokens, width), LOW), sds((tokens, part), LOW)
    flops = 2 * tokens * width * (2 * width + 4 * 4 * hidden)
    return pl.pallas_call(
        partial(token_kernel, tile),
        in_specs=[vmem] * 14,
        out_specs=[vmem] * 10,
        out_shape=[
            full, sds((tokens, width), F32), half, half,
            sds((4, tokens, hidden), LOW), sds((4, tokens, hidden), LOW),
            full, full, full, sds((16, width), F32),
        ],
        scratch_shapes=[pltpu.VMEM((4, tile, hidden), LOW)],
        compiler_params=pltpu.CompilerParams(vmem_limit_bytes=50 * MIB),
        cost_estimate=pl.CostEstimate(flops=flops, bytes_accessed=24 * MIB, transcendentals=4 * tokens * hidden),
        name="token_part",
    )(ctx_a, ctx_b, x, e, vec, mix_a, mix_b, up_a, up_b[0], up_b[1], up_bias, down_a, down_b[0], down_b[1])


def weight_kernel(pick_ref, act_ref, g_pre_ref, normed_ref, g_branch_ref, out_ref):
    out_ref[0, 0] = tn(normed_ref[...], g_pre_ref[0]).astype(LOW)
    out_ref[0, 1] = tn(act_ref[0], g_branch_ref[...]).astype(LOW)


def weight_part(pick, act, g_pre, normed, g_branch):
    _, tokens, hidden = act.shape
    width = normed.shape[1]
    chunk = pl.BlockSpec((1, tokens, hidden), lambda i, pick: (pick[i], 0, 0))
    fixed = pl.BlockSpec((tokens, width), lambda i, pick: (0, 0))
    return pl.pallas_call(
        weight_kernel,
        grid_spec=pltpu.PrefetchScalarGridSpec(
            num_scalar_prefetch=1,
            grid=(2,),
            in_specs=[chunk, chunk, fixed, fixed],
            out_specs=pl.BlockSpec((1, 2, width, hidden), lambda i, pick: (i, 0, 0, 0)),
        ),
        out_shape=jax.ShapeDtypeStruct((2, 2, width, hidden), LOW),
        compiler_params=pltpu.CompilerParams(vmem_limit_bytes=32 * MIB),
        cost_estimate=pl.CostEstimate(flops=8 * tokens * width * hidden, bytes_accessed=9 * MIB, transcendentals=0),
        name="weight_part",
    )(pick, act, g_pre, normed, g_branch)


def swap(value, axis, bit):
    size = lax.axis_size(axis)
    return lax.ppermute(value, axis, [(i, i ^ bit) for i in range(size)])


def wide(value):
    return value.astype(F32)


def cut(value, at, size):
    return lax.dynamic_slice_in_dim(value, at, size, 0)


def halve(value, dp, bit):
    half = value.shape[0] // 2
    mine = ((dp & bit) != 0).astype(jnp.int32)
    got = swap(cut(value, (1 - mine) * half, half), "dp", bit)
    return (wide(cut(value, mine * half, half)) + wide(got)).astype(value.dtype)


def join(value, dp, bit):
    got = swap(value, "dp", bit)
    return jnp.where(
        (dp & bit) != 0, jnp.concatenate([got, value]), jnp.concatenate([value, got])
    )


def dp_bits():
    return [1 << i for i in range(lax.axis_size("dp").bit_length() - 1)]


def sum_small(value, bits):
    for bit in bits:
        value = value + swap(value, "dp", bit)
    return value


def per_device(
    inputs, upstream, lengths, query_weight, key_weight, value_weight, query_bias, value_bias, mix_weight, mix_bias,
    mid_gain, mid_shift, up_weight, up_bias, down_weight, down_bias, end_gain, end_shift,
):
    dp = lax.axis_index("dp")
    side = lax.axis_index("tensor")
    core = dp & 1
    tokens, width = inputs.shape
    part = query_weight.shape[1]
    hidden = up_weight.shape[1] // 2
    bits = dp_bits()
    x_got = swap(inputs, "tensor", 1)
    qkv_weight = jnp.concatenate([query_weight, key_weight, value_weight], axis=1)
    qkv_bias = jnp.concatenate([wide(query_bias), jnp.zeros((part,), F32), wide(value_bias)])

    def project(v):
        return (nn(v, qkv_weight) + qkv_bias).astype(LOW)

    mix_got = swap(mix_weight, "tensor", 1)
    bias_rows = up_bias.reshape(2, hidden)
    bias_got = swap(bias_rows, "tensor", 1)
    up_c = swap(lax.dynamic_slice_in_dim(up_weight, core * hidden, hidden, 1), "tensor", 1)
    down_c = swap(cut(down_weight, core * hidden, hidden), "tensor", 1)
    up_got = (up_c, swap(up_c, "dp", 1))
    down_got = (down_c, swap(down_c, "dp", 1))
    bias_got = jnp.where(core == 0, bias_got, bias_got[::-1])
    up_bias_all = wide(jnp.concatenate([bias_rows, bias_got]))
    vec = wide(jnp.stack([mix_bias, mid_gain, mid_shift, down_bias, end_gain, end_shift]))

    own, got = project(inputs), project(x_got)
    side_row = side.astype(jnp.int32).reshape(1)
    context, lse = attend(lengths, side_row, own, got)
    ctx_got = swap(context[tokens:], "tensor", 1)
    ctx_own = context[:tokens]
    (
        outputs, g_first, g_ctx_own, g_ctx_send, act, g_pre, normed, g_branch, g_att, sums,
    ) = token_part(
        ctx_own, ctx_got, inputs, upstream, vec, mix_weight, mix_got, up_weight, up_got, up_bias_all, down_weight, down_got
    )
    g_ctx_got = swap(g_ctx_send, "tensor", 1)
    two = jnp.int32(2)
    send = weight_part(jnp.stack([1 - core, two + 1]), act, g_pre, normed, g_branch)
    from_core = swap(send, "dp", 1)
    keep = weight_part(jnp.stack([core, two]), act, g_pre, normed, g_branch)
    mix_own, mix_send = tn(ctx_own, g_att).astype(LOW), tn(ctx_got, g_att).astype(LOW)
    mix_sum = (wide(mix_own) + wide(swap(mix_send, "tensor", 1))).astype(LOW)

    g_qkv, qkv_bias_grad = attend_back(lengths, side_row, own, got, g_ctx_own, g_ctx_got, context, lse)
    total = lax.dot_general(g_qkv, qkv_weight, (((1,), (1,)), ((), ())), preferred_element_type=F32)
    input_got = swap(total[tokens:].astype(LOW), "tensor", 1)
    input_grad = (g_first + total[:tokens] + wide(input_got)).astype(LOW)

    paired = (wide(keep) + wide(from_core)).astype(LOW)
    ffn = (wide(paired[0]) + wide(swap(paired[1], "tensor", 1))).astype(LOW)
    mix_half = halve(mix_sum, dp, 1)
    flat = jnp.concatenate([ffn.reshape(2 * width, hidden), mix_half])
    for bit in bits[1:]:
        flat = halve(flat, dp, bit)
    for bit in bits[:0:-1]:
        flat = join(flat, dp, bit)
    other = swap(flat, "dp", 1)
    first, second = jnp.where(core == 0, flat, other), jnp.where(core == 0, other, flat)
    up_grad = wide(jnp.concatenate([first[:width], second[:width]], axis=1))
    down_grad = wide(jnp.concatenate([first[width : 2 * width], second[width : 2 * width]]))
    mix_grad = wide(jnp.concatenate([first[2 * width :], second[2 * width :]]))

    whole = jnp.concatenate([inputs, x_got])
    qkv_grad = tn(whole, g_qkv).astype(LOW)
    for bit in bits:
        qkv_grad = halve(qkv_grad, dp, bit)
    for bit in bits[::-1]:
        qkv_grad = join(qkv_grad, dp, bit)
    qkv_grad = wide(qkv_grad)

    up_send = jnp.where(core == 0, sums[8:10], sums[9:7:-1])
    small = sums[:8] + swap(jnp.concatenate([sums[:6], up_send]), "tensor", 1)
    small = sum_small(small, bits)
    qkv_bias_grad = sum_small(qkv_bias_grad, bits)
    return (
        outputs,
        input_grad,
        qkv_grad[:, :part],
        qkv_grad[:, part : 2 * part],
        qkv_grad[:, 2 * part :],
        qkv_bias_grad[0],
        qkv_bias_grad[1],
        mix_grad,
        small[0],
        small[1],
        small[2],
        up_grad,
        small[6:8].reshape(2 * hidden),
        down_grad,
        small[3],
        small[4],
        small[5],
    )


def solution(mesh):
    placed = (
        P(("dp", "tensor"), None),
        P(("dp", "tensor"), None),
        P("dp", None),
        P(None, "tensor"),
        P(None, "tensor"),
        P(None, "tensor"),
        P("tensor"),
        P("tensor"),
        P("tensor", None),
        P(),
        P(),
        P(),
        P(None, "tensor"),
        P("tensor"),
        P("tensor", None),
        P(),
        P(),
        P(),
    )
    return jax.shard_map(
        per_device,
        mesh=mesh,
        in_specs=placed,
        out_specs=(
            P(("dp", "tensor"), None),
            P(("dp", "tensor"), None),
            P(None, "tensor"),
            P(None, "tensor"),
            P(None, "tensor"),
            P("tensor"),
            P("tensor"),
            P("tensor", None),
            P(),
            P(),
            P(),
            P(None, "tensor"),
            P("tensor"),
            P("tensor", None),
            P(),
            P(),
            P(),
        ),
        check_vma=False,
    )
```

```python
from functools import partial

import jax
import jax.numpy as jnp
from jax import lax
from jax.experimental import pallas as pl
from jax.experimental.pallas import tpu as pltpu
from jax.sharding import PartitionSpec as P

HEAD_DIM = 64
PAIR = 128
SEQ = 1024
LOW = jnp.bfloat16
F32 = jnp.float32
FAR = -1e30


def nt(a, b):
    return lax.dot_general(a, b, (((1,), (1,)), ((), ())), preferred_element_type=F32)


def tn(a, b):
    return lax.dot_general(a, b, (((0,), (0,)), ((), ())), preferred_element_type=F32)


def nn(a, b):
    return lax.dot_general(a, b, (((1,), (0,)), ((), ())), preferred_element_type=F32)


def seg_ends(len_ref):
    ends, total = [], jnp.int32(0)
    for j in range(len_ref.shape[1]):
        total = total + len_ref[0, j]
        ends.append(total)
    return ends


def seg_marks(ends, shift):
    pos = (lax.broadcasted_iota(jnp.int32, (SEQ, PAIR), 0) + shift) & (SEQ - 1)
    lane = lax.broadcasted_iota(jnp.int32, (SEQ, PAIR), 1) & (HEAD_DIM - 1)
    seg = jnp.zeros((SEQ, PAIR), jnp.int32)
    for e in ends:
        seg = seg + (pos >= e).astype(jnp.int32)
    own = seg == lane
    used = lane < len(ends)
    key_mark = jnp.where(own, 1.0, 0.0)
    query_mark = jnp.where(used & jnp.logical_not(own), FAR, 0.0)
    return key_mark, query_mark


def key_range(ends, first, size, step):
    begin, stop = jnp.int32(0), jnp.int32(SEQ)
    for e in ends:
        begin = jnp.where(e <= first, e, begin)
    for e in reversed(ends):
        stop = jnp.where(e >= first + size, e, stop)
    return (begin // step) * step, stop


def head_mask(h):
    lane = lax.broadcasted_iota(jnp.int32, (1, PAIR), 1)
    return (lane >= h * HEAD_DIM) & (lane < (h + 1) * HEAD_DIM)


def over_queries(ends, shift, bq, bk, step, body):
    most = -(-SEQ // bk)

    def one(t, _):
        q_at = pl.multiple_of(t * bq, bq)
        q_pos = (q_at + shift) & (SEQ - 1)
        begin, stop = key_range(ends, q_pos, bq, step)
        count = (stop - begin + bk - 1) // bk
        begin = jnp.minimum(begin, SEQ - count * bk)
        begin = pl.multiple_of(begin, step)
        for n in range(1, most + 1):

            @pl.when(count == n)
            def _():
                body(q_at, begin, n)

        return 0

    lax.fori_loop(0, SEQ // bq, one, 0)


def true_order(dst, src, shift):
    half = SEQ // 2
    dst[pl.ds(pl.multiple_of(shift, half), half), :] = src[:half]
    dst[pl.ds(pl.multiple_of(half - shift, half), half), :] = src[half:]


def both(own_ref, got_ref, at, pair):
    cols = slice(at + pair * PAIR, at + (pair + 1) * PAIR)
    return jnp.concatenate([own_ref[:, cols], got_ref[:, cols]], axis=0)


def attend_kernel(bq, bk, step, ahead, pairs, len_ref, side_ref, own_ref, got_ref, ctx_own, ctx_send, lse_ref, qh, kh, vt, acc, tot):
    shift = side_ref[0] * (SEQ // 2)
    half = SEQ // 2
    ends = seg_ends(len_ref)
    key_mark, query_mark = seg_marks(ends, shift)
    width = own_ref.shape[1] // 3
    heads = 2 * len(pairs)
    for p, pair in enumerate(pairs):
        cols = slice(p * PAIR, (p + 1) * PAIR)
        q = both(own_ref, got_ref, 0, pair).astype(F32) * 0.125
        k = both(own_ref, got_ref, width, pair).astype(F32)
        for h in range(2):
            qh[2 * p + h] = jnp.where(head_mask(h), q, query_mark).astype(LOW)
            true_order(kh.at[2 * p + h], jnp.where(head_mask(h), k, key_mark).astype(LOW), shift)
        vals = jnp.transpose(both(own_ref, got_ref, 2 * width, pair).astype(F32)).astype(LOW)
        vt[cols, pl.ds(pl.multiple_of(shift, half), half)] = vals[:, :half]
        vt[cols, pl.ds(pl.multiple_of(half - shift, half), half)] = vals[:, half:]

    def body(q_at, begin, n):
        qs = pl.ds(q_at, bq)
        at = [pl.ds(pl.multiple_of(begin + i * bk, step), bk) for i in range(n)]

        def score(h):
            query = qh[h, qs, :]
            return [nt(kh[h, at[i], :], query) for i in range(n)]

        ready = [score(h) for h in range(ahead)]
        for h in range(heads):
            dims = slice(h * HEAD_DIM, (h + 1) * HEAD_DIM)
            if h + ahead < heads:
                ready.append(score(h + ahead))
            parts = ready[h]
            top = jnp.max(parts[0], axis=0, keepdims=True)
            for s in parts[1:]:
                top = jnp.maximum(top, jnp.max(s, axis=0, keepdims=True))
            total, out = 0.0, 0.0
            for i, s in enumerate(parts):
                p = jnp.exp(s - top)
                total = total + jnp.sum(p, axis=0, keepdims=True)
                out = out + nn(vt[dims, at[i]], p.astype(LOW))
            acc[dims, qs] = out * (1.0 / total)
            tot[h : h + 1, qs] = top + jnp.log(total)

    over_queries(ends, shift, bq, bk, step, body)
    context = jnp.transpose(acc[...]).astype(LOW)
    ctx_own[...] = context[:half]
    ctx_send[...] = context[half:]
    lse_ref[...] = tot[...]


def attend(lengths, side, own, got, pairs, bq=256, bk=256, step=128, ahead=2):
    heads = 2 * len(pairs)
    width = heads * HEAD_DIM
    assert heads <= 8
    smem = pl.BlockSpec(memory_space=pltpu.SMEM)
    vmem = pl.BlockSpec(memory_space=pltpu.VMEM)
    return pl.pallas_call(
        partial(attend_kernel, bq, bk, step, ahead, pairs),
        in_specs=[smem, smem, vmem, vmem],
        out_specs=[vmem, vmem, vmem],
        out_shape=[
            jax.ShapeDtypeStruct((SEQ // 2, width), LOW),
            jax.ShapeDtypeStruct((SEQ // 2, width), LOW),
            jax.ShapeDtypeStruct((8, SEQ), F32),
        ],
        scratch_shapes=[
            pltpu.VMEM((heads, SEQ, PAIR), LOW),
            pltpu.VMEM((heads, SEQ, PAIR), LOW),
            pltpu.VMEM((width, SEQ), LOW),
            pltpu.VMEM((width, SEQ), F32),
            pltpu.VMEM((8, SEQ), F32),
        ],
        compiler_params=pltpu.CompilerParams(vmem_limit_bytes=32 * 1024 * 1024),
        name="attend",
    )(lengths, side, own, got)


def attend_back_kernel(
    bq, bk, step, ahead, pairs, len_ref, side_ref, own_ref, got_ref, do_own_ref, do_got_ref,
    ctx_own, ctx_send, lse_ref, g_ref, qh, qz, dom, kh, vals, kt, inner, dqt, dk, dv,
):
    shift = side_ref[0] * (SEQ // 2)
    half = SEQ // 2
    ends = seg_ends(len_ref)
    key_mark, query_mark = seg_marks(ends, shift)
    width = own_ref.shape[1] // 3
    heads = 2 * len(pairs)
    first = pl.ds(pl.multiple_of(shift, half), half)
    second = pl.ds(pl.multiple_of(half - shift, half), half)
    for p, pair in enumerate(pairs):
        cols = slice(p * PAIR, (p + 1) * PAIR)
        q = both(own_ref, got_ref, 0, pair).astype(F32) * 0.125
        k = both(own_ref, got_ref, width, pair).astype(F32)
        do = both(do_own_ref, do_got_ref, 0, pair).astype(F32)
        for h in range(2):
            mask = head_mask(h)
            at = 2 * p + h
            qh[at] = jnp.where(mask, q, query_mark).astype(LOW)
            qz[at] = jnp.where(mask, q, 0.0).astype(LOW)
            dom[at] = jnp.where(mask, do, 0.0).astype(LOW)
            true_order(kh.at[at], jnp.where(mask, k, key_mark).astype(LOW), shift)
        true_order(vals.at[p], both(own_ref, got_ref, 2 * width, pair), shift)
        turned = jnp.transpose(k).astype(LOW)
        kt[cols, first] = turned[:, :half]
        kt[cols, second] = turned[:, half:]
        prod = jnp.transpose(do * both(ctx_own, ctx_send, 0, p).astype(F32))
        for h in range(2):
            inner[2 * p + h : 2 * p + h + 1, :] = jnp.sum(
                prod[h * HEAD_DIM : (h + 1) * HEAD_DIM], axis=0, keepdims=True
            )
    dk[...] = jnp.zeros_like(dk)
    dv[...] = jnp.zeros_like(dv)

    def body(q_at, begin, n):
        qs = pl.ds(q_at, bq)
        at = [pl.ds(pl.multiple_of(begin + i * bk, step), bk) for i in range(n)]

        def score(h):
            query, grad = qh[h, qs, :], dom[h, qs, :]
            return [(nt(kh[h, at[i], :], query), nt(vals[h // 2, at[i], :], grad)) for i in range(n)]

        ready = [score(h) for h in range(ahead)]
        for h in range(heads):
            if h + ahead < heads:
                ready.append(score(h + ahead))
            dims = slice(h * HEAD_DIM, (h + 1) * HEAD_DIM)
            plain, grad = qz[h, qs, :], dom[h, qs, :]
            lse, mean = lse_ref[h : h + 1, qs], inner[h : h + 1, qs]
            out = 0.0
            for i, (s, gp) in enumerate(ready[h]):
                p = jnp.exp(s - lse)
                ds = (p * (gp - mean)).astype(LOW)
                dv[h // 2, at[i], :] += nn(p.astype(LOW), grad)
                dk[h // 2, at[i], :] += nn(ds, plain)
                out = out + nn(kt[dims, at[i]], ds)
            dqt[dims, qs] = out

    over_queries(ends, shift, bq, bk, step, body)
    part = heads * HEAD_DIM
    g_ref[:, :part] = (jnp.transpose(dqt[...]) * 0.125).astype(LOW)
    for p in range(heads // 2):
        for at, src in ((part + p * PAIR, dk), (2 * part + p * PAIR, dv)):
            g_ref[:half, at : at + PAIR] = src[p, first, :].astype(LOW)
            g_ref[half:, at : at + PAIR] = src[p, second, :].astype(LOW)


def attend_back(lengths, side, own, got, g_own, g_got, ctx_own, ctx_send, lse, pairs, bq=256, bk=256, step=128, ahead=1):
    heads = 2 * len(pairs)
    width = heads * HEAD_DIM
    smem = pl.BlockSpec(memory_space=pltpu.SMEM)
    vmem = pl.BlockSpec(memory_space=pltpu.VMEM)
    return pl.pallas_call(
        partial(attend_back_kernel, bq, bk, step, ahead, pairs),
        in_specs=[smem, smem] + [vmem] * 7,
        out_specs=vmem,
        out_shape=jax.ShapeDtypeStruct((SEQ, 3 * width), LOW),
        scratch_shapes=[
            pltpu.VMEM((heads, SEQ, PAIR), LOW),
            pltpu.VMEM((heads, SEQ, PAIR), LOW),
            pltpu.VMEM((heads, SEQ, PAIR), LOW),
            pltpu.VMEM((heads, SEQ, PAIR), LOW),
            pltpu.VMEM((heads // 2, SEQ, PAIR), LOW),
            pltpu.VMEM((width, SEQ), LOW),
            pltpu.VMEM((8, SEQ), F32),
            pltpu.VMEM((width, SEQ), F32),
            pltpu.VMEM((heads // 2, SEQ, PAIR), F32),
            pltpu.VMEM((heads // 2, SEQ, PAIR), F32),
        ],
        compiler_params=pltpu.CompilerParams(vmem_limit_bytes=48 * 1024 * 1024),
        name="attend_back",
    )(lengths, side, own, got, g_own, g_got, ctx_own, ctx_send, lse)


MIB = 1024 * 1024


def unit_norm(resid):
    middle = jnp.mean(resid, axis=-1, keepdims=True)
    centered = resid - middle
    spread = jnp.mean(centered * centered, axis=-1, keepdims=True)
    scaled = lax.rsqrt(spread + 1e-06)
    return centered * scaled, scaled


def norm_back(grad, unit, scaled, gain):
    weighted = grad * gain
    first_mean = jnp.mean(weighted, axis=-1, keepdims=True)
    second_mean = jnp.mean(weighted * unit, axis=-1, keepdims=True)
    return scaled * (weighted - first_mean - unit * second_mean)


def gelu_pair(v):
    cdf = 0.5 + 0.5 * lax.erf(v * 0.7071067811865476)
    bell = jnp.exp(-0.5 * (v * v))
    return v * cdf, cdf + (v * 0.3989422804014327) * bell


def rows_sum(v):
    return jnp.sum(v, axis=0, keepdims=True)


def after(value, *others):
    return lax.optimization_barrier((value, *others))[0]


def vmem_specs(count):
    return [pl.BlockSpec(memory_space=pltpu.VMEM)] * count


def any_specs(count):
    return [pl.BlockSpec(memory_space=pl.ANY)] * count


SMEM = pl.BlockSpec(memory_space=pltpu.SMEM)


def hbm(*arrays):
    return [pltpu.with_memory_space_constraint(v, pltpu.HBM) for v in arrays]


def in_hbm(shape, dtype=LOW):
    return pltpu.HBM(shape, dtype)


class Copies:
    def __init__(self, sem):
        self.sem, self.count = sem, 0

    def start(self, src, dst):
        copy = pltpu.make_async_copy(src, dst, self.sem.at[self.count])
        copy.start()
        self.count += 1
        return copy


def wait_all(copies):
    for copy in copies:
        copy.wait()


def quarters(core, other):
    mine, theirs = other
    return [2 * core + mine, 2 * core + 1 - mine, 2 * (1 - core) + theirs, 2 * (1 - core) + 1 - theirs]


def place(at, rows):
    return pl.ds(pl.multiple_of(at * rows, rows), rows)


def fetch_mix(go, scal, pieces, dst):
    rows = dst.shape[0] // 2
    return [
        go.start(src.at[:rows, :], dst.at[place(at, rows), :])
        for src, at in zip(pieces, (scal[0], 1 - scal[0]))
    ]


def fetch_own(go, up, down, ups, downs):
    size = ups.shape[2]
    waits = []
    for k in range(ups.shape[0]):
        cols = slice(k * size, (k + 1) * size)
        waits.append(([go.start(up.at[:, cols], ups.at[k])], [go.start(down.at[cols, :], downs.at[cols, :])]))
    return waits


def fetch_got(go, scal, pieces, ups, downs):
    order = quarters(scal[0], (scal[1], scal[2]))
    rows = ups.shape[1] // 4
    waits = []
    for k in range(ups.shape[0]):
        part = slice(k * rows, (k + 1) * rows)
        waits.append(([go.start(src.at[part, :], ups.at[k, place(at, rows), :]) for src, at in zip(pieces, order)], []))
    first, rows = 2 * rows, downs.shape[0] // 4
    for src, at in zip(pieces, order):
        waits[0][1].append(go.start(src.at[first : first + rows, :], downs.at[place(at, rows), :]))
    return waits


def row_loop(first, count, step, body, carry=0):
    for at in range(first, first + count, step):
        carry = body(slice(at, at + step), carry)
    return carry


def fold(v):
    return jnp.sum(v.reshape(-1, 8, v.shape[-1]), axis=0)


ROWS = 128


def feed_chunks(tile, low, bias, ups, downs, waits, branch, act, slope, done):
    tiles = low.shape[0] // tile
    size = ups.shape[2]
    span = [slice(r * tile, (r + 1) * tile) for r in range(tiles)]
    order = [(j, r) for j in range(ups.shape[0]) for r in range(tiles)]

    def pre(j, r):
        if r == 0:
            wait_all(waits[j][0])
        return nn(low[span[r], :], ups[j]) + bias(j)

    ahead = pre(*order[0])
    for t, (j, r) in enumerate(order):
        value, ahead = ahead, (pre(*order[t + 1]) if t + 1 < len(order) else None)
        active, incline = gelu_pair(value)
        active = active.astype(LOW)
        if act is not None:
            act[j, span[r], :] = active
        slope[j, span[r], :] = incline.astype(LOW)
        if r == 0:
            wait_all(waits[j][1])
        branch[span[r], :] += nn(active, downs[j * size : (j + 1) * size, :])
        if r == tiles - 1:
            done(j)


def first_kernel(
    tile, scal, ctx_own, ctx_got, x_ref, mix_own, mix_bias, gain_ref, shift_ref, down_bias, bias_ref,
    m_0, m_1, up_in, down_in, resid_out, low_out, branch_out, act_out, slope_out,
    mix_got, ups, downs, resid, low, branch, act, slope, sem,
):
    go = Copies(sem)
    mix_wait = fetch_mix(go, scal, (m_0, m_1), mix_got)
    waits = fetch_own(go, up_in, down_in, ups, downs)
    gain, shift, offset, more = (r[...].astype(F32) for r in (gain_ref, shift_ref, mix_bias, down_bias))
    pending = []
    for r in range(x_ref.shape[0] // tile):
        rows = slice(r * tile, (r + 1) * tile)
        attended = nn(ctx_own[rows, :], mix_own[...])
        if r == 0:
            wait_all(mix_wait)
        attended += nn(ctx_got[rows, :], mix_got[...])
        resid[rows, :] = attended

        def norm(at, _):
            value = resid[at, :] + x_ref[at, :].astype(F32) + offset
            resid[at, :] = value
            normed = unit_norm(value)[0] * gain + shift
            low[at, :] = normed.astype(LOW)
            branch[at, :] = normed + more
            return 0

        row_loop(r * tile, tile, ROWS, norm)
    pending += [go.start(resid, resid_out), go.start(low, low_out)]

    def done(j):
        pending.extend([go.start(act.at[j], act_out.at[j]), go.start(slope.at[j], slope_out.at[j])])

    feed_chunks(
        tile, low, lambda j: bias_ref[j : j + 1, :].astype(F32), ups, downs, waits, branch, act, slope, done
    )
    pending.append(go.start(branch, branch_out))
    wait_all(pending)


def first_part(scal, ctx_own, ctx_got, x, mix_own, vecs, bias, m_got, up, down, tile=256):
    tokens, width = x.shape
    hidden = up.shape[1] // 2
    both_chunks = (2, tokens, hidden)
    return pl.pallas_call(
        partial(first_kernel, tile),
        in_specs=[SMEM] + vmem_specs(9) + any_specs(4),
        out_specs=any_specs(5),
        out_shape=[
            in_hbm((tokens, width), F32), in_hbm((tokens, width)), in_hbm((tokens, width), F32),
            in_hbm(both_chunks), in_hbm(both_chunks),
        ],
        scratch_shapes=[
            pltpu.VMEM(mix_own.shape, LOW), pltpu.VMEM((2, width, hidden), LOW), pltpu.VMEM((2 * hidden, width), LOW),
            pltpu.VMEM((tokens, width), F32), pltpu.VMEM((tokens, width), LOW), pltpu.VMEM((tokens, width), F32),
            pltpu.VMEM(both_chunks, LOW), pltpu.VMEM(both_chunks, LOW), pltpu.SemaphoreType.DMA((16,)),
        ],
        compiler_params=pltpu.CompilerParams(vmem_limit_bytes=48 * MIB),
        cost_estimate=pl.CostEstimate(
            flops=2 * tokens * width * (width + 4 * hidden), bytes_accessed=16 * MIB, transcendentals=4 * tokens * hidden
        ),
        name="first_part",
    )(scal, *hbm(ctx_own, ctx_got, x, mix_own), *vecs, bias, *hbm(*m_got, up, down))


def second_kernel(
    tile, scal, low, down_gain, end_shift, m_0, branch_in, e_in, *rest,
):
    pieces = rest[:4]
    out_out, g_second_out, g_branch_out, slope_out, sum_ref = rest[4:9]
    ups, downs, branch, e_ref, slope, out, g_second, g_branch, sem = rest[9:]
    go = Copies(sem)
    start = [go.start(branch_in, branch)]
    waits = fetch_got(go, scal, pieces, ups, downs)
    later = [go.start(e_in, e_ref)]
    waits[0][1].extend(start)
    pending = []
    bias_at = m_0.shape[0] - 16

    def done(j):
        pending.append(go.start(slope.at[j], slope_out.at[j]))

    feed_chunks(
        tile, low, lambda j: m_0[bias_at + j : bias_at + j + 1, :].astype(F32), ups, downs, waits, branch, None, slope, done
    )
    wait_all(later)
    gain, shift = down_gain[...].astype(F32), end_shift[...].astype(F32)
    width = branch.shape[1]
    sums = tuple(jnp.zeros((8, width), F32) for _ in range(3))

    def norm(at, sums):
        unit, scaled = unit_norm(branch[at, :])
        out[at, :] = (unit * gain + shift).astype(LOW)
        e = e_ref[at, :].astype(F32)
        grad = norm_back(e, unit, scaled, gain)
        g_second[at, :] = grad
        g_branch[at, :] = grad.astype(LOW)
        return tuple(a + fold(b) for a, b in zip(sums, (grad, e * unit, e)))

    half = branch.shape[0] // 2
    for r in range(2):
        sums = row_loop(r * half, half, ROWS, norm, sums)
        at = pl.ds(r * half, half)
        for src, dst in ((g_branch, g_branch_out), (g_second, g_second_out), (out, out_out)):
            pending.append(go.start(src.at[at, :], dst.at[at, :]))
    sum_ref[...] = jnp.concatenate([rows_sum(v) for v in sums] + [jnp.zeros((5, width), F32)], axis=0)
    wait_all(pending)


def second_part(scal, low, end_gain, end_shift, m_0, branch, e, pieces, tile=256):
    tokens, width = low.shape
    hidden = width
    sds = jax.ShapeDtypeStruct
    return pl.pallas_call(
        partial(second_kernel, tile),
        in_specs=[SMEM] + vmem_specs(4) + any_specs(6),
        out_specs=any_specs(4) + vmem_specs(1),
        out_shape=[
            in_hbm((tokens, width)), in_hbm((tokens, width), F32), in_hbm((tokens, width)),
            in_hbm((2, tokens, hidden)), sds((8, width), F32),
        ],
        scratch_shapes=[
            pltpu.VMEM((2, width, hidden), LOW), pltpu.VMEM((2 * hidden, width), LOW), pltpu.VMEM((tokens, width), F32),
            pltpu.VMEM((tokens, width), LOW), pltpu.VMEM((2, tokens, hidden), LOW), pltpu.VMEM((tokens, width), LOW),
            pltpu.VMEM((tokens, width), F32), pltpu.VMEM((tokens, width), LOW), pltpu.SemaphoreType.DMA((24,)),
        ],
        compiler_params=pltpu.CompilerParams(vmem_limit_bytes=48 * MIB),
        cost_estimate=pl.CostEstimate(
            flops=8 * tokens * width * hidden, bytes_accessed=14 * MIB, transcendentals=4 * tokens * hidden
        ),
        name="second_part",
    )(scal, *hbm(low), end_gain, end_shift, *hbm(m_0, branch, e, *pieces))


def back_kernel(tile, scal, g_branch, gain_ref, mix_own, g_second_in, resid_in, slope_a, slope_b, m_0, m_1, up_in, down_in, *rest):
    pieces = rest[:4]
    g_first_out, g_att_out, ctx_a_out, ctx_b_out, g_pre_out, sum_ref = rest[4:10]
    ups, downs, mix_got, slope, grad, resid, g_pre, g_att, g_ctx, sem = rest[10:]
    half = ups.shape[0] // 2
    size = ups.shape[2]
    go = Copies(sem)
    slope_wait = [go.start(slope_a.at[0], slope.at[0])]
    waits = fetch_own(go, up_in, down_in, ups.at[:half], downs.at[: half * size])
    start = go.start(g_second_in, grad)
    slope_wait += [go.start(slope_a.at[j], slope.at[j]) for j in range(1, half)]
    waits += fetch_got(go, scal, pieces, ups.at[half:], downs.at[half * size :])
    slope_wait += [go.start(slope_b.at[j], slope.at[half + j]) for j in range(half)]
    resid_wait = go.start(resid_in, resid)
    mix_wait = fetch_mix(go, scal, (m_0, m_1), mix_got)
    tokens = grad.shape[0]
    tiles = tokens // tile
    span = [slice(r * tile, (r + 1) * tile) for r in range(tiles)]
    order = [(j, r) for j in range(2 * half) for r in range(tiles)]
    pending = []

    def g_active(j, r):
        if r == 0:
            wait_all(waits[j][1])
        return nt(g_branch[span[r], :], downs[j * size : (j + 1) * size, :])

    ahead = g_active(*order[0])
    start.wait()
    for t, (j, r) in enumerate(order):
        value, ahead = ahead, (g_active(*order[t + 1]) if t + 1 < len(order) else None)
        if r == 0:
            slope_wait[j].wait()
            wait_all(waits[j][0])
        low = (value * slope[j, span[r], :].astype(F32)).astype(LOW)
        if j < half:
            g_pre[j, span[r], :] = low
            if r == tiles - 1:
                pending.append(go.start(g_pre.at[j], g_pre_out.at[j]))
        grad[span[r], :] += nt(low, ups[j])
    resid_wait.wait()
    gain = gain_ref[...].astype(F32)
    width = grad.shape[1]
    sums = tuple(jnp.zeros((8, width), F32) for _ in range(3))

    def norm(at, sums):
        unit, scaled = unit_norm(resid[at, :])
        e = grad[at, :]
        first = norm_back(e, unit, scaled, gain)
        grad[at, :] = first
        g_att[at, :] = first.astype(LOW)
        return tuple(a + fold(b) for a, b in zip(sums, (first, e * unit, e)))

    wait_all(mix_wait)
    for r in range(tiles):
        sums = row_loop(r * tile, tile, ROWS, norm, sums)
        g_ctx[1, span[r], :] = nt(g_att[span[r], :], mix_got[...]).astype(LOW)
        g_ctx[0, span[r], :] = nt(g_att[span[r], :], mix_own[...]).astype(LOW)
        at = pl.ds(r * tile, tile)
        for src, dst in ((g_ctx.at[1], ctx_b_out), (g_ctx.at[0], ctx_a_out), (g_att, g_att_out), (grad, g_first_out)):
            pending.append(go.start(src.at[at, :], dst.at[at, :]))
    sum_ref[...] = jnp.concatenate([rows_sum(v) for v in sums] + [jnp.zeros((5, width), F32)], axis=0)
    wait_all(pending)


def back_part(scal, g_branch, gain, mix_own, g_second, resid, slopes, m_got, up, down, pieces, tile=256):
    tokens, width = g_branch.shape
    part = mix_own.shape[0]
    hidden = up.shape[1] // 2
    sds = jax.ShapeDtypeStruct
    return pl.pallas_call(
        partial(back_kernel, tile),
        in_specs=[SMEM] + vmem_specs(3) + any_specs(12),
        out_specs=any_specs(5) + vmem_specs(1),
        out_shape=[
            in_hbm((tokens, width), F32), in_hbm((tokens, width)), in_hbm((tokens, part)), in_hbm((tokens, part)),
            in_hbm((2, tokens, hidden)), sds((8, width), F32),
        ],
        scratch_shapes=[
            pltpu.VMEM((4, width, hidden), LOW), pltpu.VMEM((4 * hidden, width), LOW), pltpu.VMEM((part, width), LOW),
            pltpu.VMEM((4, tokens, hidden), LOW), pltpu.VMEM((tokens, width), F32), pltpu.VMEM((tokens, width), F32),
            pltpu.VMEM((2, tokens, hidden), LOW), pltpu.VMEM((tokens, width), LOW), pltpu.VMEM((2, tokens, part), LOW),
            pltpu.SemaphoreType.DMA((40,)),
        ],
        compiler_params=pltpu.CompilerParams(vmem_limit_bytes=50 * MIB),
        cost_estimate=pl.CostEstimate(flops=16 * tokens * width * hidden, bytes_accessed=24 * MIB, transcendentals=0),
        name="back_part",
    )(scal, *hbm(g_branch), gain, *hbm(mix_own, g_second, resid, *slopes, *m_got, up, down, *pieces))


def weight_kernel(
    pick, act_ref, g_pre_ref, low_ref, low_got, g_branch_ref, g_branch_got, up_ref, down_ref, bias_ref, out, bias_out,
):
    width = low_ref.shape[1]
    bias = bias_ref[...].astype(F32)
    pre = nn(low_got[...], up_ref[...]) + jnp.where(pick[0] == 0, bias[0:1], bias[1:2])
    g_active = nt(g_branch_got[...], down_ref[...])
    active, incline = gelu_pair(pre)
    g_pre = g_active * incline
    bias_out[...] = rows_sum(g_pre) + rows_sum(g_pre_ref[0].astype(F32))
    g_pre = g_pre.astype(LOW)
    out[:width, :] = (tn(low_ref[...], g_pre_ref[0]) + tn(low_got[...], g_pre)).astype(LOW)
    out[width:, :] = (tn(act_ref[0], g_branch_ref[...]) + tn(active.astype(LOW), g_branch_got[...])).astype(LOW)


def weight_part(pick, act, g_pre, low, low_got, g_branch, g_branch_got, up, down, bias):
    chunks, tokens, hidden = act.shape
    width = low.shape[1]
    assert hidden == width
    chunk = pl.BlockSpec((1, tokens, hidden), lambda i, pick: (pick[0], 0, 0))
    fixed = pl.BlockSpec((tokens, width), lambda i, pick: (0, 0))
    return pl.pallas_call(
        weight_kernel,
        grid_spec=pltpu.PrefetchScalarGridSpec(
            num_scalar_prefetch=1,
            grid=(1,),
            in_specs=[
                chunk, chunk, fixed, fixed, fixed, fixed,
                pl.BlockSpec((width, hidden), lambda i, pick: (0, pick[0])),
                pl.BlockSpec((hidden, width), lambda i, pick: (pick[0], 0)),
                pl.BlockSpec((chunks, hidden), lambda i, pick: (0, 0)),
            ],
            out_specs=[
                pl.BlockSpec((width + hidden, width), lambda i, pick: (0, 0)),
                pl.BlockSpec((1, hidden), lambda i, pick: (0, 0)),
            ],
        ),
        out_shape=[in_hbm((width + hidden, width)), jax.ShapeDtypeStruct((1, hidden), F32)],
        compiler_params=pltpu.CompilerParams(vmem_limit_bytes=50 * MIB),
        cost_estimate=pl.CostEstimate(
            flops=12 * tokens * width * hidden, bytes_accessed=10 * MIB, transcendentals=2 * tokens * hidden
        ),
        name="weight_part",
    )(pick, *hbm(act, g_pre, low, low_got, g_branch, g_branch_got, up, down), bias)


def mix_grad_kernel(ctx_own, ctx_got, g_att, own_out, got_out):
    own_out[...] = tn(ctx_own[...], g_att[...]).astype(LOW)
    got_out[...] = tn(ctx_got[...], g_att[...]).astype(LOW)


def mix_grad(ctx_own, ctx_got, g_att):
    tokens, width = g_att.shape
    part = ctx_own.shape[1]
    return pl.pallas_call(
        mix_grad_kernel,
        in_specs=vmem_specs(3),
        out_specs=vmem_specs(2),
        out_shape=[in_hbm((part, width))] * 2,
        compiler_params=pltpu.CompilerParams(vmem_limit_bytes=24 * MIB),
        cost_estimate=pl.CostEstimate(flops=4 * tokens * width * part, bytes_accessed=4 * MIB, transcendentals=0),
        name="mix_grad",
    )(*hbm(ctx_own, ctx_got, g_att))


def late_kernel(scal, own_ref, got_ref, g_ref, mix_own, mix_other, small_ref, keep, send, out):
    half, width = own_ref.shape
    cols = g_ref.shape[1]
    out[:, :cols] = (tn(own_ref[...], g_ref[:half, :]) + tn(got_ref[...], g_ref[half:, :])).astype(LOW)
    part = mix_own.shape[0]
    for k in range(2):
        side = slice(k * part, (k + 1) * part)
        total = mix_own[:, side].astype(F32) + mix_other[:part, side].astype(F32)
        out[side, cols : cols + part] = total.astype(LOW)
    sums = nn(jnp.ones((8, 2 * half), LOW), g_ref[...])[:1]
    sums = jnp.concatenate([sums[:, :part], sums[:, 2 * part :]], axis=1)
    rows = jnp.concatenate([small_ref[...], sums, jnp.zeros((PAIR - 9, width), F32)], axis=0)
    out[:, cols + part :] = jnp.transpose(rows).astype(LOW)
    for c in range(2):

        @pl.when(scal[0] == c)
        def _():
            keep[...] = out[c * part : (c + 1) * part, :]
            send[...] = out[(1 - c) * part : (2 - c) * part, :]


def late_grads(scal, own, got, g, mix_own, mix_other, small):
    tokens, width = own.shape
    part = mix_own.shape[0]
    assert 2 * part == width and small.shape[0] == 8
    cols = g.shape[1] + part + PAIR
    return pl.pallas_call(
        late_kernel,
        in_specs=[SMEM] + vmem_specs(6),
        out_specs=vmem_specs(2),
        out_shape=[in_hbm((part, cols))] * 2,
        scratch_shapes=[pltpu.VMEM((width, cols), LOW)],
        compiler_params=pltpu.CompilerParams(vmem_limit_bytes=40 * MIB),
        cost_estimate=pl.CostEstimate(flops=4 * tokens * width * g.shape[1], bytes_accessed=8 * MIB, transcendentals=0),
        name="late_grads",
    )(scal, *hbm(own, got, g, mix_own, mix_other), small)


def finish_feed_kernel(scal, *refs):
    up_out, down_out = refs[4:]
    width = down_out.shape[2]
    for k in range(2):
        core, side = scal[0] ^ k, scal[1 + k]
        for n in range(2):
            piece = refs[2 * k + n][...].astype(F32)

            @pl.when(side == n)
            def _():
                up_out[:, pl.ds(pl.multiple_of(core * width, width), width)] = piece

            @pl.when(side != n)
            def _():
                down_out[core] = piece


def finish_feed(scal, pieces, steps=4):
    width = pieces[0].shape[1]
    rows = width // steps
    block = pl.BlockSpec((rows, width), lambda i, scal: (i, 0))
    up, down = pl.pallas_call(
        finish_feed_kernel,
        grid_spec=pltpu.PrefetchScalarGridSpec(
            num_scalar_prefetch=1,
            grid=(steps,),
            in_specs=[block] * 4,
            out_specs=[
                pl.BlockSpec((rows, 2 * width), lambda i, scal: (i, 0)),
                pl.BlockSpec((2, rows, width), lambda i, scal: (0, i, 0)),
            ],
        ),
        out_shape=[in_hbm((width, 2 * width), F32), in_hbm((2, width, width), F32)],
        compiler_params=pltpu.CompilerParams(vmem_limit_bytes=32 * MIB),
        cost_estimate=pl.CostEstimate(flops=0, bytes_accessed=14 * MIB, transcendentals=0),
        name="finish_feed",
    )(scal, *hbm(*pieces))
    return up, down.reshape(2 * width, width)


def finish_late_kernel(scal, *refs):
    q_out, k_out, v_out, mix_out, small_out = refs[4:]
    part = q_out.shape[1]
    half = part // 2
    for k in range(2):
        core = scal[0] ^ k
        for n in range(2):
            side = scal[1 + k] ^ n
            piece = refs[2 * k + n]
            rows = pl.ds(pl.multiple_of(core * part + side * half, half), half)
            for m, out in enumerate((q_out, k_out, v_out)):
                out[rows, :] = piece[:, m * part : (m + 1) * part].astype(F32)
            some = pl.ds(pl.multiple_of(side * half, half), half)
            mix_out[some, pl.ds(pl.multiple_of(core * part, part), part)] = piece[:, 3 * part : 4 * part].astype(F32)
            small = jnp.transpose(piece[:, 4 * part :].astype(F32))[:16]
            for at in range(4):

                @pl.when(2 * core + side == at)
                def _():
                    small_out[:, at * half : (at + 1) * half] = small


def finish_late(scal, pieces):
    part = 2 * pieces[0].shape[0]
    sds = jax.ShapeDtypeStruct
    return pl.pallas_call(
        finish_late_kernel,
        in_specs=[SMEM] + vmem_specs(4),
        out_specs=vmem_specs(5),
        out_shape=[in_hbm((2 * part, part), F32)] * 3 + [in_hbm((part, 2 * part), F32), sds((16, 2 * part), F32)],
        compiler_params=pltpu.CompilerParams(vmem_limit_bytes=32 * MIB),
        cost_estimate=pl.CostEstimate(flops=0, bytes_accessed=8 * MIB, transcendentals=0),
        name="finish_late",
    )(scal, *hbm(*pieces))


def swap(value, axis, bit):
    even, odd = bit if isinstance(bit, tuple) else (bit, bit)
    return lax.ppermute(value, axis, [(i, i ^ (odd if i & 1 else even)) for i in range(lax.axis_size(axis))])


def wide(value):
    return value.astype(F32)


def cut(value, at, size):
    return lax.dynamic_slice_in_dim(value, at, size, 0)


def side_of(dp, mask):
    if isinstance(mask, tuple):
        mask = jnp.where(dp & 1, mask[1], mask[0])
    return ((dp & mask) != 0).astype(jnp.int32)


def dp_masks():
    return [1 << i for i in range(lax.axis_size("dp").bit_length() - 1)]


def total(terms):
    return sum(wide(t) for t in terms).astype(LOW)


class Chain:
    def __init__(self, dp, masks, terms):
        self.dp, self.masks, self.terms = dp, masks, terms
        self.step, self.value, self.sent, self.got = 0, None, None, None

    def start(self, *others):
        last = len(self.masks) - 1
        if self.step < last:
            mask = self.masks[self.step]
            half, mine = self.terms[0].shape[0] // 2, side_of(self.dp, mask)
            self.sent = total([cut(t, (1 - mine) * half, half) for t in self.terms])
            self.terms = [cut(t, mine * half, half) for t in self.terms]
        elif self.step == last:
            mask = self.masks[last]
            self.sent = self.value = total(self.terms)
        else:
            mask = self.masks[2 * last - self.step]
            self.sent = self.value
        if others:
            self.sent = after(self.sent, *others)
        self.got = swap(self.sent, "dp", mask)

    def finish(self, *others):
        got = after(self.got, *others) if others else self.got
        last = len(self.masks) - 1
        if self.step < last:
            self.terms = self.terms + [got]
        elif self.step == last:
            self.value = (wide(self.value) + wide(got)).astype(LOW)
        elif self.step < 2 * last:
            side = side_of(self.dp, self.masks[2 * last - self.step])
            self.value = jnp.where(side == 1, jnp.concatenate([got, self.value]), jnp.concatenate([self.value, got]))
        self.step += 1
        self.got = got

    @property
    def done(self):
        return self.step == 2 * len(self.masks) - 1


def per_device(
    inputs, upstream, lengths, query_weight, key_weight, value_weight, query_bias, value_bias, mix_weight, mix_bias,
    mid_gain, mid_shift, up_weight, up_bias, down_weight, down_bias, end_gain, end_shift,
):
    dp = lax.axis_index("dp").astype(jnp.int32)
    side = lax.axis_index("tensor").astype(jnp.int32).reshape(1)
    masks = dp_masks()
    core = dp & 1
    order = [(masks[1], masks[2]), (masks[2], masks[1])] + masks[3:]
    mine = side_of(dp, order[0])
    scal = jnp.stack([core] + [side_of(dp, mask) for mask in order[:-1]])
    tokens, width = inputs.shape
    part = query_weight.shape[1]
    own_hidden = up_weight.shape[1]
    hidden = own_hidden // 2
    row = lambda v: v.reshape(1, -1)
    across = lambda v: swap(v, "tensor", 1)

    x_got = across(inputs)
    pairs = tuple(range(part // PAIR))
    qkv_weight = jnp.concatenate([query_weight, key_weight, value_weight], axis=1)
    qkv_bias = jnp.concatenate([wide(query_bias), jnp.zeros((part,), F32), wide(value_bias)])
    bias_own = up_bias.reshape(2, hidden)
    m_piece = jnp.concatenate([cut(mix_weight, core * (part // 2), part // 2), bias_own, jnp.zeros((14, width), LOW)])
    up_piece = cut(up_weight, (2 * core + mine) * (width // 4), width // 4)
    down_piece = cut(down_weight, (2 * core + mine) * (own_hidden // 4), own_hidden // 4)
    piece = jnp.concatenate([up_piece[:, :hidden], up_piece[:, hidden:], down_piece])

    def project(v):
        return (nn(v, qkv_weight) + qkv_bias).astype(LOW)

    own = project(inputs)
    x_got = after(x_got, own, m_piece, piece)
    m_0, piece_0 = across(after(m_piece, x_got)), across(after(piece, x_got))
    got = project(x_got)
    ctx_own, ctx_send, lse = attend(lengths, side, own, got, pairs)
    ctx_send, m_0, piece_0 = lax.optimization_barrier((ctx_send, m_0, piece_0))
    ctx_got = across(ctx_send)
    m_got = [m_0, swap(m_0, "dp", 1)]
    piece_1 = swap(piece_0, "dp", order[0])
    resid, low, branch, act, slope_own = first_part(
        scal, ctx_own, ctx_got, inputs, mix_weight, [row(v) for v in (mix_bias, mid_gain, mid_shift, down_bias)], bias_own,
        m_got, up_weight, down_weight,
    )
    low_got = across(low)
    piece_1 = after(piece_1, low)
    pieces = [piece_0, piece_1, swap(piece_0, "dp", 1), swap(piece_1, "dp", 1)]
    outputs, g_second, g_branch, slope_got, end_sums = second_part(
        scal, low, row(end_gain), row(end_shift), m_0, branch, upstream, pieces
    )
    g_branch_got = across(g_branch)
    g_first, g_att, g_ctx_own, g_ctx_send, g_pre, mid_sums = back_part(
        scal, g_branch, row(mid_gain), mix_weight, g_second, resid, (slope_own, slope_got),
        m_got, up_weight, down_weight, pieces,
    )
    g_ctx_got = across(g_ctx_send)
    mix_own, mix_send = mix_grad(ctx_own, ctx_got, after(g_att, low_got))
    shared = (low, low_got, g_branch, g_branch_got, up_weight, down_weight, bias_own)
    send, bias_send = weight_part((1 - core).reshape(1), act, after(g_pre, mix_own), *shared)
    keep, bias_keep = weight_part(after(core.reshape(1), send, g_ctx_got), act, g_pre, *shared)
    up_rows = jnp.where(core == 0, jnp.concatenate([bias_keep, bias_send]), jnp.concatenate([bias_send, bias_keep]))
    small = jnp.concatenate([mid_sums[:3], end_sums[:3]])
    mix_send = after(mix_send, keep)
    mix_other = across(jnp.concatenate([mix_send, small.astype(LOW), jnp.zeros((10, width), LOW)]))
    feed = Chain(dp, order, [keep, swap(after(send, g_ctx_got), "dp", 1)])
    feed.start()
    g_qkv = attend_back(
        lengths, side, own, got, g_ctx_own, after(g_ctx_got, feed.sent), ctx_own, ctx_send, lse, pairs,
    )
    feed.finish(g_qkv)
    mix_other = after(mix_other, g_qkv)
    g_qkv = after(g_qkv, mix_other, feed.got)
    feed.start()
    input_got = across(nt(g_qkv[tokens:], qkv_weight).astype(LOW))
    small = jnp.concatenate([small + wide(mix_other[part : part + 6]), up_rows])
    late_keep, late_send = late_grads(scal, inputs, x_got, g_qkv, mix_own, mix_other, small)
    feed.finish(late_keep)
    proj = Chain(dp, order, [late_keep, swap(after(late_send, feed.got), "dp", 1)])
    proj.start()
    feed.start(proj.sent)
    proj.finish(feed.sent)
    proj.start()
    proj.finish()
    feed.finish(proj.got)
    input_got = after(input_got, proj.got)
    proj.start(feed.got, input_got)
    input_own = g_first + nt(after(g_qkv, proj.sent)[:tokens], qkv_weight)
    while not feed.done:
        feed.start()
        proj.finish(feed.sent)
        proj.start()
        feed.finish(proj.sent)
    feed_pieces = [feed.value, feed.got]
    feed_pieces += [swap(v, "dp", 1) for v in feed_pieces]
    input_grad = (input_own + wide(after(input_got, feed.got))).astype(LOW)
    up_grad, down_grad = finish_feed(after(scal, input_grad), feed_pieces)
    proj.finish(up_grad)
    while not proj.done:
        proj.start()
        proj.finish()
    late_pieces = [proj.value, proj.got]
    late_pieces += [swap(v, "dp", 1) for v in late_pieces]
    *qkv, mix_grads, small = finish_late(scal, late_pieces)
    return (
        outputs,
        input_grad,
        qkv[0],
        qkv[1],
        qkv[2],
        small[8, :part],
        small[8, part:],
        mix_grads,
        small[0],
        small[1],
        small[2],
        up_grad,
        small[6:8].reshape(own_hidden),
        down_grad,
        small[3],
        small[4],
        small[5],
    )


def solution(mesh):
    placed = (
        P(("dp", "tensor"), None),
        P(("dp", "tensor"), None),
        P("dp", None),
        P(None, "tensor"),
        P(None, "tensor"),
        P(None, "tensor"),
        P("tensor"),
        P("tensor"),
        P("tensor", None),
        P(),
        P(),
        P(),
        P(None, "tensor"),
        P("tensor"),
        P("tensor", None),
        P(),
        P(),
        P(),
    )
    return jax.shard_map(
        per_device,
        mesh=mesh,
        in_specs=placed,
        out_specs=(
            P(("dp", "tensor"), None),
            P(("dp", "tensor"), None),
            P(None, "tensor"),
            P(None, "tensor"),
            P(None, "tensor"),
            P("tensor"),
            P("tensor"),
            P("tensor", None),
            P(),
            P(),
            P(),
            P(None, "tensor"),
            P("tensor"),
            P("tensor", None),
            P(),
            P(),
            P(),
        ),
        check_vma=False,
    )
```

```python
from functools import partial

import jax
import jax.numpy as jnp
from jax import lax
from jax.experimental import pallas as pl
from jax.experimental.pallas import tpu as pltpu
from jax.sharding import PartitionSpec as P

HEAD_DIM = 64
PAIR = 128
SEQ = 1024
LOW = jnp.bfloat16
F32 = jnp.float32
FAR = -1e30


def nt(a, b):
    return lax.dot_general(a, b, (((1,), (1,)), ((), ())), preferred_element_type=F32)


def tn(a, b):
    return lax.dot_general(a, b, (((0,), (0,)), ((), ())), preferred_element_type=F32)


def nn(a, b):
    return lax.dot_general(a, b, (((1,), (0,)), ((), ())), preferred_element_type=F32)


def seg_ends(len_ref):
    ends, total = [], jnp.int32(0)
    for j in range(len_ref.shape[1]):
        total = total + len_ref[0, j]
        ends.append(total)
    return ends


def seg_marks(ends, shift):
    pos = (lax.broadcasted_iota(jnp.int32, (SEQ, PAIR), 0) + shift) & (SEQ - 1)
    lane = lax.broadcasted_iota(jnp.int32, (SEQ, PAIR), 1) & (HEAD_DIM - 1)
    seg = jnp.zeros((SEQ, PAIR), jnp.int32)
    for e in ends:
        seg = seg + (pos >= e).astype(jnp.int32)
    own = seg == lane
    used = lane < len(ends)
    key_mark = jnp.where(own, 1.0, 0.0)
    query_mark = jnp.where(used & jnp.logical_not(own), FAR, 0.0)
    return key_mark, query_mark


def key_range(ends, first, size, step):
    begin, stop = jnp.int32(0), jnp.int32(SEQ)
    for e in ends:
        begin = jnp.where(e <= first, e, begin)
    for e in reversed(ends):
        stop = jnp.where(e >= first + size, e, stop)
    return (begin // step) * step, stop


def head_mask(h):
    lane = lax.broadcasted_iota(jnp.int32, (1, PAIR), 1)
    return (lane >= h * HEAD_DIM) & (lane < (h + 1) * HEAD_DIM)


def over_queries(ends, shift, bq, bk, step, body):
    most = -(-SEQ // bk)

    def one(t, _):
        q_at = pl.multiple_of(t * bq, bq)
        q_pos = (q_at + shift) & (SEQ - 1)
        begin, stop = key_range(ends, q_pos, bq, step)
        count = (stop - begin + bk - 1) // bk
        begin = jnp.minimum(begin, SEQ - count * bk)
        begin = pl.multiple_of(begin, step)
        for n in range(1, most + 1):

            @pl.when(count == n)
            def _():
                body(q_at, begin, n)

        return 0

    lax.fori_loop(0, SEQ // bq, one, 0)


def true_order(dst, src, shift):
    half = SEQ // 2
    dst[pl.ds(pl.multiple_of(shift, half), half), :] = src[:half]
    dst[pl.ds(pl.multiple_of(half - shift, half), half), :] = src[half:]


def both(own_ref, got_ref, at, pair):
    cols = slice(at + pair * PAIR, at + (pair + 1) * PAIR)
    return jnp.concatenate([own_ref[:, cols], got_ref[:, cols]], axis=0)


def attend_kernel(bq, bk, step, ahead, pairs, len_ref, side_ref, own_ref, got_ref, ctx_own, ctx_send, lse_ref, qh, kh, vt, acc, tot):
    shift = side_ref[0] * (SEQ // 2)
    half = SEQ // 2
    ends = seg_ends(len_ref)
    key_mark, query_mark = seg_marks(ends, shift)
    width = own_ref.shape[1] // 3
    heads = 2 * len(pairs)
    for p, pair in enumerate(pairs):
        cols = slice(p * PAIR, (p + 1) * PAIR)
        q = both(own_ref, got_ref, 0, pair).astype(F32) * 0.125
        k = both(own_ref, got_ref, width, pair).astype(F32)
        for h in range(2):
            qh[2 * p + h] = jnp.where(head_mask(h), q, query_mark).astype(LOW)
            true_order(kh.at[2 * p + h], jnp.where(head_mask(h), k, key_mark).astype(LOW), shift)
        vals = jnp.transpose(both(own_ref, got_ref, 2 * width, pair).astype(F32)).astype(LOW)
        vt[cols, pl.ds(pl.multiple_of(shift, half), half)] = vals[:, :half]
        vt[cols, pl.ds(pl.multiple_of(half - shift, half), half)] = vals[:, half:]

    def body(q_at, begin, n):
        qs = pl.ds(q_at, bq)
        at = [pl.ds(pl.multiple_of(begin + i * bk, step), bk) for i in range(n)]

        def score(h):
            query = qh[h, qs, :]
            return [nt(kh[h, at[i], :], query) for i in range(n)]

        ready = [score(h) for h in range(ahead)]
        for h in range(heads):
            dims = slice(h * HEAD_DIM, (h + 1) * HEAD_DIM)
            if h + ahead < heads:
                ready.append(score(h + ahead))
            parts = ready[h]
            top = jnp.max(parts[0], axis=0, keepdims=True)
            for s in parts[1:]:
                top = jnp.maximum(top, jnp.max(s, axis=0, keepdims=True))
            total, out = 0.0, 0.0
            for i, s in enumerate(parts):
                p = jnp.exp(s - top)
                total = total + jnp.sum(p, axis=0, keepdims=True)
                out = out + nn(vt[dims, at[i]], p.astype(LOW))
            acc[dims, qs] = out * (1.0 / total)
            tot[h : h + 1, qs] = top + jnp.log(total)

    over_queries(ends, shift, bq, bk, step, body)
    context = jnp.transpose(acc[...]).astype(LOW)
    ctx_own[...] = context[:half]
    ctx_send[...] = context[half:]
    lse_ref[...] = tot[...]


def attend(lengths, side, own, got, pairs, bq=256, bk=256, step=128, ahead=2):
    heads = 2 * len(pairs)
    width = heads * HEAD_DIM
    assert heads <= 8
    smem = pl.BlockSpec(memory_space=pltpu.SMEM)
    vmem = pl.BlockSpec(memory_space=pltpu.VMEM)
    return pl.pallas_call(
        partial(attend_kernel, bq, bk, step, ahead, pairs),
        in_specs=[smem, smem, vmem, vmem],
        out_specs=[vmem, vmem, vmem],
        out_shape=[
            jax.ShapeDtypeStruct((SEQ // 2, width), LOW),
            jax.ShapeDtypeStruct((SEQ // 2, width), LOW),
            jax.ShapeDtypeStruct((8, SEQ), F32),
        ],
        scratch_shapes=[
            pltpu.VMEM((heads, SEQ, PAIR), LOW),
            pltpu.VMEM((heads, SEQ, PAIR), LOW),
            pltpu.VMEM((width, SEQ), LOW),
            pltpu.VMEM((width, SEQ), F32),
            pltpu.VMEM((8, SEQ), F32),
        ],
        compiler_params=pltpu.CompilerParams(vmem_limit_bytes=32 * 1024 * 1024),
        name="attend",
    )(lengths, side, own, got)


def attend_back_kernel(
    bq, bk, step, ahead, pairs, len_ref, side_ref, own_ref, got_ref, do_own_ref, do_got_ref,
    ctx_own, ctx_send, lse_ref, g_ref, qh, qz, dom, kh, vals, kt, inner, dqt, dk, dv,
):
    shift = side_ref[0] * (SEQ // 2)
    half = SEQ // 2
    ends = seg_ends(len_ref)
    key_mark, query_mark = seg_marks(ends, shift)
    width = own_ref.shape[1] // 3
    heads = 2 * len(pairs)
    first = pl.ds(pl.multiple_of(shift, half), half)
    second = pl.ds(pl.multiple_of(half - shift, half), half)
    for p, pair in enumerate(pairs):
        cols = slice(p * PAIR, (p + 1) * PAIR)
        q = both(own_ref, got_ref, 0, pair).astype(F32) * 0.125
        k = both(own_ref, got_ref, width, pair).astype(F32)
        do = both(do_own_ref, do_got_ref, 0, pair).astype(F32)
        for h in range(2):
            mask = head_mask(h)
            at = 2 * p + h
            qh[at] = jnp.where(mask, q, query_mark).astype(LOW)
            qz[at] = jnp.where(mask, q, 0.0).astype(LOW)
            dom[at] = jnp.where(mask, do, 0.0).astype(LOW)
            true_order(kh.at[at], jnp.where(mask, k, key_mark).astype(LOW), shift)
        true_order(vals.at[p], both(own_ref, got_ref, 2 * width, pair), shift)
        turned = jnp.transpose(k).astype(LOW)
        kt[cols, first] = turned[:, :half]
        kt[cols, second] = turned[:, half:]
        prod = jnp.transpose(do * both(ctx_own, ctx_send, 0, p).astype(F32))
        for h in range(2):
            inner[2 * p + h : 2 * p + h + 1, :] = jnp.sum(
                prod[h * HEAD_DIM : (h + 1) * HEAD_DIM], axis=0, keepdims=True
            )
    dk[...] = jnp.zeros_like(dk)
    dv[...] = jnp.zeros_like(dv)

    def body(q_at, begin, n):
        qs = pl.ds(q_at, bq)
        at = [pl.ds(pl.multiple_of(begin + i * bk, step), bk) for i in range(n)]

        def score(h):
            query, grad = qh[h, qs, :], dom[h, qs, :]
            return [(nt(kh[h, at[i], :], query), nt(vals[h // 2, at[i], :], grad)) for i in range(n)]

        ready = [score(h) for h in range(ahead)]
        for h in range(heads):
            if h + ahead < heads:
                ready.append(score(h + ahead))
            dims = slice(h * HEAD_DIM, (h + 1) * HEAD_DIM)
            plain, grad = qz[h, qs, :], dom[h, qs, :]
            lse, mean = lse_ref[h : h + 1, qs], inner[h : h + 1, qs]
            out = 0.0
            for i, (s, gp) in enumerate(ready[h]):
                p = jnp.exp(s - lse)
                ds = (p * (gp - mean)).astype(LOW)
                dv[h // 2, at[i], :] += nn(p.astype(LOW), grad)
                dk[h // 2, at[i], :] += nn(ds, plain)
                out = out + nn(kt[dims, at[i]], ds)
            dqt[dims, qs] = out

    over_queries(ends, shift, bq, bk, step, body)
    part = heads * HEAD_DIM
    g_ref[:, :part] = (jnp.transpose(dqt[...]) * 0.125).astype(LOW)
    for p in range(heads // 2):
        for at, src in ((part + p * PAIR, dk), (2 * part + p * PAIR, dv)):
            g_ref[:half, at : at + PAIR] = src[p, first, :].astype(LOW)
            g_ref[half:, at : at + PAIR] = src[p, second, :].astype(LOW)


def attend_back(lengths, side, own, got, g_own, g_got, ctx_own, ctx_send, lse, pairs, bq=256, bk=256, step=128, ahead=1):
    heads = 2 * len(pairs)
    width = heads * HEAD_DIM
    smem = pl.BlockSpec(memory_space=pltpu.SMEM)
    vmem = pl.BlockSpec(memory_space=pltpu.VMEM)
    return pl.pallas_call(
        partial(attend_back_kernel, bq, bk, step, ahead, pairs),
        in_specs=[smem, smem] + [vmem] * 7,
        out_specs=vmem,
        out_shape=jax.ShapeDtypeStruct((SEQ, 3 * width), LOW),
        scratch_shapes=[
            pltpu.VMEM((heads, SEQ, PAIR), LOW),
            pltpu.VMEM((heads, SEQ, PAIR), LOW),
            pltpu.VMEM((heads, SEQ, PAIR), LOW),
            pltpu.VMEM((heads, SEQ, PAIR), LOW),
            pltpu.VMEM((heads // 2, SEQ, PAIR), LOW),
            pltpu.VMEM((width, SEQ), LOW),
            pltpu.VMEM((8, SEQ), F32),
            pltpu.VMEM((width, SEQ), F32),
            pltpu.VMEM((heads // 2, SEQ, PAIR), F32),
            pltpu.VMEM((heads // 2, SEQ, PAIR), F32),
        ],
        compiler_params=pltpu.CompilerParams(vmem_limit_bytes=48 * 1024 * 1024),
        name="attend_back",
    )(lengths, side, own, got, g_own, g_got, ctx_own, ctx_send, lse)


MIB = 1024 * 1024


def unit_norm(resid):
    middle = jnp.mean(resid, axis=-1, keepdims=True)
    centered = resid - middle
    spread = jnp.mean(centered * centered, axis=-1, keepdims=True)
    scaled = lax.rsqrt(spread + 1e-06)
    return centered * scaled, scaled


def norm_back(grad, unit, scaled, gain):
    weighted = grad * gain
    first_mean = jnp.mean(weighted, axis=-1, keepdims=True)
    second_mean = jnp.mean(weighted * unit, axis=-1, keepdims=True)
    return scaled * (weighted - first_mean - unit * second_mean)


def gelu_pair(v):
    cdf = 0.5 + 0.5 * lax.erf(v * 0.7071067811865476)
    bell = jnp.exp(-0.5 * (v * v))
    return v * cdf, cdf + (v * 0.3989422804014327) * bell


def rows_sum(v):
    return jnp.sum(v, axis=0, keepdims=True)


def after(value, *others):
    return lax.optimization_barrier((value, *others))[0]


def vmem_specs(count):
    return [pl.BlockSpec(memory_space=pltpu.VMEM)] * count


def any_specs(count):
    return [pl.BlockSpec(memory_space=pl.ANY)] * count


SMEM = pl.BlockSpec(memory_space=pltpu.SMEM)


def hbm(*arrays):
    return [pltpu.with_memory_space_constraint(v, pltpu.HBM) for v in arrays]


def in_hbm(shape, dtype=LOW):
    return pltpu.HBM(shape, dtype)


class Copies:
    def __init__(self, sem):
        self.sem, self.count = sem, 0

    def start(self, src, dst):
        copy = pltpu.make_async_copy(src, dst, self.sem.at[self.count])
        copy.start()
        self.count += 1
        return copy


def wait_all(copies):
    for copy in copies:
        copy.wait()


def eighths(scal):
    core, one, two = scal[0], scal[1], scal[2]
    order = []
    for c, a, b in ((core, one, two), (1 - core, two, one)):
        order += [4 * c + 2 * (a ^ (k & 1)) + (b ^ (k >> 1)) for k in range(4)]
    return order


def place(at, rows):
    return pl.ds(pl.multiple_of(at * rows, rows), rows)


class Stages:
    def __init__(self, go, groups, depth):
        self.go, self.groups, self.depth, self.next = go, groups, depth, 0
        self.running = []
        for _ in range(depth):
            self.begin()

    def begin(self):
        if len(self.running) < len(self.groups):
            self.running.append([self.go.start(src, dst) for src, dst in self.groups[len(self.running)]])

    def need(self):
        wait_all(self.running[self.next])
        self.next += 1
        self.begin()


def mix_copies(scal, pieces, dst):
    rows = dst.shape[0] // 2
    return [(src.at[:rows, :], dst.at[place(at, rows), :]) for src, at in zip(pieces, (scal[0], 1 - scal[0]))]


def own_copies(up, down, ups, downs):
    size = ups.shape[2]
    cols = [slice(k * size, (k + 1) * size) for k in range(ups.shape[0])]
    return [([(up.at[:, c], ups.at[k])], [(down.at[c, :], downs.at[c, :])]) for k, c in enumerate(cols)]


def got_copies(scal, pieces, ups, downs):
    order = eighths(scal)
    rows = ups.shape[1] // 8
    copies = []
    for k in range(ups.shape[0]):
        part = slice(k * rows, (k + 1) * rows)
        copies.append(([(src.at[part, :], ups.at[k, place(at, rows), :]) for src, at in zip(pieces, order)], []))
    first, rows = 2 * rows, downs.shape[0] // 8
    for src, at in zip(pieces, order):
        copies[0][1].append((src.at[first : first + rows, :], downs.at[place(at, rows), :]))
    return copies


def row_loop(first, count, step, body, carry=0):
    for at in range(first, first + count, step):
        carry = body(slice(at, at + step), carry)
    return carry


def fold(v):
    return jnp.sum(v.reshape(-1, 8, v.shape[-1]), axis=0)


ROWS = 128


def feed_chunks(tile, low, bias, ups, downs, need, branch, act, slope, done):
    tiles = low.shape[0] // tile
    size = ups.shape[2]
    span = [slice(r * tile, (r + 1) * tile) for r in range(tiles)]
    order = [(j, r) for j in range(ups.shape[0]) for r in range(tiles)]

    def pre(j, r):
        if r == 0:
            need()
        return nn(low[span[r], :], ups[j]) + bias(j)

    ahead = pre(*order[0])
    for t, (j, r) in enumerate(order):
        value, ahead = ahead, (pre(*order[t + 1]) if t + 1 < len(order) else None)
        active, incline = gelu_pair(value)
        active = active.astype(LOW)
        if act is not None:
            act[j, span[r], :] = active
        slope[j, span[r], :] = incline.astype(LOW)
        if r == 0:
            need()
        branch[span[r], :] += nn(active, downs[j * size : (j + 1) * size, :])
        if r == tiles - 1:
            done(j)


def first_kernel(
    tile, scal, mix_bias, gain_ref, shift_ref, down_bias, bias_ref, own_in, got_in, x_in, mix_in, m_0, m_1, up_in, down_in,
    resid_out, low_out, branch_out, act_out, slope_out,
    ctx_own, ctx_got, x_ref, mix_own, mix_got, ups, downs, resid, low, branch, act, slope, sem,
):
    go = Copies(sem)
    groups = [[(own_in, ctx_own), (mix_in, mix_own)], [(got_in, ctx_got)] + mix_copies(scal, (m_0, m_1), mix_got), [(x_in, x_ref)]]
    for up, down in own_copies(up_in, down_in, ups, downs):
        groups += [up, down]
    stages = Stages(go, groups, 3)
    gain, shift, offset, more = (r[...].astype(F32) for r in (gain_ref, shift_ref, mix_bias, down_bias))
    pending = []
    for r in range(x_ref.shape[0] // tile):
        rows = slice(r * tile, (r + 1) * tile)
        if r == 0:
            stages.need()
        attended = nn(ctx_own[rows, :], mix_own[...])
        if r == 0:
            stages.need()
        attended += nn(ctx_got[rows, :], mix_got[...])
        if r == 0:
            stages.need()
        resid[rows, :] = attended

        def norm(at, _):
            value = resid[at, :] + x_ref[at, :].astype(F32) + offset
            resid[at, :] = value
            normed = unit_norm(value)[0] * gain + shift
            low[at, :] = normed.astype(LOW)
            branch[at, :] = normed + more
            return 0

        row_loop(r * tile, tile, ROWS, norm)
    pending += [go.start(resid, resid_out), go.start(low, low_out)]

    def done(j):
        pending.extend([go.start(act.at[j], act_out.at[j]), go.start(slope.at[j], slope_out.at[j])])

    feed_chunks(
        tile, low, lambda j: bias_ref[j : j + 1, :].astype(F32), ups, downs, stages.need, branch, act, slope, done
    )
    pending.append(go.start(branch, branch_out))
    wait_all(pending)


def first_part(scal, ctx_own, ctx_got, x, mix_own, vecs, bias, m_got, up, down, tile=256):
    tokens, width = x.shape
    hidden = up.shape[1] // 2
    both_chunks = (2, tokens, hidden)
    return pl.pallas_call(
        partial(first_kernel, tile),
        in_specs=[SMEM] + vmem_specs(5) + any_specs(8),
        out_specs=any_specs(5),
        out_shape=[
            in_hbm((tokens, width), F32), in_hbm((tokens, width)), in_hbm((tokens, width), F32),
            in_hbm(both_chunks), in_hbm(both_chunks),
        ],
        scratch_shapes=[
            pltpu.VMEM(ctx_own.shape, LOW), pltpu.VMEM(ctx_own.shape, LOW), pltpu.VMEM((tokens, width), LOW),
            pltpu.VMEM(mix_own.shape, LOW), pltpu.VMEM(mix_own.shape, LOW),
            pltpu.VMEM((2, width, hidden), LOW), pltpu.VMEM((2 * hidden, width), LOW),
            pltpu.VMEM((tokens, width), F32), pltpu.VMEM((tokens, width), LOW), pltpu.VMEM((tokens, width), F32),
            pltpu.VMEM(both_chunks, LOW), pltpu.VMEM(both_chunks, LOW), pltpu.SemaphoreType.DMA((24,)),
        ],
        compiler_params=pltpu.CompilerParams(vmem_limit_bytes=48 * MIB),
        cost_estimate=pl.CostEstimate(
            flops=2 * tokens * width * (width + 4 * hidden), bytes_accessed=16 * MIB, transcendentals=4 * tokens * hidden
        ),
        name="first_part",
    )(scal, *vecs, bias, *hbm(ctx_own, ctx_got, x, mix_own, *m_got, up, down))


def second_kernel(
    tile, scal, down_gain, end_shift, m_0, low_in, branch_in, e_in, *rest,
):
    pieces = rest[:8]
    out_out, g_second_out, g_branch_out, slope_out, sum_ref = rest[8:13]
    ups, downs, low, branch, e_ref, slope, out, g_second, g_branch, sem = rest[13:]
    go = Copies(sem)
    (up_0, down), (up_1, _) = got_copies(scal, pieces, ups, downs)
    stages = Stages(go, [[(low_in, low)] + up_0, down + [(branch_in, branch)], up_1, [], [(e_in, e_ref)]], 2)
    pending = []
    bias_at = m_0.shape[0] - 16

    def done(j):
        pending.append(go.start(slope.at[j], slope_out.at[j]))

    feed_chunks(
        tile, low, lambda j: m_0[bias_at + j : bias_at + j + 1, :].astype(F32), ups, downs, stages.need, branch, None, slope, done
    )
    stages.need()
    gain, shift = down_gain[...].astype(F32), end_shift[...].astype(F32)
    width = branch.shape[1]
    sums = tuple(jnp.zeros((8, width), F32) for _ in range(3))

    def norm(at, sums):
        unit, scaled = unit_norm(branch[at, :])
        out[at, :] = (unit * gain + shift).astype(LOW)
        e = e_ref[at, :].astype(F32)
        grad = norm_back(e, unit, scaled, gain)
        g_second[at, :] = grad
        g_branch[at, :] = grad.astype(LOW)
        return tuple(a + fold(b) for a, b in zip(sums, (grad, e * unit, e)))

    half = branch.shape[0] // 2
    for r in range(2):
        sums = row_loop(r * half, half, ROWS, norm, sums)
        at = pl.ds(r * half, half)
        for src, dst in ((g_branch, g_branch_out), (g_second, g_second_out), (out, out_out)):
            pending.append(go.start(src.at[at, :], dst.at[at, :]))
    sum_ref[...] = jnp.concatenate([rows_sum(v) for v in sums] + [jnp.zeros((5, width), F32)], axis=0)
    wait_all(pending)


def second_part(scal, low, end_gain, end_shift, m_0, branch, e, pieces, tile=256):
    tokens, width = low.shape
    hidden = width
    sds = jax.ShapeDtypeStruct
    return pl.pallas_call(
        partial(second_kernel, tile),
        in_specs=[SMEM] + vmem_specs(3) + any_specs(11),
        out_specs=any_specs(4) + vmem_specs(1),
        out_shape=[
            in_hbm((tokens, width)), in_hbm((tokens, width), F32), in_hbm((tokens, width)),
            in_hbm((2, tokens, hidden)), sds((8, width), F32),
        ],
        scratch_shapes=[
            pltpu.VMEM((2, width, hidden), LOW), pltpu.VMEM((2 * hidden, width), LOW), pltpu.VMEM((tokens, width), LOW),
            pltpu.VMEM((tokens, width), F32),
            pltpu.VMEM((tokens, width), LOW), pltpu.VMEM((2, tokens, hidden), LOW), pltpu.VMEM((tokens, width), LOW),
            pltpu.VMEM((tokens, width), F32), pltpu.VMEM((tokens, width), LOW), pltpu.SemaphoreType.DMA((40,)),
        ],
        compiler_params=pltpu.CompilerParams(vmem_limit_bytes=48 * MIB),
        cost_estimate=pl.CostEstimate(
            flops=8 * tokens * width * hidden, bytes_accessed=14 * MIB, transcendentals=4 * tokens * hidden
        ),
        name="second_part",
    )(scal, end_gain, end_shift, *hbm(m_0, low, branch, e, *pieces))


def back_kernel(
    tile, scal, gain_ref, g_branch_in, mix_in, g_second_in, resid_in, slope_a, slope_b, m_0, m_1, up_in, down_in, *rest
):
    pieces = rest[:8]
    g_first_out, g_att_out, ctx_a_out, ctx_b_out, g_pre_out, sum_ref = rest[8:14]
    ups, downs, g_branch, mix_own, mix_got, slope, grad, resid, g_pre, g_att, g_ctx, sem = rest[14:]
    half = ups.shape[0] // 2
    size = ups.shape[2]
    go = Copies(sem)
    copies = own_copies(up_in, down_in, ups.at[:half], downs.at[: half * size])
    copies += got_copies(scal, pieces, ups.at[half:], downs.at[half * size :])
    slopes = [(s.at[j], slope.at[k * half + j]) for k, s in enumerate((slope_a, slope_b)) for j in range(half)]
    groups = []
    for k, (up, down) in enumerate(copies):
        groups += [down + [slopes[k]], up]
    groups[0] = [(g_branch_in, g_branch)] + groups[0]
    groups[1] = groups[1] + [(g_second_in, grad)]
    groups += [[(resid_in, resid), (mix_in, mix_own)] + mix_copies(scal, (m_0, m_1), mix_got)]
    stages = Stages(go, groups, 3)
    tokens = grad.shape[0]
    tiles = tokens // tile
    span = [slice(r * tile, (r + 1) * tile) for r in range(tiles)]
    order = [(j, r) for j in range(2 * half) for r in range(tiles)]
    pending = []

    def g_active(j, r):
        if r == 0:
            stages.need()
        return nt(g_branch[span[r], :], downs[j * size : (j + 1) * size, :])

    ahead = g_active(*order[0])
    for t, (j, r) in enumerate(order):
        value, ahead = ahead, (g_active(*order[t + 1]) if t + 1 < len(order) else None)
        if r == 0:
            stages.need()
        low = (value * slope[j, span[r], :].astype(F32)).astype(LOW)
        if j < half:
            g_pre[j, span[r], :] = low
            if r == tiles - 1:
                pending.append(go.start(g_pre.at[j], g_pre_out.at[j]))
        grad[span[r], :] += nt(low, ups[j])
    stages.need()
    gain = gain_ref[...].astype(F32)
    width = grad.shape[1]
    sums = tuple(jnp.zeros((8, width), F32) for _ in range(3))

    def norm(at, sums):
        unit, scaled = unit_norm(resid[at, :])
        e = grad[at, :]
        first = norm_back(e, unit, scaled, gain)
        grad[at, :] = first
        g_att[at, :] = first.astype(LOW)
        return tuple(a + fold(b) for a, b in zip(sums, (first, e * unit, e)))

    for r in range(tiles):
        sums = row_loop(r * tile, tile, ROWS, norm, sums)
        g_ctx[1, span[r], :] = nt(g_att[span[r], :], mix_got[...]).astype(LOW)
        g_ctx[0, span[r], :] = nt(g_att[span[r], :], mix_own[...]).astype(LOW)
        at = pl.ds(r * tile, tile)
        for src, dst in ((g_ctx.at[1], ctx_b_out), (g_ctx.at[0], ctx_a_out), (g_att, g_att_out), (grad, g_first_out)):
            pending.append(go.start(src.at[at, :], dst.at[at, :]))
    sum_ref[...] = jnp.concatenate([rows_sum(v) for v in sums] + [jnp.zeros((5, width), F32)], axis=0)
    wait_all(pending)


def back_part(scal, g_branch, gain, mix_own, g_second, resid, slopes, m_got, up, down, pieces, tile=256):
    tokens, width = g_branch.shape
    part = mix_own.shape[0]
    hidden = up.shape[1] // 2
    sds = jax.ShapeDtypeStruct
    return pl.pallas_call(
        partial(back_kernel, tile),
        in_specs=[SMEM] + vmem_specs(1) + any_specs(18),
        out_specs=any_specs(5) + vmem_specs(1),
        out_shape=[
            in_hbm((tokens, width), F32), in_hbm((tokens, width)), in_hbm((tokens, part)), in_hbm((tokens, part)),
            in_hbm((2, tokens, hidden)), sds((8, width), F32),
        ],
        scratch_shapes=[
            pltpu.VMEM((4, width, hidden), LOW), pltpu.VMEM((4 * hidden, width), LOW), pltpu.VMEM((tokens, width), LOW),
            pltpu.VMEM((part, width), LOW), pltpu.VMEM((part, width), LOW),
            pltpu.VMEM((4, tokens, hidden), LOW), pltpu.VMEM((tokens, width), F32), pltpu.VMEM((tokens, width), F32),
            pltpu.VMEM((2, tokens, hidden), LOW), pltpu.VMEM((tokens, width), LOW), pltpu.VMEM((2, tokens, part), LOW),
            pltpu.SemaphoreType.DMA((60,)),
        ],
        compiler_params=pltpu.CompilerParams(vmem_limit_bytes=50 * MIB),
        cost_estimate=pl.CostEstimate(flops=16 * tokens * width * hidden, bytes_accessed=24 * MIB, transcendentals=0),
        name="back_part",
    )(scal, gain, *hbm(g_branch, mix_own, g_second, resid, *slopes, *m_got, up, down, *pieces))


def weight_kernel(
    pick, bias_ref, act_in, g_pre_in, low_in, low_got_in, g_branch_in, g_branch_got_in, up_in, down_in, out, bias_out,
    act, g_pre, low, low_got, g_branch, g_branch_got, up, down, grads, sem,
):
    go = Copies(sem)
    width, hidden = up.shape
    at = pl.multiple_of(pick[0] * hidden, hidden)
    groups = [
        [(low_in, low), (g_pre_in.at[pick[0]], g_pre)],
        [(low_got_in, low_got), (up_in.at[:, pl.ds(at, hidden)], up)],
        [(g_branch_got_in, g_branch_got), (down_in.at[pl.ds(at, hidden), :], down)],
        [(act_in.at[pick[0]], act), (g_branch_in, g_branch)],
    ]
    stages = Stages(go, groups, 2)
    bias = bias_ref[...].astype(F32)
    stages.need()
    up_own = tn(low[...], g_pre[...])
    stages.need()
    pre = nn(low_got[...], up[...]) + jnp.where(pick[0] == 0, bias[0:1], bias[1:2])
    stages.need()
    g_active = nt(g_branch_got[...], down[...])
    active, incline = gelu_pair(pre)
    g_pre_got = g_active * incline
    bias_out[...] = rows_sum(g_pre_got) + rows_sum(g_pre[...].astype(F32))
    grads[:width, :] = (up_own + tn(low_got[...], g_pre_got.astype(LOW))).astype(LOW)
    first = go.start(grads.at[:width, :], out.at[:width, :])
    stages.need()
    grads[width:, :] = (tn(act[...], g_branch[...]) + tn(active.astype(LOW), g_branch_got[...])).astype(LOW)
    wait_all([go.start(grads.at[width:, :], out.at[width:, :]), first])


def weight_part(pick, act, g_pre, low, low_got, g_branch, g_branch_got, up, down, bias):
    _, tokens, hidden = act.shape
    width = low.shape[1]
    assert hidden == width
    token, square = pltpu.VMEM((tokens, width), LOW), pltpu.VMEM((width, hidden), LOW)
    return pl.pallas_call(
        weight_kernel,
        in_specs=[SMEM] + vmem_specs(1) + any_specs(8),
        out_specs=any_specs(1) + vmem_specs(1),
        out_shape=[in_hbm((width + hidden, width)), jax.ShapeDtypeStruct((1, hidden), F32)],
        scratch_shapes=[token] * 6 + [square] * 2 + [pltpu.VMEM((width + hidden, width), LOW), pltpu.SemaphoreType.DMA((10,))],
        compiler_params=pltpu.CompilerParams(vmem_limit_bytes=50 * MIB),
        cost_estimate=pl.CostEstimate(
            flops=12 * tokens * width * hidden, bytes_accessed=10 * MIB, transcendentals=2 * tokens * hidden
        ),
        name="weight_part",
    )(pick, bias, *hbm(act, g_pre, low, low_got, g_branch, g_branch_got, up, down))


def mix_grad_kernel(ctx_own, ctx_got, g_att, mid_sums, end_sums, own_out, got_out):
    own_out[...] = tn(ctx_own[...], g_att[...]).astype(LOW)
    part, width = own_out.shape
    got_out[:part, :] = tn(ctx_got[...], g_att[...]).astype(LOW)
    small = jnp.concatenate([mid_sums[:3, :], end_sums[:3, :], jnp.zeros((10, width), F32)], axis=0)
    got_out[part:, :] = small.astype(LOW)


def mix_grad(ctx_own, ctx_got, g_att, mid_sums, end_sums):
    tokens, width = g_att.shape
    part = ctx_own.shape[1]
    return pl.pallas_call(
        mix_grad_kernel,
        in_specs=vmem_specs(5),
        out_specs=vmem_specs(2),
        out_shape=[in_hbm((part, width)), in_hbm((part + 16, width))],
        compiler_params=pltpu.CompilerParams(vmem_limit_bytes=24 * MIB),
        cost_estimate=pl.CostEstimate(flops=4 * tokens * width * part, bytes_accessed=4 * MIB, transcendentals=0),
        name="mix_grad",
    )(*hbm(ctx_own, ctx_got, g_att), mid_sums, end_sums)


def late_kernel(
    scal, own_ref, got_ref, g_ref, mix_own, mix_other, mid_sums, end_sums, bias_keep, bias_send, keep, send, out
):
    half, width = own_ref.shape
    cols = g_ref.shape[1]
    out[:, :cols] = (tn(own_ref[...], g_ref[:half, :]) + tn(got_ref[...], g_ref[half:, :])).astype(LOW)
    part = mix_own.shape[0]
    for k in range(2):
        side = slice(k * part, (k + 1) * part)
        total = mix_own[:, side].astype(F32) + mix_other[:part, side].astype(F32)
        out[side, cols : cols + part] = total.astype(LOW)
    sums = nn(jnp.ones((8, 2 * half), LOW), g_ref[...])[:1]
    sums = jnp.concatenate([sums[:, :part], sums[:, 2 * part :]], axis=1)
    small = jnp.concatenate([mid_sums[:3, :], end_sums[:3, :]], axis=0) + mix_other[part : part + 6, :].astype(F32)
    first = scal[0] == 0
    ups = [jnp.where(first, bias_keep[...], bias_send[...]), jnp.where(first, bias_send[...], bias_keep[...])]
    rows = jnp.concatenate([small, *ups, sums, jnp.zeros((PAIR - 9, width), F32)], axis=0)
    out[:, cols + part :] = jnp.transpose(rows).astype(LOW)
    for c in range(2):

        @pl.when(scal[0] == c)
        def _():
            keep[...] = out[c * part : (c + 1) * part, :]
            send[...] = out[(1 - c) * part : (2 - c) * part, :]


def late_grads(scal, own, got, g, mix_own, mix_other, sums):
    tokens, width = own.shape
    part = mix_own.shape[0]
    assert 2 * part == width
    cols = g.shape[1] + part + PAIR
    return pl.pallas_call(
        late_kernel,
        in_specs=[SMEM] + vmem_specs(9),
        out_specs=vmem_specs(2),
        out_shape=[in_hbm((part, cols))] * 2,
        scratch_shapes=[pltpu.VMEM((width, cols), LOW)],
        compiler_params=pltpu.CompilerParams(vmem_limit_bytes=40 * MIB),
        cost_estimate=pl.CostEstimate(flops=4 * tokens * width * g.shape[1], bytes_accessed=8 * MIB, transcendentals=0),
        name="late_grads",
    )(scal, *hbm(own, got, g, mix_own, mix_other), *sums)


def finish_feed_kernel(scal, *refs):
    up_out, down_out = refs[4:]
    width = down_out.shape[2]
    for k in range(2):
        core, side = scal[0] ^ k, scal[1 + k]
        for n in range(2):
            piece = refs[2 * k + n][...].astype(F32)

            @pl.when(side == n)
            def _():
                up_out[:, pl.ds(pl.multiple_of(core * width, width), width)] = piece

            @pl.when(side != n)
            def _():
                down_out[core] = piece


def finish_feed(scal, pieces, steps=4):
    width = pieces[0].shape[1]
    rows = width // steps
    block = pl.BlockSpec((rows, width), lambda i, scal: (i, 0))
    up, down = pl.pallas_call(
        finish_feed_kernel,
        grid_spec=pltpu.PrefetchScalarGridSpec(
            num_scalar_prefetch=1,
            grid=(steps,),
            in_specs=[block] * 4,
            out_specs=[
                pl.BlockSpec((rows, 2 * width), lambda i, scal: (i, 0)),
                pl.BlockSpec((2, rows, width), lambda i, scal: (0, i, 0)),
            ],
        ),
        out_shape=[in_hbm((width, 2 * width), F32), in_hbm((2, width, width), F32)],
        compiler_params=pltpu.CompilerParams(vmem_limit_bytes=32 * MIB),
        cost_estimate=pl.CostEstimate(flops=0, bytes_accessed=14 * MIB, transcendentals=0),
        name="finish_feed",
    )(scal, *pieces)
    return up, down.reshape(2 * width, width)


def finish_late_kernel(scal, *refs):
    q_out, k_out, v_out, mix_out, small_out = refs[4:]
    part = q_out.shape[1]
    half = part // 2
    for k in range(2):
        core = scal[0] ^ k
        for n in range(2):
            side = scal[1 + k] ^ n
            piece = refs[2 * k + n]
            rows = pl.ds(pl.multiple_of(core * part + side * half, half), half)
            for m, out in enumerate((q_out, k_out, v_out)):
                out[rows, :] = piece[:, m * part : (m + 1) * part].astype(F32)
            some = pl.ds(pl.multiple_of(side * half, half), half)
            mix_out[some, pl.ds(pl.multiple_of(core * part, part), part)] = piece[:, 3 * part : 4 * part].astype(F32)
            small = jnp.transpose(piece[:, 4 * part :].astype(F32))[:16]
            for at in range(4):

                @pl.when(2 * core + side == at)
                def _():
                    small_out[:, at * half : (at + 1) * half] = small


def finish_late(scal, pieces):
    part = 2 * pieces[0].shape[0]
    sds = jax.ShapeDtypeStruct
    return pl.pallas_call(
        finish_late_kernel,
        in_specs=[SMEM] + vmem_specs(4),
        out_specs=vmem_specs(5),
        out_shape=[in_hbm((2 * part, part), F32)] * 3 + [in_hbm((part, 2 * part), F32), sds((16, 2 * part), F32)],
        compiler_params=pltpu.CompilerParams(vmem_limit_bytes=32 * MIB),
        cost_estimate=pl.CostEstimate(flops=0, bytes_accessed=8 * MIB, transcendentals=0),
        name="finish_late",
    )(scal, *pieces)


def swap(value, axis, bit):
    even, odd = bit if isinstance(bit, tuple) else (bit, bit)
    return lax.ppermute(value, axis, [(i, i ^ (odd if i & 1 else even)) for i in range(lax.axis_size(axis))])


def wide(value):
    return value.astype(F32)


def cut(value, at, size):
    return lax.dynamic_slice_in_dim(value, at, size, 0)


def side_of(dp, mask):
    if isinstance(mask, tuple):
        mask = jnp.where(dp & 1, mask[1], mask[0])
    return ((dp & mask) != 0).astype(jnp.int32)


def dp_masks():
    return [1 << i for i in range(lax.axis_size("dp").bit_length() - 1)]


def total(terms):
    return sum(wide(t) for t in terms).astype(LOW)


class Chain:
    def __init__(self, dp, masks, terms):
        self.dp, self.masks, self.terms = dp, masks, terms
        self.step, self.value, self.sent, self.got = 0, None, None, None

    def start(self, *others):
        last = len(self.masks) - 1
        if self.step < last:
            mask = self.masks[self.step]
            half, mine = self.terms[0].shape[0] // 2, side_of(self.dp, mask)
            self.sent = total([cut(t, (1 - mine) * half, half) for t in self.terms])
            self.terms = [cut(t, mine * half, half) for t in self.terms]
        elif self.step == last:
            mask = self.masks[last]
            self.sent = self.value = total(self.terms)
        else:
            mask = self.masks[2 * last - self.step]
            self.sent = self.value
        if others:
            self.sent = after(self.sent, *others)
        self.got = swap(self.sent, "dp", mask)

    def finish(self, *others):
        got = after(self.got, *others) if others else self.got
        last = len(self.masks) - 1
        if self.step < last:
            self.terms = self.terms + [got]
        elif self.step == last:
            self.value = (wide(self.value) + wide(got)).astype(LOW)
        elif self.step < 2 * last:
            side = side_of(self.dp, self.masks[2 * last - self.step])
            self.value = jnp.where(side == 1, jnp.concatenate([got, self.value]), jnp.concatenate([self.value, got]))
        self.step += 1
        self.got = got

    @property
    def done(self):
        return self.step == 2 * len(self.masks) - 1


def per_device(
    inputs, upstream, lengths, query_weight, key_weight, value_weight, query_bias, value_bias, mix_weight, mix_bias,
    mid_gain, mid_shift, up_weight, up_bias, down_weight, down_bias, end_gain, end_shift,
):
    dp = lax.axis_index("dp").astype(jnp.int32)
    side = lax.axis_index("tensor").astype(jnp.int32).reshape(1)
    masks = dp_masks()
    core = dp & 1
    order = [(masks[1], masks[2]), (masks[2], masks[1])] + masks[3:]
    scal = jnp.stack([core] + [side_of(dp, mask) for mask in order[:-1]])
    tokens, width = inputs.shape
    part = query_weight.shape[1]
    own_hidden = up_weight.shape[1]
    hidden = own_hidden // 2
    row = lambda v: v.reshape(1, -1)
    across = lambda v: swap(v, "tensor", 1)

    x_got = across(inputs)
    pairs = tuple(range(part // PAIR))
    qkv_weight = jnp.concatenate([query_weight, key_weight, value_weight], axis=1)
    qkv_bias = jnp.concatenate([wide(query_bias), jnp.zeros((part,), F32), wide(value_bias)])
    bias_own = up_bias.reshape(2, hidden)
    m_piece = jnp.concatenate([cut(mix_weight, core * (part // 2), part // 2), bias_own, jnp.zeros((14, width), LOW)])
    eighth = 4 * core + 2 * side_of(dp, order[0]) + side_of(dp, order[1])
    up_piece = cut(up_weight, eighth * (width // 8), width // 8)
    down_piece = cut(down_weight, eighth * (own_hidden // 8), own_hidden // 8)
    piece = jnp.concatenate([up_piece[:, :hidden], up_piece[:, hidden:], down_piece])

    def project(v):
        return (nn(v, qkv_weight) + qkv_bias).astype(LOW)

    own = project(inputs)
    x_got = after(x_got, own, m_piece, piece)
    m_0, piece_0 = across(after(m_piece, x_got)), across(after(piece, x_got))
    got = project(x_got)
    ctx_own, ctx_send, lse = attend(lengths, side, own, got, pairs)
    ctx_send, m_0, piece_0 = lax.optimization_barrier((ctx_send, m_0, piece_0))
    ctx_got = across(ctx_send)
    m_got = [m_0, swap(m_0, "dp", 1)]
    piece_1 = swap(piece_0, "dp", order[0])
    piece_2, piece_3 = swap(piece_0, "dp", order[1]), swap(piece_1, "dp", order[1])
    resid, low, branch, act, slope_own = first_part(
        scal, ctx_own, ctx_got, inputs, mix_weight, [row(v) for v in (mix_bias, mid_gain, mid_shift, down_bias)], bias_own,
        m_got, up_weight, down_weight,
    )
    low_got = across(low)
    pieces = [piece_0, piece_1, after(piece_2, low), after(piece_3, low)]
    pieces += [swap(v, "dp", 1) for v in pieces]
    outputs, g_second, g_branch, slope_got, end_sums = second_part(
        scal, low, row(end_gain), row(end_shift), m_0, branch, upstream, pieces
    )
    g_branch_got = across(g_branch)
    g_first, g_att, g_ctx_own, g_ctx_send, g_pre, mid_sums = back_part(
        scal, g_branch, row(mid_gain), mix_weight, g_second, resid, (slope_own, slope_got),
        m_got, up_weight, down_weight, pieces,
    )
    g_ctx_got = across(g_ctx_send)
    mix_own, mix_send = mix_grad(ctx_own, ctx_got, after(g_att, low_got), mid_sums, end_sums)
    shared = (low, low_got, g_branch, g_branch_got, up_weight, down_weight, bias_own)
    send, bias_send = weight_part((1 - core).reshape(1), act, after(g_pre, mix_own), *shared)
    mix_other = across(after(mix_send, g_ctx_got))
    send = after(send, g_ctx_got)
    keep, bias_keep = weight_part(after(core.reshape(1), send), act, g_pre, *shared)
    feed = Chain(dp, order, [keep, swap(send, "dp", 1)])
    feed.start()
    g_qkv = attend_back(
        lengths, side, own, got, g_ctx_own, after(g_ctx_got, feed.sent), ctx_own, ctx_send, lse, pairs,
    )
    feed.finish(g_qkv)
    mix_other = after(mix_other, g_qkv)
    g_qkv = after(g_qkv, mix_other, feed.got)
    feed.start()
    late_keep, late_send = late_grads(
        scal, inputs, x_got, g_qkv, mix_own, mix_other, (mid_sums, end_sums, bias_keep, bias_send)
    )
    feed.finish(late_keep)
    proj = Chain(dp, order, [late_keep, swap(after(late_send, feed.got), "dp", 1)])
    proj.start()
    feed.start(proj.sent)
    input_got = across(nt(after(g_qkv, feed.sent)[tokens:], qkv_weight).astype(LOW))
    proj.finish(feed.sent)
    proj.start()
    proj.finish()
    feed.finish(proj.got)
    input_got = after(input_got, proj.got)
    proj.start(feed.got, input_got)
    input_own = g_first + nt(after(g_qkv, proj.sent)[:tokens], qkv_weight)
    input_grad = (input_own + wide(input_got)).astype(LOW)
    feed.start()
    proj.finish(feed.sent, input_grad)
    while not feed.done:
        proj.start()
        feed.finish(proj.sent)
        if not feed.done:
            feed.start()
            proj.finish(feed.sent)
    feed_pieces = [feed.value, feed.got]
    feed_pieces += [swap(v, "dp", 1) for v in feed_pieces]
    up_grad, down_grad = finish_feed(scal, feed_pieces)
    proj.finish(up_grad)
    assert proj.done
    late_pieces = [proj.value, proj.got]
    late_pieces += [swap(v, "dp", 1) for v in late_pieces]
    *qkv, mix_grads, small = finish_late(scal, late_pieces)
    return (
        outputs,
        input_grad,
        qkv[0],
        qkv[1],
        qkv[2],
        small[8, :part],
        small[8, part:],
        mix_grads,
        small[0],
        small[1],
        small[2],
        up_grad,
        small[6:8].reshape(own_hidden),
        down_grad,
        small[3],
        small[4],
        small[5],
    )


def solution(mesh):
    placed = (
        P(("dp", "tensor"), None),
        P(("dp", "tensor"), None),
        P("dp", None),
        P(None, "tensor"),
        P(None, "tensor"),
        P(None, "tensor"),
        P("tensor"),
        P("tensor"),
        P("tensor", None),
        P(),
        P(),
        P(),
        P(None, "tensor"),
        P("tensor"),
        P("tensor", None),
        P(),
        P(),
        P(),
    )
    return jax.shard_map(
        per_device,
        mesh=mesh,
        in_specs=placed,
        out_specs=(
            P(("dp", "tensor"), None),
            P(("dp", "tensor"), None),
            P(None, "tensor"),
            P(None, "tensor"),
            P(None, "tensor"),
            P("tensor"),
            P("tensor"),
            P("tensor", None),
            P(),
            P(),
            P(),
            P(None, "tensor"),
            P("tensor"),
            P("tensor", None),
            P(),
            P(),
            P(),
        ),
        check_vma=False,
    )
```

```python
from functools import partial

import jax
import jax.numpy as jnp
from jax import lax
from jax.experimental import pallas as pl
from jax.experimental.pallas import tpu as pltpu
from jax.sharding import PartitionSpec as P

HEAD_DIM = 64
PAIR = 128
SEQ = 1024
LOW = jnp.bfloat16
F32 = jnp.float32
FAR = -1e30


def nt(a, b):
    return lax.dot_general(a, b, (((1,), (1,)), ((), ())), preferred_element_type=F32)


def tn(a, b):
    return lax.dot_general(a, b, (((0,), (0,)), ((), ())), preferred_element_type=F32)


def nn(a, b):
    return lax.dot_general(a, b, (((1,), (0,)), ((), ())), preferred_element_type=F32)


def seg_ends(len_ref):
    ends, total = [], jnp.int32(0)
    for j in range(len_ref.shape[1]):
        total = total + len_ref[0, j]
        ends.append(total)
    return ends


def seg_marks(ends, shift):
    pos = (lax.broadcasted_iota(jnp.int32, (SEQ, PAIR), 0) + shift) & (SEQ - 1)
    lane = lax.broadcasted_iota(jnp.int32, (SEQ, PAIR), 1) & (HEAD_DIM - 1)
    seg = jnp.zeros((SEQ, PAIR), jnp.int32)
    for e in ends:
        seg = seg + (pos >= e).astype(jnp.int32)
    own = seg == lane
    used = lane < len(ends)
    key_mark = jnp.where(own, 1.0, 0.0)
    query_mark = jnp.where(used & jnp.logical_not(own), FAR, 0.0)
    return key_mark, query_mark


def key_range(ends, first, size, step):
    begin, stop = jnp.int32(0), jnp.int32(SEQ)
    for e in ends:
        begin = jnp.where(e <= first, e, begin)
    for e in reversed(ends):
        stop = jnp.where(e >= first + size, e, stop)
    return (begin // step) * step, stop


def head_mask(h):
    lane = lax.broadcasted_iota(jnp.int32, (1, PAIR), 1)
    return (lane >= h * HEAD_DIM) & (lane < (h + 1) * HEAD_DIM)


def over_queries(ends, shift, bq, bk, step, body):
    most = -(-SEQ // bk)

    def one(t, _):
        q_at = pl.multiple_of(t * bq, bq)
        q_pos = (q_at + shift) & (SEQ - 1)
        begin, stop = key_range(ends, q_pos, bq, step)
        count = (stop - begin + bk - 1) // bk
        begin = jnp.minimum(begin, SEQ - count * bk)
        begin = pl.multiple_of(begin, step)
        for n in range(1, most + 1):

            @pl.when(count == n)
            def _():
                body(q_at, begin, n)

        return 0

    lax.fori_loop(0, SEQ // bq, one, 0)


def true_order(dst, src, shift):
    half = SEQ // 2
    dst[pl.ds(pl.multiple_of(shift, half), half), :] = src[:half]
    dst[pl.ds(pl.multiple_of(half - shift, half), half), :] = src[half:]


def both(own_ref, got_ref, at, pair):
    cols = slice(at + pair * PAIR, at + (pair + 1) * PAIR)
    return jnp.concatenate([own_ref[:, cols], got_ref[:, cols]], axis=0)


def attend_kernel(bq, bk, step, ahead, pairs, len_ref, side_ref, own_ref, got_ref, ctx_own, ctx_send, lse_ref, qh, kh, vt, acc, tot):
    shift = side_ref[0] * (SEQ // 2)
    half = SEQ // 2
    ends = seg_ends(len_ref)
    key_mark, query_mark = seg_marks(ends, shift)
    width = own_ref.shape[1] // 3
    heads = 2 * len(pairs)
    for p, pair in enumerate(pairs):
        cols = slice(p * PAIR, (p + 1) * PAIR)
        q = both(own_ref, got_ref, 0, pair).astype(F32) * 0.125
        k = both(own_ref, got_ref, width, pair).astype(F32)
        for h in range(2):
            qh[2 * p + h] = jnp.where(head_mask(h), q, query_mark).astype(LOW)
            true_order(kh.at[2 * p + h], jnp.where(head_mask(h), k, key_mark).astype(LOW), shift)
        vals = jnp.transpose(both(own_ref, got_ref, 2 * width, pair).astype(F32)).astype(LOW)
        vt[cols, pl.ds(pl.multiple_of(shift, half), half)] = vals[:, :half]
        vt[cols, pl.ds(pl.multiple_of(half - shift, half), half)] = vals[:, half:]

    def body(q_at, begin, n):
        qs = pl.ds(q_at, bq)
        at = [pl.ds(pl.multiple_of(begin + i * bk, step), bk) for i in range(n)]

        def score(h):
            query = qh[h, qs, :]
            return [nt(kh[h, at[i], :], query) for i in range(n)]

        ready = [score(h) for h in range(ahead)]
        for h in range(heads):
            dims = slice(h * HEAD_DIM, (h + 1) * HEAD_DIM)
            if h + ahead < heads:
                ready.append(score(h + ahead))
            parts = ready[h]
            top = jnp.max(parts[0], axis=0, keepdims=True)
            for s in parts[1:]:
                top = jnp.maximum(top, jnp.max(s, axis=0, keepdims=True))
            total, out = 0.0, 0.0
            for i, s in enumerate(parts):
                p = jnp.exp(s - top)
                total = total + jnp.sum(p, axis=0, keepdims=True)
                out = out + nn(vt[dims, at[i]], p.astype(LOW))
            acc[dims, qs] = out * (1.0 / total)
            tot[h : h + 1, qs] = top + jnp.log(total)

    over_queries(ends, shift, bq, bk, step, body)
    context = jnp.transpose(acc[...]).astype(LOW)
    ctx_own[...] = context[:half]
    ctx_send[...] = context[half:]
    lse_ref[...] = tot[...]


def attend(lengths, side, own, got, pairs, bq=256, bk=256, step=128, ahead=2):
    heads = 2 * len(pairs)
    width = heads * HEAD_DIM
    assert heads <= 8
    smem = pl.BlockSpec(memory_space=pltpu.SMEM)
    vmem = pl.BlockSpec(memory_space=pltpu.VMEM)
    return pl.pallas_call(
        partial(attend_kernel, bq, bk, step, ahead, pairs),
        in_specs=[smem, smem, vmem, vmem],
        out_specs=[vmem, vmem, vmem],
        out_shape=[
            jax.ShapeDtypeStruct((SEQ // 2, width), LOW),
            jax.ShapeDtypeStruct((SEQ // 2, width), LOW),
            jax.ShapeDtypeStruct((8, SEQ), F32),
        ],
        scratch_shapes=[
            pltpu.VMEM((heads, SEQ, PAIR), LOW),
            pltpu.VMEM((heads, SEQ, PAIR), LOW),
            pltpu.VMEM((width, SEQ), LOW),
            pltpu.VMEM((width, SEQ), F32),
            pltpu.VMEM((8, SEQ), F32),
        ],
        compiler_params=pltpu.CompilerParams(vmem_limit_bytes=32 * 1024 * 1024),
        name="attend",
    )(lengths, side, own, got)


def attend_back_kernel(
    bq, bk, step, ahead, pairs, len_ref, side_ref, own_ref, got_ref, do_own_ref, do_got_ref,
    ctx_own, ctx_send, lse_ref, g_ref, qh, qz, dom, kh, vals, kt, inner, dqt, dk, dv,
):
    shift = side_ref[0] * (SEQ // 2)
    half = SEQ // 2
    ends = seg_ends(len_ref)
    key_mark, query_mark = seg_marks(ends, shift)
    width = own_ref.shape[1] // 3
    heads = 2 * len(pairs)
    first = pl.ds(pl.multiple_of(shift, half), half)
    second = pl.ds(pl.multiple_of(half - shift, half), half)
    for p, pair in enumerate(pairs):
        cols = slice(p * PAIR, (p + 1) * PAIR)
        q = both(own_ref, got_ref, 0, pair).astype(F32) * 0.125
        k = both(own_ref, got_ref, width, pair).astype(F32)
        do = both(do_own_ref, do_got_ref, 0, pair).astype(F32)
        for h in range(2):
            mask = head_mask(h)
            at = 2 * p + h
            qh[at] = jnp.where(mask, q, query_mark).astype(LOW)
            qz[at] = jnp.where(mask, q, 0.0).astype(LOW)
            dom[at] = jnp.where(mask, do, 0.0).astype(LOW)
            true_order(kh.at[at], jnp.where(mask, k, key_mark).astype(LOW), shift)
        true_order(vals.at[p], both(own_ref, got_ref, 2 * width, pair), shift)
        turned = jnp.transpose(k).astype(LOW)
        kt[cols, first] = turned[:, :half]
        kt[cols, second] = turned[:, half:]
        prod = jnp.transpose(do * both(ctx_own, ctx_send, 0, p).astype(F32))
        for h in range(2):
            inner[2 * p + h : 2 * p + h + 1, :] = jnp.sum(
                prod[h * HEAD_DIM : (h + 1) * HEAD_DIM], axis=0, keepdims=True
            )
    dk[...] = jnp.zeros_like(dk)
    dv[...] = jnp.zeros_like(dv)

    def body(q_at, begin, n):
        qs = pl.ds(q_at, bq)
        at = [pl.ds(pl.multiple_of(begin + i * bk, step), bk) for i in range(n)]

        def score(h):
            query, grad = qh[h, qs, :], dom[h, qs, :]
            return [(nt(kh[h, at[i], :], query), nt(vals[h // 2, at[i], :], grad)) for i in range(n)]

        ready = [score(h) for h in range(ahead)]
        for h in range(heads):
            if h + ahead < heads:
                ready.append(score(h + ahead))
            dims = slice(h * HEAD_DIM, (h + 1) * HEAD_DIM)
            plain, grad = qz[h, qs, :], dom[h, qs, :]
            lse, mean = lse_ref[h : h + 1, qs], inner[h : h + 1, qs]
            out = 0.0
            for i, (s, gp) in enumerate(ready[h]):
                p = jnp.exp(s - lse)
                ds = (p * (gp - mean)).astype(LOW)
                dv[h // 2, at[i], :] += nn(p.astype(LOW), grad)
                dk[h // 2, at[i], :] += nn(ds, plain)
                out = out + nn(kt[dims, at[i]], ds)
            dqt[dims, qs] = out

    over_queries(ends, shift, bq, bk, step, body)
    part = heads * HEAD_DIM
    g_ref[:, :part] = (jnp.transpose(dqt[...]) * 0.125).astype(LOW)
    for p in range(heads // 2):
        for at, src in ((part + p * PAIR, dk), (2 * part + p * PAIR, dv)):
            g_ref[:half, at : at + PAIR] = src[p, first, :].astype(LOW)
            g_ref[half:, at : at + PAIR] = src[p, second, :].astype(LOW)


def attend_back(lengths, side, own, got, g_own, g_got, ctx_own, ctx_send, lse, pairs, bq=256, bk=256, step=128, ahead=1):
    heads = 2 * len(pairs)
    width = heads * HEAD_DIM
    smem = pl.BlockSpec(memory_space=pltpu.SMEM)
    vmem = pl.BlockSpec(memory_space=pltpu.VMEM)
    return pl.pallas_call(
        partial(attend_back_kernel, bq, bk, step, ahead, pairs),
        in_specs=[smem, smem] + [vmem] * 7,
        out_specs=vmem,
        out_shape=jax.ShapeDtypeStruct((SEQ, 3 * width), LOW),
        scratch_shapes=[
            pltpu.VMEM((heads, SEQ, PAIR), LOW),
            pltpu.VMEM((heads, SEQ, PAIR), LOW),
            pltpu.VMEM((heads, SEQ, PAIR), LOW),
            pltpu.VMEM((heads, SEQ, PAIR), LOW),
            pltpu.VMEM((heads // 2, SEQ, PAIR), LOW),
            pltpu.VMEM((width, SEQ), LOW),
            pltpu.VMEM((8, SEQ), F32),
            pltpu.VMEM((width, SEQ), F32),
            pltpu.VMEM((heads // 2, SEQ, PAIR), F32),
            pltpu.VMEM((heads // 2, SEQ, PAIR), F32),
        ],
        compiler_params=pltpu.CompilerParams(vmem_limit_bytes=48 * 1024 * 1024),
        name="attend_back",
    )(lengths, side, *(pltpu.with_memory_space_constraint(v, pltpu.HBM) for v in (own, got, g_own, g_got, ctx_own, ctx_send)), lse)


MIB = 1024 * 1024


def unit_norm(resid):
    middle = jnp.mean(resid, axis=-1, keepdims=True)
    centered = resid - middle
    spread = jnp.mean(centered * centered, axis=-1, keepdims=True)
    scaled = lax.rsqrt(spread + 1e-06)
    return centered * scaled, scaled


def norm_back(grad, unit, scaled, gain):
    weighted = grad * gain
    first_mean = jnp.mean(weighted, axis=-1, keepdims=True)
    second_mean = jnp.mean(weighted * unit, axis=-1, keepdims=True)
    return scaled * (weighted - first_mean - unit * second_mean)


def gelu_pair(v):
    cdf = 0.5 + 0.5 * lax.erf(v * 0.7071067811865476)
    bell = jnp.exp(-0.5 * (v * v))
    return v * cdf, cdf + (v * 0.3989422804014327) * bell


def rows_sum(v):
    return jnp.sum(v, axis=0, keepdims=True)


def after(value, *others):
    return lax.optimization_barrier((value, *others))[0]


def vmem_specs(count):
    return [pl.BlockSpec(memory_space=pltpu.VMEM)] * count


def any_specs(count):
    return [pl.BlockSpec(memory_space=pl.ANY)] * count


SMEM = pl.BlockSpec(memory_space=pltpu.SMEM)


def hbm(*arrays):
    return [pltpu.with_memory_space_constraint(v, pltpu.HBM) for v in arrays]


def in_hbm(shape, dtype=LOW):
    return pltpu.HBM(shape, dtype)


class Copies:
    def __init__(self, sem):
        self.sem, self.count = sem, 0

    def start(self, src, dst):
        copy = pltpu.make_async_copy(src, dst, self.sem.at[self.count])
        copy.start()
        self.count += 1
        return copy


def wait_all(copies):
    for copy in copies:
        copy.wait()


def eighths(scal):
    core, one, two = scal[0], scal[1], scal[2]
    order = []
    for c, a, b in ((core, one, two), (1 - core, two, one)):
        order += [4 * c + 2 * (a ^ (k & 1)) + (b ^ (k >> 1)) for k in range(4)]
    return order


def place(at, rows):
    return pl.ds(pl.multiple_of(at * rows, rows), rows)


class Stages:
    def __init__(self, go, groups, depth):
        self.go, self.groups, self.depth, self.next = go, groups, depth, 0
        self.running = []
        for _ in range(depth):
            self.begin()

    def begin(self):
        if len(self.running) < len(self.groups):
            self.running.append([self.go.start(src, dst) for src, dst in self.groups[len(self.running)]])

    def need(self):
        wait_all(self.running[self.next])
        self.next += 1
        self.begin()


def mix_copies(scal, pieces, dst):
    rows = dst.shape[0] // 2
    return [(src.at[:rows, :], dst.at[place(at, rows), :]) for src, at in zip(pieces, (scal[0], 1 - scal[0]))]


def own_copies(up, down, ups, downs):
    size = ups.shape[2]
    cols = [slice(k * size, (k + 1) * size) for k in range(ups.shape[0])]
    return [([(up.at[:, c], ups.at[k])], [(down.at[c, :], downs.at[c, :])]) for k, c in enumerate(cols)]


def got_copies(scal, pieces, ups, downs):
    order = eighths(scal)
    rows = ups.shape[1] // 8
    copies = []
    for k in range(ups.shape[0]):
        part = slice(k * rows, (k + 1) * rows)
        copies.append(([(src.at[part, :], ups.at[k, place(at, rows), :]) for src, at in zip(pieces, order)], []))
    first, rows = 2 * rows, downs.shape[0] // 8
    for src, at in zip(pieces, order):
        copies[0][1].append((src.at[first : first + rows, :], downs.at[place(at, rows), :]))
    return copies


def row_loop(first, count, step, body, carry=0):
    for at in range(first, first + count, step):
        carry = body(slice(at, at + step), carry)
    return carry


def fold(v):
    return jnp.sum(v.reshape(-1, 8, v.shape[-1]), axis=0)


ROWS = 128


def feed_chunks(tile, low, bias, ups, downs, need, branch, act, slope, done):
    tiles = low.shape[0] // tile
    size = ups.shape[2]
    span = [slice(r * tile, (r + 1) * tile) for r in range(tiles)]
    order = [(j, r) for j in range(ups.shape[0]) for r in range(tiles)]

    def pre(j, r):
        if r == 0:
            need()
        return nn(low[span[r], :], ups[j]) + bias(j)

    ahead = pre(*order[0])
    for t, (j, r) in enumerate(order):
        value, ahead = ahead, (pre(*order[t + 1]) if t + 1 < len(order) else None)
        active, incline = gelu_pair(value)
        active = active.astype(LOW)
        if act is not None:
            act[j, span[r], :] = active
        slope[j, span[r], :] = incline.astype(LOW)
        if r == 0:
            need()
        branch[span[r], :] += nn(active, downs[j * size : (j + 1) * size, :])
        if r == tiles - 1:
            done(j)


def first_kernel(
    tile, scal, mix_bias, gain_ref, shift_ref, down_bias, bias_ref, own_in, got_in, x_in, mix_in, m_0, m_1, up_in, down_in,
    resid_out, low_out, branch_out, act_out, slope_out,
    ctx_own, ctx_got, x_ref, mix_own, mix_got, ups, downs, resid, low, branch, act, slope, sem,
):
    go = Copies(sem)
    groups = [[(own_in, ctx_own), (mix_in, mix_own)], [(got_in, ctx_got)] + mix_copies(scal, (m_0, m_1), mix_got), [(x_in, x_ref)]]
    for up, down in own_copies(up_in, down_in, ups, downs):
        groups += [up, down]
    stages = Stages(go, groups, 3)
    gain, shift, offset, more = (r[...].astype(F32) for r in (gain_ref, shift_ref, mix_bias, down_bias))
    pending = []
    for r in range(x_ref.shape[0] // tile):
        rows = slice(r * tile, (r + 1) * tile)
        if r == 0:
            stages.need()
        attended = nn(ctx_own[rows, :], mix_own[...])
        if r == 0:
            stages.need()
        attended += nn(ctx_got[rows, :], mix_got[...])
        if r == 0:
            stages.need()
        resid[rows, :] = attended

        def norm(at, _):
            value = resid[at, :] + x_ref[at, :].astype(F32) + offset
            resid[at, :] = value
            normed = unit_norm(value)[0] * gain + shift
            low[at, :] = normed.astype(LOW)
            branch[at, :] = normed + more
            return 0

        row_loop(r * tile, tile, ROWS, norm)
    pending += [go.start(resid, resid_out), go.start(low, low_out)]

    def done(j):
        pending.extend([go.start(act.at[j], act_out.at[j]), go.start(slope.at[j], slope_out.at[j])])

    feed_chunks(
        tile, low, lambda j: bias_ref[j : j + 1, :].astype(F32), ups, downs, stages.need, branch, act, slope, done
    )
    pending.append(go.start(branch, branch_out))
    wait_all(pending)


def first_part(scal, ctx_own, ctx_got, x, mix_own, vecs, bias, m_got, up, down, tile=256):
    tokens, width = x.shape
    hidden = up.shape[1] // 2
    both_chunks = (2, tokens, hidden)
    return pl.pallas_call(
        partial(first_kernel, tile),
        in_specs=[SMEM] + vmem_specs(5) + any_specs(8),
        out_specs=any_specs(5),
        out_shape=[
            in_hbm((tokens, width), F32), in_hbm((tokens, width)), in_hbm((tokens, width), F32),
            in_hbm(both_chunks), in_hbm(both_chunks),
        ],
        scratch_shapes=[
            pltpu.VMEM(ctx_own.shape, LOW), pltpu.VMEM(ctx_own.shape, LOW), pltpu.VMEM((tokens, width), LOW),
            pltpu.VMEM(mix_own.shape, LOW), pltpu.VMEM(mix_own.shape, LOW),
            pltpu.VMEM((2, width, hidden), LOW), pltpu.VMEM((2 * hidden, width), LOW),
            pltpu.VMEM((tokens, width), F32), pltpu.VMEM((tokens, width), LOW), pltpu.VMEM((tokens, width), F32),
            pltpu.VMEM(both_chunks, LOW), pltpu.VMEM(both_chunks, LOW), pltpu.SemaphoreType.DMA((24,)),
        ],
        compiler_params=pltpu.CompilerParams(vmem_limit_bytes=48 * MIB),
        cost_estimate=pl.CostEstimate(
            flops=2 * tokens * width * (width + 4 * hidden), bytes_accessed=16 * MIB, transcendentals=4 * tokens * hidden
        ),
        name="first_part",
    )(scal, *vecs, bias, *hbm(ctx_own, ctx_got, x, mix_own, *m_got, up, down))


def second_kernel(
    tile, scal, down_gain, end_shift, m_0, low_in, branch_in, e_in, *rest,
):
    pieces = rest[:8]
    out_out, g_second_out, g_branch_out, slope_out, sum_ref = rest[8:13]
    ups, downs, low, branch, e_ref, slope, out, g_second, g_branch, sem = rest[13:]
    go = Copies(sem)
    (up_0, down), (up_1, _) = got_copies(scal, pieces, ups, downs)
    stages = Stages(go, [[(low_in, low)] + up_0, down + [(branch_in, branch)], up_1, [], [(e_in, e_ref)]], 2)
    pending = []
    bias_at = m_0.shape[0] - 16

    def done(j):
        pending.append(go.start(slope.at[j], slope_out.at[j]))

    feed_chunks(
        tile, low, lambda j: m_0[bias_at + j : bias_at + j + 1, :].astype(F32), ups, downs, stages.need, branch, None, slope, done
    )
    stages.need()
    gain, shift = down_gain[...].astype(F32), end_shift[...].astype(F32)
    width = branch.shape[1]
    sums = tuple(jnp.zeros((8, width), F32) for _ in range(3))

    def norm(at, sums):
        unit, scaled = unit_norm(branch[at, :])
        out[at, :] = (unit * gain + shift).astype(LOW)
        e = e_ref[at, :].astype(F32)
        grad = norm_back(e, unit, scaled, gain)
        g_second[at, :] = grad
        g_branch[at, :] = grad.astype(LOW)
        return tuple(a + fold(b) for a, b in zip(sums, (grad, e * unit, e)))

    half = branch.shape[0] // 2
    for r in range(2):
        sums = row_loop(r * half, half, ROWS, norm, sums)
        at = pl.ds(r * half, half)
        for src, dst in ((g_branch, g_branch_out), (g_second, g_second_out), (out, out_out)):
            pending.append(go.start(src.at[at, :], dst.at[at, :]))
    sum_ref[...] = jnp.concatenate([rows_sum(v) for v in sums] + [jnp.zeros((5, width), F32)], axis=0)
    wait_all(pending)


def second_part(scal, low, end_gain, end_shift, m_0, branch, e, pieces, tile=256):
    tokens, width = low.shape
    hidden = width
    sds = jax.ShapeDtypeStruct
    return pl.pallas_call(
        partial(second_kernel, tile),
        in_specs=[SMEM] + vmem_specs(3) + any_specs(11),
        out_specs=any_specs(4) + vmem_specs(1),
        out_shape=[
            in_hbm((tokens, width)), in_hbm((tokens, width), F32), in_hbm((tokens, width)),
            in_hbm((2, tokens, hidden)), sds((8, width), F32),
        ],
        scratch_shapes=[
            pltpu.VMEM((2, width, hidden), LOW), pltpu.VMEM((2 * hidden, width), LOW), pltpu.VMEM((tokens, width), LOW),
            pltpu.VMEM((tokens, width), F32),
            pltpu.VMEM((tokens, width), LOW), pltpu.VMEM((2, tokens, hidden), LOW), pltpu.VMEM((tokens, width), LOW),
            pltpu.VMEM((tokens, width), F32), pltpu.VMEM((tokens, width), LOW), pltpu.SemaphoreType.DMA((40,)),
        ],
        compiler_params=pltpu.CompilerParams(vmem_limit_bytes=48 * MIB),
        cost_estimate=pl.CostEstimate(
            flops=8 * tokens * width * hidden, bytes_accessed=14 * MIB, transcendentals=4 * tokens * hidden
        ),
        name="second_part",
    )(scal, end_gain, end_shift, *hbm(m_0, low, branch, e, *pieces))


def back_kernel(
    tile, scal, gain_ref, g_branch_in, mix_in, g_second_in, resid_in, slope_a, slope_b, m_0, m_1, up_in, down_in, *rest
):
    pieces = rest[:8]
    g_first_out, g_att_out, ctx_a_out, ctx_b_out, g_pre_out, sum_ref = rest[8:14]
    ups, downs, g_branch, mix_own, mix_got, slope, grad, resid, g_pre, g_att, g_ctx, sem = rest[14:]
    half = ups.shape[0] // 2
    size = ups.shape[2]
    go = Copies(sem)
    copies = own_copies(up_in, down_in, ups.at[:half], downs.at[: half * size])
    copies += got_copies(scal, pieces, ups.at[half:], downs.at[half * size :])
    slopes = [(s.at[j], slope.at[k * half + j]) for k, s in enumerate((slope_a, slope_b)) for j in range(half)]
    groups = []
    for k, (up, down) in enumerate(copies):
        groups += [down + [slopes[k]], up]
    groups[0] = [(g_branch_in, g_branch)] + groups[0]
    groups[1] = groups[1] + [(g_second_in, grad)]
    groups += [[(resid_in, resid), (mix_in, mix_own)] + mix_copies(scal, (m_0, m_1), mix_got)]
    stages = Stages(go, groups, 3)
    tokens = grad.shape[0]
    tiles = tokens // tile
    span = [slice(r * tile, (r + 1) * tile) for r in range(tiles)]
    order = [(j, r) for j in range(2 * half) for r in range(tiles)]
    pending = []

    def g_active(j, r):
        if r == 0:
            stages.need()
        return nt(g_branch[span[r], :], downs[j * size : (j + 1) * size, :])

    ahead = g_active(*order[0])
    for t, (j, r) in enumerate(order):
        value, ahead = ahead, (g_active(*order[t + 1]) if t + 1 < len(order) else None)
        if r == 0:
            stages.need()
        low = (value * slope[j, span[r], :].astype(F32)).astype(LOW)
        if j < half:
            g_pre[j, span[r], :] = low
            if r == tiles - 1:
                pending.append(go.start(g_pre.at[j], g_pre_out.at[j]))
        grad[span[r], :] += nt(low, ups[j])
    stages.need()
    gain = gain_ref[...].astype(F32)
    width = grad.shape[1]
    sums = tuple(jnp.zeros((8, width), F32) for _ in range(3))

    def norm(at, sums):
        unit, scaled = unit_norm(resid[at, :])
        e = grad[at, :]
        first = norm_back(e, unit, scaled, gain)
        grad[at, :] = first
        g_att[at, :] = first.astype(LOW)
        return tuple(a + fold(b) for a, b in zip(sums, (first, e * unit, e)))

    for r in range(tiles):
        sums = row_loop(r * tile, tile, ROWS, norm, sums)
        g_ctx[1, span[r], :] = nt(g_att[span[r], :], mix_got[...]).astype(LOW)
        g_ctx[0, span[r], :] = nt(g_att[span[r], :], mix_own[...]).astype(LOW)
        at = pl.ds(r * tile, tile)
        for src, dst in ((g_ctx.at[1], ctx_b_out), (g_ctx.at[0], ctx_a_out), (g_att, g_att_out), (grad, g_first_out)):
            pending.append(go.start(src.at[at, :], dst.at[at, :]))
    sum_ref[...] = jnp.concatenate([rows_sum(v) for v in sums] + [jnp.zeros((5, width), F32)], axis=0)
    wait_all(pending)


def back_part(scal, g_branch, gain, mix_own, g_second, resid, slopes, m_got, up, down, pieces, tile=256):
    tokens, width = g_branch.shape
    part = mix_own.shape[0]
    hidden = up.shape[1] // 2
    sds = jax.ShapeDtypeStruct
    return pl.pallas_call(
        partial(back_kernel, tile),
        in_specs=[SMEM] + vmem_specs(1) + any_specs(18),
        out_specs=any_specs(5) + vmem_specs(1),
        out_shape=[
            in_hbm((tokens, width), F32), in_hbm((tokens, width)), in_hbm((tokens, part)), in_hbm((tokens, part)),
            in_hbm((2, tokens, hidden)), sds((8, width), F32),
        ],
        scratch_shapes=[
            pltpu.VMEM((4, width, hidden), LOW), pltpu.VMEM((4 * hidden, width), LOW), pltpu.VMEM((tokens, width), LOW),
            pltpu.VMEM((part, width), LOW), pltpu.VMEM((part, width), LOW),
            pltpu.VMEM((4, tokens, hidden), LOW), pltpu.VMEM((tokens, width), F32), pltpu.VMEM((tokens, width), F32),
            pltpu.VMEM((2, tokens, hidden), LOW), pltpu.VMEM((tokens, width), LOW), pltpu.VMEM((2, tokens, part), LOW),
            pltpu.SemaphoreType.DMA((60,)),
        ],
        compiler_params=pltpu.CompilerParams(vmem_limit_bytes=50 * MIB),
        cost_estimate=pl.CostEstimate(flops=16 * tokens * width * hidden, bytes_accessed=24 * MIB, transcendentals=0),
        name="back_part",
    )(scal, gain, *hbm(g_branch, mix_own, g_second, resid, *slopes, *m_got, up, down, *pieces))


def weight_kernel(
    pick, bias_ref, act_in, g_pre_in, low_in, low_got_in, g_branch_in, g_branch_got_in, up_in, down_in, out, bias_out,
    act, g_pre, low, low_got, g_branch, g_branch_got, up, down, grads, sem,
):
    go = Copies(sem)
    width, hidden = up.shape
    at = pl.multiple_of(pick[0] * hidden, hidden)
    groups = [
        [(low_in, low), (g_pre_in.at[pick[0]], g_pre)],
        [(low_got_in, low_got), (up_in.at[:, pl.ds(at, hidden)], up)],
        [(g_branch_got_in, g_branch_got), (down_in.at[pl.ds(at, hidden), :], down)],
        [(act_in.at[pick[0]], act), (g_branch_in, g_branch)],
    ]
    stages = Stages(go, groups, 2)
    bias = bias_ref[...].astype(F32)
    stages.need()
    up_own = tn(low[...], g_pre[...])
    stages.need()
    pre = nn(low_got[...], up[...]) + jnp.where(pick[0] == 0, bias[0:1], bias[1:2])
    stages.need()
    g_active = nt(g_branch_got[...], down[...])
    active, incline = gelu_pair(pre)
    g_pre_got = g_active * incline
    bias_out[...] = rows_sum(g_pre_got) + rows_sum(g_pre[...].astype(F32))
    grads[:width, :] = (up_own + tn(low_got[...], g_pre_got.astype(LOW))).astype(LOW)
    first = go.start(grads.at[:width, :], out.at[:width, :])
    stages.need()
    grads[width:, :] = (tn(act[...], g_branch[...]) + tn(active.astype(LOW), g_branch_got[...])).astype(LOW)
    wait_all([go.start(grads.at[width:, :], out.at[width:, :]), first])


def weight_part(pick, act, g_pre, low, low_got, g_branch, g_branch_got, up, down, bias):
    _, tokens, hidden = act.shape
    width = low.shape[1]
    assert hidden == width
    token, square = pltpu.VMEM((tokens, width), LOW), pltpu.VMEM((width, hidden), LOW)
    return pl.pallas_call(
        weight_kernel,
        in_specs=[SMEM] + vmem_specs(1) + any_specs(8),
        out_specs=any_specs(1) + vmem_specs(1),
        out_shape=[in_hbm((width + hidden, width)), jax.ShapeDtypeStruct((1, hidden), F32)],
        scratch_shapes=[token] * 6 + [square] * 2 + [pltpu.VMEM((width + hidden, width), LOW), pltpu.SemaphoreType.DMA((10,))],
        compiler_params=pltpu.CompilerParams(vmem_limit_bytes=50 * MIB),
        cost_estimate=pl.CostEstimate(
            flops=12 * tokens * width * hidden, bytes_accessed=10 * MIB, transcendentals=2 * tokens * hidden
        ),
        name="weight_part",
    )(pick, bias, *hbm(act, g_pre, low, low_got, g_branch, g_branch_got, up, down))


def mix_grad_kernel(ctx_own, ctx_got, g_att, mid_sums, end_sums, own_out, got_out):
    own_out[...] = tn(ctx_own[...], g_att[...]).astype(LOW)
    part, width = own_out.shape
    got_out[:part, :] = tn(ctx_got[...], g_att[...]).astype(LOW)
    small = jnp.concatenate([mid_sums[:3, :], end_sums[:3, :], jnp.zeros((10, width), F32)], axis=0)
    got_out[part:, :] = small.astype(LOW)


def mix_grad(ctx_own, ctx_got, g_att, mid_sums, end_sums):
    tokens, width = g_att.shape
    part = ctx_own.shape[1]
    return pl.pallas_call(
        mix_grad_kernel,
        in_specs=vmem_specs(5),
        out_specs=vmem_specs(2),
        out_shape=[in_hbm((part, width)), in_hbm((part + 16, width))],
        compiler_params=pltpu.CompilerParams(vmem_limit_bytes=24 * MIB),
        cost_estimate=pl.CostEstimate(flops=4 * tokens * width * part, bytes_accessed=4 * MIB, transcendentals=0),
        name="mix_grad",
    )(*hbm(ctx_own, ctx_got, g_att), mid_sums, end_sums)


def late_kernel(
    scal, own_ref, got_ref, g_ref, mix_own, mix_other, mid_sums, end_sums, bias_keep, bias_send,
    keep_mine, keep_away, send_mine, send_away, out,
):
    half, width = own_ref.shape
    cols = g_ref.shape[1]
    out[:, :cols] = (tn(own_ref[...], g_ref[:half, :]) + tn(got_ref[...], g_ref[half:, :])).astype(LOW)
    part = mix_own.shape[0]
    for k in range(2):
        side = slice(k * part, (k + 1) * part)
        total = mix_own[:, side].astype(F32) + mix_other[:part, side].astype(F32)
        out[side, cols : cols + part] = total.astype(LOW)
    sums = nn(jnp.ones((8, 2 * half), LOW), g_ref[...])[:1]
    sums = jnp.concatenate([sums[:, :part], sums[:, 2 * part :]], axis=1)
    small = jnp.concatenate([mid_sums[:3, :], end_sums[:3, :]], axis=0) + mix_other[part : part + 6, :].astype(F32)
    first = scal[0] == 0
    ups = [jnp.where(first, bias_keep[...], bias_send[...]), jnp.where(first, bias_send[...], bias_keep[...])]
    rows = jnp.concatenate([small, *ups, sums, jnp.zeros((PAIR - 9, width), F32)], axis=0)
    out[:, cols + part :] = jnp.transpose(rows).astype(LOW)
    rows = part // 2
    for core, side, mine, away in ((scal[0], scal[1], keep_mine, keep_away), (1 - scal[0], scal[2], send_mine, send_away)):
        mine[...] = out[place(2 * core + side, rows), :]
        away[...] = out[place(2 * core + 1 - side, rows), :]


def late_grads(scal, own, got, g, mix_own, mix_other, sums):
    tokens, width = own.shape
    part = mix_own.shape[0]
    assert 2 * part == width
    cols = g.shape[1] + part + PAIR
    return pl.pallas_call(
        late_kernel,
        in_specs=[SMEM] + vmem_specs(9),
        out_specs=vmem_specs(4),
        out_shape=[in_hbm((part // 2, cols))] * 4,
        scratch_shapes=[pltpu.VMEM((width, cols), LOW)],
        compiler_params=pltpu.CompilerParams(vmem_limit_bytes=40 * MIB),
        cost_estimate=pl.CostEstimate(flops=4 * tokens * width * g.shape[1], bytes_accessed=8 * MIB, transcendentals=0),
        name="late_grads",
    )(scal, *hbm(own, got, g, mix_own, mix_other), *sums)


def finish_feed_kernel(scal, *refs):
    up_out, down_out = refs[4:]
    width = down_out.shape[2]
    for k in range(2):
        core, side = scal[0] ^ k, scal[1 + k]
        for n in range(2):
            piece = refs[2 * k + n][...].astype(F32)

            @pl.when(side == n)
            def _():
                up_out[:, pl.ds(pl.multiple_of(core * width, width), width)] = piece

            @pl.when(side != n)
            def _():
                down_out[core] = piece


def finish_feed(scal, pieces, steps=4):
    width = pieces[0].shape[1]
    rows = width // steps
    block = pl.BlockSpec((rows, width), lambda i, scal: (i, 0))
    up, down = pl.pallas_call(
        finish_feed_kernel,
        grid_spec=pltpu.PrefetchScalarGridSpec(
            num_scalar_prefetch=1,
            grid=(steps,),
            in_specs=[block] * 4,
            out_specs=[
                pl.BlockSpec((rows, 2 * width), lambda i, scal: (i, 0)),
                pl.BlockSpec((2, rows, width), lambda i, scal: (0, i, 0)),
            ],
        ),
        out_shape=[in_hbm((width, 2 * width), F32), in_hbm((2, width, width), F32)],
        compiler_params=pltpu.CompilerParams(vmem_limit_bytes=32 * MIB),
        cost_estimate=pl.CostEstimate(flops=0, bytes_accessed=14 * MIB, transcendentals=0),
        name="finish_feed",
    )(scal, *pieces)
    return up, down.reshape(2 * width, width)


def finish_late_kernel(scal, *refs):
    q_out, k_out, v_out, mix_out, *lines, small_out = refs[4:]
    part = q_out.shape[1]
    half = part // 2
    for k in range(2):
        core = scal[0] ^ k
        for n in range(2):
            side = scal[1 + k] ^ n
            piece = refs[2 * k + n]
            rows = pl.ds(pl.multiple_of(core * part + side * half, half), half)
            for m, out in enumerate((q_out, k_out, v_out)):
                out[rows, :] = piece[:, m * part : (m + 1) * part].astype(F32)
            some = pl.ds(pl.multiple_of(side * half, half), half)
            mix_out[some, pl.ds(pl.multiple_of(core * part, part), part)] = piece[:, 3 * part : 4 * part].astype(F32)
            small = jnp.transpose(piece[:, 4 * part :].astype(F32))[:16]
            for at in range(4):

                @pl.when(2 * core + side == at)
                def _():
                    small_out[:, at * half : (at + 1) * half] = small
    *norms, ups, q_bias, v_bias = lines
    for r, out in enumerate(norms):
        out[...] = small_out[r, :]
    width = 2 * part
    for k in range(2):
        ups[k * width : (k + 1) * width] = small_out[6 + k, :]
    q_bias[...] = small_out[8, :part]
    v_bias[...] = small_out[8, part:]


def finish_late(scal, pieces):
    part = 2 * pieces[0].shape[0]
    sds = jax.ShapeDtypeStruct
    return pl.pallas_call(
        finish_late_kernel,
        in_specs=[SMEM] + vmem_specs(4),
        out_specs=vmem_specs(13),
        out_shape=[in_hbm((2 * part, part), F32)] * 3
        + [in_hbm((part, 2 * part), F32)]
        + [sds((n,), F32) for n in [2 * part] * 6 + [4 * part, part, part]],
        scratch_shapes=[pltpu.VMEM((16, 2 * part), F32)],
        compiler_params=pltpu.CompilerParams(vmem_limit_bytes=32 * MIB),
        cost_estimate=pl.CostEstimate(flops=0, bytes_accessed=8 * MIB, transcendentals=0),
        name="finish_late",
    )(scal, *pieces)


def swap(value, axis, bit):
    even, odd = bit if isinstance(bit, tuple) else (bit, bit)
    return lax.ppermute(value, axis, [(i, i ^ (odd if i & 1 else even)) for i in range(lax.axis_size(axis))])


def wide(value):
    return value.astype(F32)


def cut(value, at, size):
    return lax.dynamic_slice_in_dim(value, at, size, 0)


def side_of(dp, mask):
    if isinstance(mask, tuple):
        mask = jnp.where(dp & 1, mask[1], mask[0])
    return ((dp & mask) != 0).astype(jnp.int32)


def dp_masks():
    return [1 << i for i in range(lax.axis_size("dp").bit_length() - 1)]


def total(terms):
    return sum(wide(t) for t in terms).astype(LOW)


class Chain:
    def __init__(self, dp, masks, terms, away=None):
        self.dp, self.masks, self.terms, self.away = dp, masks, terms, away
        self.step, self.value, self.sent, self.got = 0, None, None, None

    def start(self, *others):
        last = len(self.masks) - 1
        if self.step == 0 and self.away:
            mask = self.masks[0]
            self.sent = total(self.away)
        elif self.step < last:
            mask = self.masks[self.step]
            half, mine = self.terms[0].shape[0] // 2, side_of(self.dp, mask)
            self.sent = total([cut(t, (1 - mine) * half, half) for t in self.terms])
            self.terms = [cut(t, mine * half, half) for t in self.terms]
        elif self.step == last:
            mask = self.masks[last]
            self.sent = self.value = total(self.terms)
        else:
            mask = self.masks[2 * last - self.step]
            self.sent = self.value
        if others:
            self.sent = after(self.sent, *others)
        self.got = swap(self.sent, "dp", mask)

    def finish(self, *others):
        got = after(self.got, *others) if others else self.got
        last = len(self.masks) - 1
        if self.step < last:
            self.terms = self.terms + [got]
        elif self.step == last:
            self.value = (wide(self.value) + wide(got)).astype(LOW)
        elif self.step < 2 * last:
            side = side_of(self.dp, self.masks[2 * last - self.step])
            self.value = jnp.where(side == 1, jnp.concatenate([got, self.value]), jnp.concatenate([self.value, got]))
        self.step += 1
        self.got = got

    @property
    def done(self):
        return self.step == 2 * len(self.masks) - 1


def per_device(
    inputs, upstream, lengths, query_weight, key_weight, value_weight, query_bias, value_bias, mix_weight, mix_bias,
    mid_gain, mid_shift, up_weight, up_bias, down_weight, down_bias, end_gain, end_shift,
):
    dp = lax.axis_index("dp").astype(jnp.int32)
    side = lax.axis_index("tensor").astype(jnp.int32).reshape(1)
    masks = dp_masks()
    core = dp & 1
    order = [(masks[1], masks[2]), (masks[2], masks[1])] + masks[3:]
    scal = jnp.stack([core] + [side_of(dp, mask) for mask in order[:-1]])
    tokens, width = inputs.shape
    part = query_weight.shape[1]
    own_hidden = up_weight.shape[1]
    hidden = own_hidden // 2
    row = lambda v: v.reshape(1, -1)
    across = lambda v: swap(v, "tensor", 1)

    x_got = across(inputs)
    pairs = tuple(range(part // PAIR))
    qkv_weight = jnp.concatenate([query_weight, key_weight, value_weight], axis=1)
    qkv_bias = jnp.concatenate([wide(query_bias), jnp.zeros((part,), F32), wide(value_bias)])
    bias_own = up_bias.reshape(2, hidden)
    m_piece = jnp.concatenate([cut(mix_weight, core * (part // 2), part // 2), bias_own, jnp.zeros((14, width), LOW)])
    eighth = 4 * core + 2 * side_of(dp, order[0]) + side_of(dp, order[1])
    up_piece = cut(up_weight, eighth * (width // 8), width // 8)
    down_piece = cut(down_weight, eighth * (own_hidden // 8), own_hidden // 8)
    piece = jnp.concatenate([up_piece[:, :hidden], up_piece[:, hidden:], down_piece])

    def project(v):
        return (nn(v, qkv_weight) + qkv_bias).astype(LOW)

    own = project(inputs)
    x_got = after(x_got, own, m_piece, piece)
    piece_0 = across(after(piece, x_got))
    got = project(x_got)
    ctx_own, ctx_send, lse = attend(lengths, side, own, got, pairs)
    ctx_send, piece_0 = lax.optimization_barrier((ctx_send, piece_0))
    ctx_got = across(ctx_send)
    m_0 = across(after(m_piece, ctx_send))
    m_got = [m_0, swap(m_0, "dp", 1)]
    piece_1 = swap(piece_0, "dp", order[0])
    piece_2, piece_3 = swap(piece_0, "dp", order[1]), swap(piece_1, "dp", order[1])
    resid, low, branch, act, slope_own = first_part(
        scal, ctx_own, ctx_got, inputs, mix_weight, [row(v) for v in (mix_bias, mid_gain, mid_shift, down_bias)], bias_own,
        m_got, up_weight, down_weight,
    )
    low_got = across(low)
    pieces = [piece_0, piece_1, after(piece_2, low), after(piece_3, low)]
    pieces += [swap(v, "dp", 1) for v in pieces]
    outputs, g_second, g_branch, slope_got, end_sums = second_part(
        scal, low, row(end_gain), row(end_shift), m_0, branch, upstream, pieces
    )
    g_branch_got = across(g_branch)
    g_first, g_att, g_ctx_own, g_ctx_send, g_pre, mid_sums = back_part(
        scal, g_branch, row(mid_gain), mix_weight, g_second, resid, (slope_own, slope_got),
        m_got, up_weight, down_weight, pieces,
    )
    g_ctx_got = across(g_ctx_send)
    mix_own, mix_send = mix_grad(ctx_own, ctx_got, after(g_att, low_got), mid_sums, end_sums)
    shared = (low, low_got, g_branch, g_branch_got, up_weight, down_weight, bias_own)
    send, bias_send = weight_part((1 - core).reshape(1), act, after(g_pre, mix_own), *shared)
    mix_other = across(after(mix_send, g_ctx_got))
    send = after(send, g_ctx_got)
    keep, bias_keep = weight_part(after(core.reshape(1), send), act, g_pre, *shared)
    feed = Chain(dp, order, [keep, swap(send, "dp", 1)])
    feed.start()
    g_qkv = attend_back(
        lengths, side, own, got, g_ctx_own, after(g_ctx_got, feed.sent), ctx_own, ctx_send, lse, pairs,
    )
    feed.finish(g_qkv)
    mix_other = after(mix_other, g_qkv)
    g_qkv = after(g_qkv, mix_other, feed.got)
    feed.start()
    keep_mine, keep_away, send_mine, send_away = late_grads(
        scal, inputs, x_got, g_qkv, mix_own, mix_other, (mid_sums, end_sums, bias_keep, bias_send)
    )
    feed.finish(keep_mine)
    away_got, mine_got = swap(after(send_away, feed.got), "dp", 1), swap(after(send_mine, feed.got), "dp", 1)
    proj = Chain(dp, order, [keep_mine, mine_got], [keep_away, away_got])
    proj.start()
    feed.start(proj.sent)
    input_got = across(nt(after(g_qkv, feed.sent)[tokens:], qkv_weight).astype(LOW))
    proj.finish(feed.sent)
    proj.start()
    proj.finish()
    feed.finish(proj.got)
    input_got = after(input_got, proj.got)
    proj.start(feed.got, input_got)
    input_own = g_first + nt(after(g_qkv, proj.sent)[:tokens], qkv_weight)
    input_grad = (input_own + wide(input_got)).astype(LOW)
    feed.start()
    proj.finish(feed.sent, input_grad)
    while not feed.done:
        proj.start()
        feed.finish(proj.sent)
        if not feed.done:
            feed.start()
            proj.finish(feed.sent)
    feed_pieces = [feed.value, feed.got]
    feed_pieces += [swap(v, "dp", 1) for v in feed_pieces]
    up_grad, down_grad = finish_feed(scal, feed_pieces)
    proj.finish(up_grad)
    assert proj.done
    late_pieces = [proj.value, proj.got]
    late_pieces += [swap(v, "dp", 1) for v in late_pieces]
    q_grad, k_grad, v_grad, mix_grads, *norms, up_bias_grad, q_bias_grad, v_bias_grad = finish_late(scal, late_pieces)
    return (
        outputs,
        input_grad,
        q_grad,
        k_grad,
        v_grad,
        q_bias_grad,
        v_bias_grad,
        mix_grads,
        *norms[:3],
        up_grad,
        up_bias_grad,
        down_grad,
        *norms[3:],
    )


def solution(mesh):
    placed = (
        P(("dp", "tensor"), None),
        P(("dp", "tensor"), None),
        P("dp", None),
        P(None, "tensor"),
        P(None, "tensor"),
        P(None, "tensor"),
        P("tensor"),
        P("tensor"),
        P("tensor", None),
        P(),
        P(),
        P(),
        P(None, "tensor"),
        P("tensor"),
        P("tensor", None),
        P(),
        P(),
        P(),
    )
    return jax.shard_map(
        per_device,
        mesh=mesh,
        in_specs=placed,
        out_specs=(
            P(("dp", "tensor"), None),
            P(("dp", "tensor"), None),
            P(None, "tensor"),
            P(None, "tensor"),
            P(None, "tensor"),
            P("tensor"),
            P("tensor"),
            P("tensor", None),
            P(),
            P(),
            P(),
            P(None, "tensor"),
            P("tensor"),
            P("tensor", None),
            P(),
            P(),
            P(),
        ),
        check_vma=False,
    )
```

```python
from functools import partial

import jax
import jax.numpy as jnp
from jax import lax
from jax.experimental import pallas as pl
from jax.experimental.pallas import tpu as pltpu
from jax.sharding import PartitionSpec as P

HEAD_DIM = 64
PAIR = 128
SEQ = 1024
LOW = jnp.bfloat16
F32 = jnp.float32
FAR = -1e30


def nt(a, b):
    return lax.dot_general(a, b, (((1,), (1,)), ((), ())), preferred_element_type=F32)


def tn(a, b):
    return lax.dot_general(a, b, (((0,), (0,)), ((), ())), preferred_element_type=F32)


def nn(a, b):
    return lax.dot_general(a, b, (((1,), (0,)), ((), ())), preferred_element_type=F32)


def seg_ends(len_ref):
    ends, total = [], jnp.int32(0)
    for j in range(len_ref.shape[1]):
        total = total + len_ref[0, j]
        ends.append(total)
    return ends


def seg_marks(ends, shift):
    pos = (lax.broadcasted_iota(jnp.int32, (SEQ, PAIR), 0) + shift) & (SEQ - 1)
    lane = lax.broadcasted_iota(jnp.int32, (SEQ, PAIR), 1) & (HEAD_DIM - 1)
    seg = jnp.zeros((SEQ, PAIR), jnp.int32)
    for e in ends:
        seg = seg + (pos >= e).astype(jnp.int32)
    own = seg == lane
    used = lane < len(ends)
    key_mark = jnp.where(own, 1.0, 0.0)
    query_mark = jnp.where(used & jnp.logical_not(own), FAR, 0.0)
    return key_mark, query_mark


def key_range(ends, first, size, step):
    begin, stop = jnp.int32(0), jnp.int32(SEQ)
    for e in ends:
        begin = jnp.where(e <= first, e, begin)
    for e in reversed(ends):
        stop = jnp.where(e >= first + size, e, stop)
    return (begin // step) * step, stop


def head_mask(h):
    lane = lax.broadcasted_iota(jnp.int32, (1, PAIR), 1)
    return (lane >= h * HEAD_DIM) & (lane < (h + 1) * HEAD_DIM)


def over_queries(ends, shift, bq, bk, step, body):
    most = -(-SEQ // bk)

    def one(t, _):
        q_at = pl.multiple_of(t * bq, bq)
        q_pos = (q_at + shift) & (SEQ - 1)
        begin, stop = key_range(ends, q_pos, bq, step)
        count = (stop - begin + bk - 1) // bk
        begin = jnp.minimum(begin, SEQ - count * bk)
        begin = pl.multiple_of(begin, step)
        for n in range(1, most + 1):

            @pl.when(count == n)
            def _():
                body(q_at, begin, n)

        return 0

    lax.fori_loop(0, SEQ // bq, one, 0)


def true_order(dst, src, shift):
    half = SEQ // 2
    dst[pl.ds(pl.multiple_of(shift, half), half), :] = src[:half]
    dst[pl.ds(pl.multiple_of(half - shift, half), half), :] = src[half:]


def both(own_ref, got_ref, at, pair):
    cols = slice(at + pair * PAIR, at + (pair + 1) * PAIR)
    return jnp.concatenate([own_ref[:, cols], got_ref[:, cols]], axis=0)


def attend_kernel(bq, bk, step, ahead, pairs, len_ref, side_ref, own_ref, got_ref, ctx_own, ctx_send, lse_ref, qh, kh, vt, acc, tot):
    shift = side_ref[0] * (SEQ // 2)
    half = SEQ // 2
    ends = seg_ends(len_ref)
    key_mark, query_mark = seg_marks(ends, shift)
    width = own_ref.shape[1] // 3
    heads = 2 * len(pairs)
    for p, pair in enumerate(pairs):
        cols = slice(p * PAIR, (p + 1) * PAIR)
        q = both(own_ref, got_ref, 0, pair).astype(F32) * 0.125
        k = both(own_ref, got_ref, width, pair).astype(F32)
        for h in range(2):
            qh[2 * p + h] = jnp.where(head_mask(h), q, query_mark).astype(LOW)
            true_order(kh.at[2 * p + h], jnp.where(head_mask(h), k, key_mark).astype(LOW), shift)
        vals = jnp.transpose(both(own_ref, got_ref, 2 * width, pair).astype(F32)).astype(LOW)
        vt[cols, pl.ds(pl.multiple_of(shift, half), half)] = vals[:, :half]
        vt[cols, pl.ds(pl.multiple_of(half - shift, half), half)] = vals[:, half:]

    def body(q_at, begin, n):
        qs = pl.ds(q_at, bq)
        at = [pl.ds(pl.multiple_of(begin + i * bk, step), bk) for i in range(n)]

        def score(h):
            query = qh[h, qs, :]
            return [nt(kh[h, at[i], :], query) for i in range(n)]

        ready = [score(h) for h in range(ahead)]
        for h in range(heads):
            dims = slice(h * HEAD_DIM, (h + 1) * HEAD_DIM)
            if h + ahead < heads:
                ready.append(score(h + ahead))
            parts = ready[h]
            top = jnp.max(parts[0], axis=0, keepdims=True)
            for s in parts[1:]:
                top = jnp.maximum(top, jnp.max(s, axis=0, keepdims=True))
            total, out = 0.0, 0.0
            for i, s in enumerate(parts):
                p = jnp.exp(s - top)
                total = total + jnp.sum(p, axis=0, keepdims=True)
                out = out + nn(vt[dims, at[i]], p.astype(LOW))
            acc[dims, qs] = out * (1.0 / total)
            tot[h : h + 1, qs] = top + jnp.log(total)

    over_queries(ends, shift, bq, bk, step, body)
    context = jnp.transpose(acc[...]).astype(LOW)
    ctx_own[...] = context[:half]
    ctx_send[...] = context[half:]
    lse_ref[...] = tot[...]


def attend(lengths, side, own, got, pairs, bq=256, bk=256, step=128, ahead=2):
    heads = 2 * len(pairs)
    width = heads * HEAD_DIM
    assert heads <= 8
    smem = pl.BlockSpec(memory_space=pltpu.SMEM)
    vmem = pl.BlockSpec(memory_space=pltpu.VMEM)
    return pl.pallas_call(
        partial(attend_kernel, bq, bk, step, ahead, pairs),
        in_specs=[smem, smem, vmem, vmem],
        out_specs=[vmem, vmem, vmem],
        out_shape=[
            jax.ShapeDtypeStruct((SEQ // 2, width), LOW),
            jax.ShapeDtypeStruct((SEQ // 2, width), LOW),
            jax.ShapeDtypeStruct((8, SEQ), F32),
        ],
        scratch_shapes=[
            pltpu.VMEM((heads, SEQ, PAIR), LOW),
            pltpu.VMEM((heads, SEQ, PAIR), LOW),
            pltpu.VMEM((width, SEQ), LOW),
            pltpu.VMEM((width, SEQ), F32),
            pltpu.VMEM((8, SEQ), F32),
        ],
        compiler_params=pltpu.CompilerParams(vmem_limit_bytes=32 * 1024 * 1024),
        name="attend",
    )(lengths, side, own, got)


def attend_back_kernel(
    bq, bk, step, ahead, pairs, len_ref, side_ref, own_ref, got_ref, do_own_ref, do_got_ref,
    ctx_own, ctx_send, lse_ref, g_ref, qh, qz, dom, kh, vals, kt, inner, dqt, dk, dv,
):
    shift = side_ref[0] * (SEQ // 2)
    half = SEQ // 2
    ends = seg_ends(len_ref)
    key_mark, query_mark = seg_marks(ends, shift)
    width = own_ref.shape[1] // 3
    heads = 2 * len(pairs)
    first = pl.ds(pl.multiple_of(shift, half), half)
    second = pl.ds(pl.multiple_of(half - shift, half), half)
    for p, pair in enumerate(pairs):
        cols = slice(p * PAIR, (p + 1) * PAIR)
        q = both(own_ref, got_ref, 0, pair).astype(F32) * 0.125
        k = both(own_ref, got_ref, width, pair).astype(F32)
        do = both(do_own_ref, do_got_ref, 0, pair).astype(F32)
        for h in range(2):
            mask = head_mask(h)
            at = 2 * p + h
            qh[at] = jnp.where(mask, q, query_mark).astype(LOW)
            qz[at] = jnp.where(mask, q, 0.0).astype(LOW)
            dom[at] = jnp.where(mask, do, 0.0).astype(LOW)
            true_order(kh.at[at], jnp.where(mask, k, key_mark).astype(LOW), shift)
        true_order(vals.at[p], both(own_ref, got_ref, 2 * width, pair), shift)
        turned = jnp.transpose(k).astype(LOW)
        kt[cols, first] = turned[:, :half]
        kt[cols, second] = turned[:, half:]
        prod = jnp.transpose(do * both(ctx_own, ctx_send, 0, p).astype(F32))
        for h in range(2):
            inner[2 * p + h : 2 * p + h + 1, :] = jnp.sum(
                prod[h * HEAD_DIM : (h + 1) * HEAD_DIM], axis=0, keepdims=True
            )
    dk[...] = jnp.zeros_like(dk)
    dv[...] = jnp.zeros_like(dv)

    def body(q_at, begin, n):
        qs = pl.ds(q_at, bq)
        at = [pl.ds(pl.multiple_of(begin + i * bk, step), bk) for i in range(n)]

        def score(h):
            query, grad = qh[h, qs, :], dom[h, qs, :]
            return [(nt(kh[h, at[i], :], query), nt(vals[h // 2, at[i], :], grad)) for i in range(n)]

        ready = [score(h) for h in range(ahead)]
        for h in range(heads):
            if h + ahead < heads:
                ready.append(score(h + ahead))
            dims = slice(h * HEAD_DIM, (h + 1) * HEAD_DIM)
            plain, grad = qz[h, qs, :], dom[h, qs, :]
            lse, mean = lse_ref[h : h + 1, qs], inner[h : h + 1, qs]
            out = 0.0
            for i, (s, gp) in enumerate(ready[h]):
                p = jnp.exp(s - lse)
                ds = (p * (gp - mean)).astype(LOW)
                dv[h // 2, at[i], :] += nn(p.astype(LOW), grad)
                dk[h // 2, at[i], :] += nn(ds, plain)
                out = out + nn(kt[dims, at[i]], ds)
            dqt[dims, qs] = out

    over_queries(ends, shift, bq, bk, step, body)
    part = heads * HEAD_DIM
    g_ref[:, :part] = (jnp.transpose(dqt[...]) * 0.125).astype(LOW)
    for p in range(heads // 2):
        for at, src in ((part + p * PAIR, dk), (2 * part + p * PAIR, dv)):
            g_ref[:half, at : at + PAIR] = src[p, first, :].astype(LOW)
            g_ref[half:, at : at + PAIR] = src[p, second, :].astype(LOW)


def attend_back(lengths, side, own, got, g_own, g_got, ctx_own, ctx_send, lse, pairs, bq=256, bk=256, step=128, ahead=1):
    heads = 2 * len(pairs)
    width = heads * HEAD_DIM
    smem = pl.BlockSpec(memory_space=pltpu.SMEM)
    vmem = pl.BlockSpec(memory_space=pltpu.VMEM)
    return pl.pallas_call(
        partial(attend_back_kernel, bq, bk, step, ahead, pairs),
        in_specs=[smem, smem] + [vmem] * 7,
        out_specs=vmem,
        out_shape=jax.ShapeDtypeStruct((SEQ, 3 * width), LOW),
        scratch_shapes=[
            pltpu.VMEM((heads, SEQ, PAIR), LOW),
            pltpu.VMEM((heads, SEQ, PAIR), LOW),
            pltpu.VMEM((heads, SEQ, PAIR), LOW),
            pltpu.VMEM((heads, SEQ, PAIR), LOW),
            pltpu.VMEM((heads // 2, SEQ, PAIR), LOW),
            pltpu.VMEM((width, SEQ), LOW),
            pltpu.VMEM((8, SEQ), F32),
            pltpu.VMEM((width, SEQ), F32),
            pltpu.VMEM((heads // 2, SEQ, PAIR), F32),
            pltpu.VMEM((heads // 2, SEQ, PAIR), F32),
        ],
        compiler_params=pltpu.CompilerParams(vmem_limit_bytes=48 * 1024 * 1024),
        name="attend_back",
    )(lengths, side, *(pltpu.with_memory_space_constraint(v, pltpu.HBM) for v in (own, got, g_own, g_got, ctx_own, ctx_send)), lse)


MIB = 1024 * 1024


def unit_norm(resid):
    middle = jnp.mean(resid, axis=-1, keepdims=True)
    centered = resid - middle
    spread = jnp.mean(centered * centered, axis=-1, keepdims=True)
    scaled = lax.rsqrt(spread + 1e-06)
    return centered * scaled, scaled


def norm_back(grad, unit, scaled, gain):
    weighted = grad * gain
    first_mean = jnp.mean(weighted, axis=-1, keepdims=True)
    second_mean = jnp.mean(weighted * unit, axis=-1, keepdims=True)
    return scaled * (weighted - first_mean - unit * second_mean)


def gelu_pair(v):
    cdf = 0.5 + 0.5 * lax.erf(v * 0.7071067811865476)
    bell = jnp.exp(-0.5 * (v * v))
    return v * cdf, cdf + (v * 0.3989422804014327) * bell


def rows_sum(v):
    return jnp.sum(v, axis=0, keepdims=True)


def after(value, *others):
    return lax.optimization_barrier((value, *others))[0]


def vmem_specs(count):
    return [pl.BlockSpec(memory_space=pltpu.VMEM)] * count


def any_specs(count):
    return [pl.BlockSpec(memory_space=pl.ANY)] * count


SMEM = pl.BlockSpec(memory_space=pltpu.SMEM)


def hbm(*arrays):
    return [pltpu.with_memory_space_constraint(v, pltpu.HBM) for v in arrays]


def in_hbm(shape, dtype=LOW):
    return pltpu.HBM(shape, dtype)


class Copies:
    def __init__(self, sem):
        self.sem, self.count = sem, 0

    def start(self, src, dst):
        copy = pltpu.make_async_copy(src, dst, self.sem.at[self.count])
        copy.start()
        self.count += 1
        return copy


def wait_all(copies):
    for copy in copies:
        copy.wait()


def eighths(scal):
    core, one, two = scal[0], scal[1], scal[2]
    order = []
    for c, a, b in ((core, one, two), (1 - core, two, one)):
        order += [4 * c + 2 * (a ^ (k & 1)) + (b ^ (k >> 1)) for k in range(4)]
    return order


def place(at, rows):
    return pl.ds(pl.multiple_of(at * rows, rows), rows)


class Stages:
    def __init__(self, go, groups, depth):
        self.go, self.groups, self.depth, self.next = go, groups, depth, 0
        self.running = []
        for _ in range(depth):
            self.begin()

    def begin(self):
        if len(self.running) < len(self.groups):
            self.running.append([self.go.start(src, dst) for src, dst in self.groups[len(self.running)]])

    def need(self):
        wait_all(self.running[self.next])
        self.next += 1
        self.begin()


def mix_copies(scal, pieces, dst):
    rows = dst.shape[0] // 4
    order = [2 * core + (side ^ k) for core, side in ((scal[0], scal[1]), (1 - scal[0], scal[2])) for k in range(2)]
    return [(src.at[:rows, :], dst.at[place(at, rows), :]) for src, at in zip(pieces, order)]


def own_copies(up, down, ups, downs):
    size = ups.shape[2]
    cols = [slice(k * size, (k + 1) * size) for k in range(ups.shape[0])]
    return [([(up.at[:, c], ups.at[k])], [(down.at[c, :], downs.at[c, :])]) for k, c in enumerate(cols)]


def got_copies(scal, pieces, ups, downs):
    order = eighths(scal)
    rows = ups.shape[1] // 8
    copies = []
    for k in range(ups.shape[0]):
        part = slice(k * rows, (k + 1) * rows)
        copies.append(([(src.at[part, :], ups.at[k, place(at, rows), :]) for src, at in zip(pieces, order)], []))
    first, rows = 2 * rows, downs.shape[0] // 8
    for src, at in zip(pieces, order):
        copies[0][1].append((src.at[first : first + rows, :], downs.at[place(at, rows), :]))
    return copies


def row_loop(first, count, step, body, carry=0):
    for at in range(first, first + count, step):
        carry = body(slice(at, at + step), carry)
    return carry


def fold(v):
    return jnp.sum(v.reshape(-1, 8, v.shape[-1]), axis=0)


ROWS = 128


def feed_chunks(tile, low, bias, ups, downs, need, branch, act, slope, done):
    tiles = low.shape[0] // tile
    size = ups.shape[2]
    span = [slice(r * tile, (r + 1) * tile) for r in range(tiles)]
    order = [(j, r) for j in range(ups.shape[0]) for r in range(tiles)]

    def pre(j, r):
        if r == 0:
            need()
        return nn(low[span[r], :], ups[j]) + bias(j)

    ahead = pre(*order[0])
    for t, (j, r) in enumerate(order):
        value, ahead = ahead, (pre(*order[t + 1]) if t + 1 < len(order) else None)
        active, incline = gelu_pair(value)
        active = active.astype(LOW)
        if act is not None:
            act[j, span[r], :] = active
        slope[j, span[r], :] = incline.astype(LOW)
        if r == 0:
            need()
        branch[span[r], :] += nn(active, downs[j * size : (j + 1) * size, :])
        if r == tiles - 1:
            done(j)


def first_kernel(
    tile, scal, mix_bias, gain_ref, shift_ref, down_bias, bias_ref, own_in, got_in, x_in, mix_in, m_0, m_1, m_2, m_3, up_in, down_in,
    resid_out, low_out, branch_out, act_out, slope_out,
    ctx_own, ctx_got, x_ref, mix_own, mix_got, ups, downs, resid, low, branch, act, slope, sem,
):
    go = Copies(sem)
    groups = [[(own_in, ctx_own), (mix_in, mix_own)], [(got_in, ctx_got)] + mix_copies(scal, (m_0, m_1, m_2, m_3), mix_got), [(x_in, x_ref)]]
    for up, down in own_copies(up_in, down_in, ups, downs):
        groups += [up, down]
    stages = Stages(go, groups, 3)
    gain, shift, offset, more = (r[...].astype(F32) for r in (gain_ref, shift_ref, mix_bias, down_bias))
    pending = []
    for r in range(x_ref.shape[0] // tile):
        rows = slice(r * tile, (r + 1) * tile)
        if r == 0:
            stages.need()
        attended = nn(ctx_own[rows, :], mix_own[...])
        if r == 0:
            stages.need()
        attended += nn(ctx_got[rows, :], mix_got[...])
        if r == 0:
            stages.need()
        resid[rows, :] = attended

        def norm(at, _):
            value = resid[at, :] + x_ref[at, :].astype(F32) + offset
            resid[at, :] = value
            normed = unit_norm(value)[0] * gain + shift
            low[at, :] = normed.astype(LOW)
            branch[at, :] = normed + more
            return 0

        row_loop(r * tile, tile, ROWS, norm)
    pending += [go.start(resid, resid_out), go.start(low, low_out)]

    def done(j):
        pending.extend([go.start(act.at[j], act_out.at[j]), go.start(slope.at[j], slope_out.at[j])])

    feed_chunks(
        tile, low, lambda j: bias_ref[j : j + 1, :].astype(F32), ups, downs, stages.need, branch, act, slope, done
    )
    pending.append(go.start(branch, branch_out))
    wait_all(pending)


def first_part(scal, ctx_own, ctx_got, x, mix_own, vecs, bias, m_got, up, down, tile=128):
    tokens, width = x.shape
    hidden = up.shape[1] // 2
    both_chunks = (2, tokens, hidden)
    return pl.pallas_call(
        partial(first_kernel, tile),
        in_specs=[SMEM] + vmem_specs(5) + any_specs(10),
        out_specs=any_specs(5),
        out_shape=[
            in_hbm((tokens, width), F32), in_hbm((tokens, width)), in_hbm((tokens, width), F32),
            in_hbm(both_chunks), in_hbm(both_chunks),
        ],
        scratch_shapes=[
            pltpu.VMEM(ctx_own.shape, LOW), pltpu.VMEM(ctx_own.shape, LOW), pltpu.VMEM((tokens, width), LOW),
            pltpu.VMEM(mix_own.shape, LOW), pltpu.VMEM(mix_own.shape, LOW),
            pltpu.VMEM((2, width, hidden), LOW), pltpu.VMEM((2 * hidden, width), LOW),
            pltpu.VMEM((tokens, width), F32), pltpu.VMEM((tokens, width), LOW), pltpu.VMEM((tokens, width), F32),
            pltpu.VMEM(both_chunks, LOW), pltpu.VMEM(both_chunks, LOW), pltpu.SemaphoreType.DMA((24,)),
        ],
        compiler_params=pltpu.CompilerParams(vmem_limit_bytes=48 * MIB),
        cost_estimate=pl.CostEstimate(
            flops=2 * tokens * width * (width + 4 * hidden), bytes_accessed=16 * MIB, transcendentals=4 * tokens * hidden
        ),
        name="first_part",
    )(scal, *vecs, bias, *hbm(ctx_own, ctx_got, x, mix_own, *m_got, up, down))


def second_kernel(
    tile, scal, down_gain, end_shift, m_0, low_in, branch_in, e_in, *rest,
):
    pieces = rest[:8]
    out_out, g_second_out, g_branch_out, slope_out, sum_ref = rest[8:13]
    ups, downs, low, branch, e_ref, slope, out, g_second, g_branch, sem = rest[13:]
    go = Copies(sem)
    (up_0, down), (up_1, _) = got_copies(scal, pieces, ups, downs)
    stages = Stages(go, [[(low_in, low)] + up_0, down + [(branch_in, branch)], up_1, [], [(e_in, e_ref)]], 2)
    pending = []
    bias_at = m_0.shape[0] - 16

    def done(j):
        pending.append(go.start(slope.at[j], slope_out.at[j]))

    feed_chunks(
        tile, low, lambda j: m_0[bias_at + j : bias_at + j + 1, :].astype(F32), ups, downs, stages.need, branch, None, slope, done
    )
    stages.need()
    gain, shift = down_gain[...].astype(F32), end_shift[...].astype(F32)
    width = branch.shape[1]
    sums = tuple(jnp.zeros((8, width), F32) for _ in range(3))

    def norm(at, sums):
        unit, scaled = unit_norm(branch[at, :])
        out[at, :] = (unit * gain + shift).astype(LOW)
        e = e_ref[at, :].astype(F32)
        grad = norm_back(e, unit, scaled, gain)
        g_second[at, :] = grad
        g_branch[at, :] = grad.astype(LOW)
        return tuple(a + fold(b) for a, b in zip(sums, (grad, e * unit, e)))

    half = branch.shape[0] // 2
    for r in range(2):
        sums = row_loop(r * half, half, ROWS, norm, sums)
        at = pl.ds(r * half, half)
        for src, dst in ((g_branch, g_branch_out), (g_second, g_second_out), (out, out_out)):
            pending.append(go.start(src.at[at, :], dst.at[at, :]))
    sum_ref[...] = jnp.concatenate([rows_sum(v) for v in sums] + [jnp.zeros((5, width), F32)], axis=0)
    wait_all(pending)


def second_part(scal, low, end_gain, end_shift, m_0, branch, e, pieces, tile=256):
    tokens, width = low.shape
    hidden = width
    sds = jax.ShapeDtypeStruct
    return pl.pallas_call(
        partial(second_kernel, tile),
        in_specs=[SMEM] + vmem_specs(3) + any_specs(11),
        out_specs=any_specs(4) + vmem_specs(1),
        out_shape=[
            in_hbm((tokens, width)), in_hbm((tokens, width), F32), in_hbm((tokens, width)),
            in_hbm((2, tokens, hidden)), sds((8, width), F32),
        ],
        scratch_shapes=[
            pltpu.VMEM((2, width, hidden), LOW), pltpu.VMEM((2 * hidden, width), LOW), pltpu.VMEM((tokens, width), LOW),
            pltpu.VMEM((tokens, width), F32),
            pltpu.VMEM((tokens, width), LOW), pltpu.VMEM((2, tokens, hidden), LOW), pltpu.VMEM((tokens, width), LOW),
            pltpu.VMEM((tokens, width), F32), pltpu.VMEM((tokens, width), LOW), pltpu.SemaphoreType.DMA((40,)),
        ],
        compiler_params=pltpu.CompilerParams(vmem_limit_bytes=48 * MIB),
        cost_estimate=pl.CostEstimate(
            flops=8 * tokens * width * hidden, bytes_accessed=14 * MIB, transcendentals=4 * tokens * hidden
        ),
        name="second_part",
    )(scal, end_gain, end_shift, *hbm(m_0, low, branch, e, *pieces))


def back_kernel(
    tile, scal, gain_ref, g_branch_in, mix_in, g_second_in, resid_in, slope_a, slope_b, m_0, m_1, m_2, m_3, up_in, down_in, *rest
):
    pieces = rest[:8]
    g_first_out, g_att_out, ctx_a_out, ctx_b_out, g_pre_out, sum_ref = rest[8:14]
    ups, downs, g_branch, mix_own, mix_got, slope, grad, resid, g_pre, g_att, g_ctx, sem = rest[14:]
    half = ups.shape[0] // 2
    size = ups.shape[2]
    go = Copies(sem)
    copies = own_copies(up_in, down_in, ups.at[:half], downs.at[: half * size])
    copies += got_copies(scal, pieces, ups.at[half:], downs.at[half * size :])
    slopes = [(s.at[j], slope.at[k * half + j]) for k, s in enumerate((slope_a, slope_b)) for j in range(half)]
    groups = []
    for k, (up, down) in enumerate(copies):
        groups += [down + [slopes[k]], up]
    groups[0] = [(g_branch_in, g_branch)] + groups[0]
    groups[1] = groups[1] + [(g_second_in, grad)]
    groups += [[(resid_in, resid), (mix_in, mix_own)] + mix_copies(scal, (m_0, m_1, m_2, m_3), mix_got)]
    stages = Stages(go, groups, 3)
    tokens = grad.shape[0]
    tiles = tokens // tile
    span = [slice(r * tile, (r + 1) * tile) for r in range(tiles)]
    order = [(j, r) for j in range(2 * half) for r in range(tiles)]
    pending = []

    def g_active(j, r):
        if r == 0:
            stages.need()
        return nt(g_branch[span[r], :], downs[j * size : (j + 1) * size, :])

    ahead = g_active(*order[0])
    for t, (j, r) in enumerate(order):
        value, ahead = ahead, (g_active(*order[t + 1]) if t + 1 < len(order) else None)
        if r == 0:
            stages.need()
        low = (value * slope[j, span[r], :].astype(F32)).astype(LOW)
        if j < half:
            g_pre[j, span[r], :] = low
            if r == tiles - 1:
                pending.append(go.start(g_pre.at[j], g_pre_out.at[j]))
        grad[span[r], :] += nt(low, ups[j])
    stages.need()
    gain = gain_ref[...].astype(F32)
    width = grad.shape[1]
    sums = tuple(jnp.zeros((8, width), F32) for _ in range(3))

    def norm(at, sums):
        unit, scaled = unit_norm(resid[at, :])
        e = grad[at, :]
        first = norm_back(e, unit, scaled, gain)
        grad[at, :] = first
        g_att[at, :] = first.astype(LOW)
        return tuple(a + fold(b) for a, b in zip(sums, (first, e * unit, e)))

    for r in range(tiles):
        sums = row_loop(r * tile, tile, ROWS, norm, sums)
        g_ctx[1, span[r], :] = nt(g_att[span[r], :], mix_got[...]).astype(LOW)
        g_ctx[0, span[r], :] = nt(g_att[span[r], :], mix_own[...]).astype(LOW)
        at = pl.ds(r * tile, tile)
        for src, dst in ((g_ctx.at[1], ctx_b_out), (g_ctx.at[0], ctx_a_out), (g_att, g_att_out), (grad, g_first_out)):
            pending.append(go.start(src.at[at, :], dst.at[at, :]))
    sum_ref[...] = jnp.concatenate([rows_sum(v) for v in sums] + [jnp.zeros((5, width), F32)], axis=0)
    wait_all(pending)


def back_part(scal, g_branch, gain, mix_own, g_second, resid, slopes, m_got, up, down, pieces, tile=256):
    tokens, width = g_branch.shape
    part = mix_own.shape[0]
    hidden = up.shape[1] // 2
    sds = jax.ShapeDtypeStruct
    return pl.pallas_call(
        partial(back_kernel, tile),
        in_specs=[SMEM] + vmem_specs(1) + any_specs(20),
        out_specs=any_specs(5) + vmem_specs(1),
        out_shape=[
            in_hbm((tokens, width), F32), in_hbm((tokens, width)), in_hbm((tokens, part)), in_hbm((tokens, part)),
            in_hbm((2, tokens, hidden)), sds((8, width), F32),
        ],
        scratch_shapes=[
            pltpu.VMEM((4, width, hidden), LOW), pltpu.VMEM((4 * hidden, width), LOW), pltpu.VMEM((tokens, width), LOW),
            pltpu.VMEM((part, width), LOW), pltpu.VMEM((part, width), LOW),
            pltpu.VMEM((4, tokens, hidden), LOW), pltpu.VMEM((tokens, width), F32), pltpu.VMEM((tokens, width), F32),
            pltpu.VMEM((2, tokens, hidden), LOW), pltpu.VMEM((tokens, width), LOW), pltpu.VMEM((2, tokens, part), LOW),
            pltpu.SemaphoreType.DMA((60,)),
        ],
        compiler_params=pltpu.CompilerParams(vmem_limit_bytes=50 * MIB),
        cost_estimate=pl.CostEstimate(flops=16 * tokens * width * hidden, bytes_accessed=24 * MIB, transcendentals=0),
        name="back_part",
    )(scal, gain, *hbm(g_branch, mix_own, g_second, resid, *slopes, *m_got, up, down, *pieces))


def weight_kernel(
    pick, bias_ref, act_in, g_pre_in, low_in, low_got_in, g_branch_in, g_branch_got_in, up_in, down_in, out, bias_out,
    act, g_pre, low, low_got, g_branch, g_branch_got, up, down, grads, sem,
):
    go = Copies(sem)
    width, hidden = up.shape
    at = pl.multiple_of(pick[0] * hidden, hidden)
    groups = [
        [(low_in, low), (g_pre_in.at[pick[0]], g_pre)],
        [(low_got_in, low_got), (up_in.at[:, pl.ds(at, hidden)], up)],
        [(g_branch_got_in, g_branch_got), (down_in.at[pl.ds(at, hidden), :], down)],
        [(act_in.at[pick[0]], act), (g_branch_in, g_branch)],
    ]
    stages = Stages(go, groups, 2)
    bias = bias_ref[...].astype(F32)
    stages.need()
    up_own = tn(low[...], g_pre[...])
    stages.need()
    pre = nn(low_got[...], up[...]) + jnp.where(pick[0] == 0, bias[0:1], bias[1:2])
    stages.need()
    g_active = nt(g_branch_got[...], down[...])
    active, incline = gelu_pair(pre)
    g_pre_got = g_active * incline
    bias_out[...] = rows_sum(g_pre_got) + rows_sum(g_pre[...].astype(F32))
    grads[:width, :] = (up_own + tn(low_got[...], g_pre_got.astype(LOW))).astype(LOW)
    first = go.start(grads.at[:width, :], out.at[:width, :])
    stages.need()
    grads[width:, :] = (tn(act[...], g_branch[...]) + tn(active.astype(LOW), g_branch_got[...])).astype(LOW)
    wait_all([go.start(grads.at[width:, :], out.at[width:, :]), first])


def weight_part(pick, act, g_pre, low, low_got, g_branch, g_branch_got, up, down, bias):
    _, tokens, hidden = act.shape
    width = low.shape[1]
    assert hidden == width
    token, square = pltpu.VMEM((tokens, width), LOW), pltpu.VMEM((width, hidden), LOW)
    return pl.pallas_call(
        weight_kernel,
        in_specs=[SMEM] + vmem_specs(1) + any_specs(8),
        out_specs=any_specs(1) + vmem_specs(1),
        out_shape=[in_hbm((width + hidden, width)), jax.ShapeDtypeStruct((1, hidden), F32)],
        scratch_shapes=[token] * 6 + [square] * 2 + [pltpu.VMEM((width + hidden, width), LOW), pltpu.SemaphoreType.DMA((10,))],
        compiler_params=pltpu.CompilerParams(vmem_limit_bytes=50 * MIB),
        cost_estimate=pl.CostEstimate(
            flops=12 * tokens * width * hidden, bytes_accessed=10 * MIB, transcendentals=2 * tokens * hidden
        ),
        name="weight_part",
    )(pick, bias, *hbm(act, g_pre, low, low_got, g_branch, g_branch_got, up, down))


def mix_grad_kernel(ctx_own, ctx_got, g_att, mid_sums, end_sums, own_out, got_out):
    own_out[...] = tn(ctx_own[...], g_att[...]).astype(LOW)
    part, width = own_out.shape
    got_out[:part, :] = tn(ctx_got[...], g_att[...]).astype(LOW)
    small = jnp.concatenate([mid_sums[:3, :], end_sums[:3, :], jnp.zeros((10, width), F32)], axis=0)
    got_out[part:, :] = small.astype(LOW)


def mix_grad(ctx_own, ctx_got, g_att, mid_sums, end_sums):
    tokens, width = g_att.shape
    part = ctx_own.shape[1]
    return pl.pallas_call(
        mix_grad_kernel,
        in_specs=vmem_specs(5),
        out_specs=vmem_specs(2),
        out_shape=[in_hbm((part, width)), in_hbm((part + 16, width))],
        compiler_params=pltpu.CompilerParams(vmem_limit_bytes=24 * MIB),
        cost_estimate=pl.CostEstimate(flops=4 * tokens * width * part, bytes_accessed=4 * MIB, transcendentals=0),
        name="mix_grad",
    )(*hbm(ctx_own, ctx_got, g_att), mid_sums, end_sums)


def late_kernel(
    scal, own_ref, got_ref, g_ref, mix_own, mix_other, mid_sums, end_sums, bias_keep, bias_send,
    keep_mine, keep_away, send_mine, send_away, out,
):
    half, width = own_ref.shape
    cols = g_ref.shape[1]
    out[:, :cols] = (tn(own_ref[...], g_ref[:half, :]) + tn(got_ref[...], g_ref[half:, :])).astype(LOW)
    part = mix_own.shape[0]
    for k in range(2):
        side = slice(k * part, (k + 1) * part)
        total = mix_own[:, side].astype(F32) + mix_other[:part, side].astype(F32)
        out[side, cols : cols + part] = total.astype(LOW)
    sums = nn(jnp.ones((8, 2 * half), LOW), g_ref[...])[:1]
    sums = jnp.concatenate([sums[:, :part], sums[:, 2 * part :]], axis=1)
    small = jnp.concatenate([mid_sums[:3, :], end_sums[:3, :]], axis=0) + mix_other[part : part + 6, :].astype(F32)
    first = scal[0] == 0
    ups = [jnp.where(first, bias_keep[...], bias_send[...]), jnp.where(first, bias_send[...], bias_keep[...])]
    rows = jnp.concatenate([small, *ups, sums, jnp.zeros((PAIR - 9, width), F32)], axis=0)
    out[:, cols + part :] = jnp.transpose(rows).astype(LOW)
    rows = part // 2
    for core, side, mine, away in ((scal[0], scal[1], keep_mine, keep_away), (1 - scal[0], scal[2], send_mine, send_away)):
        mine[...] = out[place(2 * core + side, rows), :]
        away[...] = out[place(2 * core + 1 - side, rows), :]


def late_grads(scal, own, got, g, mix_own, mix_other, sums):
    tokens, width = own.shape
    part = mix_own.shape[0]
    assert 2 * part == width
    cols = g.shape[1] + part + PAIR
    return pl.pallas_call(
        late_kernel,
        in_specs=[SMEM] + vmem_specs(9),
        out_specs=vmem_specs(4),
        out_shape=[in_hbm((part // 2, cols))] * 4,
        scratch_shapes=[pltpu.VMEM((width, cols), LOW)],
        compiler_params=pltpu.CompilerParams(vmem_limit_bytes=40 * MIB),
        cost_estimate=pl.CostEstimate(flops=4 * tokens * width * g.shape[1], bytes_accessed=8 * MIB, transcendentals=0),
        name="late_grads",
    )(scal, *hbm(own, got, g, mix_own, mix_other), *sums)


def finish_feed_kernel(scal, *refs):
    up_out, down_out = refs[4:]
    width = down_out.shape[2]
    for k in range(2):
        core, side = scal[0] ^ k, scal[1 + k]
        for n in range(2):
            piece = refs[2 * k + n][...].astype(F32)

            @pl.when(side == n)
            def _():
                up_out[:, pl.ds(pl.multiple_of(core * width, width), width)] = piece

            @pl.when(side != n)
            def _():
                down_out[core] = piece


def finish_feed(scal, pieces, steps=4):
    width = pieces[0].shape[1]
    rows = width // steps
    block = pl.BlockSpec((rows, width), lambda i, scal: (i, 0))
    up, down = pl.pallas_call(
        finish_feed_kernel,
        grid_spec=pltpu.PrefetchScalarGridSpec(
            num_scalar_prefetch=1,
            grid=(steps,),
            in_specs=[block] * 4,
            out_specs=[
                pl.BlockSpec((rows, 2 * width), lambda i, scal: (i, 0)),
                pl.BlockSpec((2, rows, width), lambda i, scal: (0, i, 0)),
            ],
        ),
        out_shape=[in_hbm((width, 2 * width), F32), in_hbm((2, width, width), F32)],
        compiler_params=pltpu.CompilerParams(vmem_limit_bytes=32 * MIB),
        cost_estimate=pl.CostEstimate(flops=0, bytes_accessed=14 * MIB, transcendentals=0),
        name="finish_feed",
    )(scal, *pieces)
    return up, down.reshape(2 * width, width)


def finish_late_kernel(scal, *refs):
    q_out, k_out, v_out, mix_out, *lines, small_out = refs[4:]
    part = q_out.shape[1]
    half = part // 2
    for k in range(2):
        core = scal[0] ^ k
        for n in range(2):
            side = scal[1 + k] ^ n
            piece = refs[2 * k + n]
            rows = pl.ds(pl.multiple_of(core * part + side * half, half), half)
            for m, out in enumerate((q_out, k_out, v_out)):
                out[rows, :] = piece[:, m * part : (m + 1) * part].astype(F32)
            some = pl.ds(pl.multiple_of(side * half, half), half)
            mix_out[some, pl.ds(pl.multiple_of(core * part, part), part)] = piece[:, 3 * part : 4 * part].astype(F32)
            small = jnp.transpose(piece[:, 4 * part :].astype(F32))[:16]
            for at in range(4):

                @pl.when(2 * core + side == at)
                def _():
                    small_out[:, at * half : (at + 1) * half] = small
    *norms, ups, q_bias, v_bias = lines
    for r, out in enumerate(norms):
        out[...] = small_out[r, :]
    width = 2 * part
    for k in range(2):
        ups[k * width : (k + 1) * width] = small_out[6 + k, :]
    q_bias[...] = small_out[8, :part]
    v_bias[...] = small_out[8, part:]


def finish_late(scal, pieces):
    part = 2 * pieces[0].shape[0]
    sds = jax.ShapeDtypeStruct
    return pl.pallas_call(
        finish_late_kernel,
        in_specs=[SMEM] + vmem_specs(4),
        out_specs=vmem_specs(13),
        out_shape=[in_hbm((2 * part, part), F32)] * 3
        + [in_hbm((part, 2 * part), F32)]
        + [sds((n,), F32) for n in [2 * part] * 6 + [4 * part, part, part]],
        scratch_shapes=[pltpu.VMEM((16, 2 * part), F32)],
        compiler_params=pltpu.CompilerParams(vmem_limit_bytes=32 * MIB),
        cost_estimate=pl.CostEstimate(flops=0, bytes_accessed=8 * MIB, transcendentals=0),
        name="finish_late",
    )(scal, *pieces)


def swap(value, axis, bit):
    even, odd = bit if isinstance(bit, tuple) else (bit, bit)
    return lax.ppermute(value, axis, [(i, i ^ (odd if i & 1 else even)) for i in range(lax.axis_size(axis))])


def wide(value):
    return value.astype(F32)


def cut(value, at, size):
    return lax.dynamic_slice_in_dim(value, at, size, 0)


def side_of(dp, mask):
    if isinstance(mask, tuple):
        mask = jnp.where(dp & 1, mask[1], mask[0])
    return ((dp & mask) != 0).astype(jnp.int32)


def dp_masks():
    return [1 << i for i in range(lax.axis_size("dp").bit_length() - 1)]


def total(terms):
    return sum(wide(t) for t in terms).astype(LOW)


class Chain:
    def __init__(self, dp, masks, terms, away=None):
        self.dp, self.masks, self.terms, self.away = dp, masks, terms, away
        self.step, self.value, self.sent, self.got = 0, None, None, None

    def start(self, *others):
        last = len(self.masks) - 1
        if self.step == 0 and self.away:
            mask = self.masks[0]
            self.sent = total(self.away)
        elif self.step < last:
            mask = self.masks[self.step]
            half, mine = self.terms[0].shape[0] // 2, side_of(self.dp, mask)
            self.sent = total([cut(t, (1 - mine) * half, half) for t in self.terms])
            self.terms = [cut(t, mine * half, half) for t in self.terms]
        elif self.step == last:
            mask = self.masks[last]
            self.sent = self.value = total(self.terms)
        else:
            mask = self.masks[2 * last - self.step]
            self.sent = self.value
        if others:
            self.sent = after(self.sent, *others)
        self.got = swap(self.sent, "dp", mask)

    def finish(self, *others):
        got = after(self.got, *others) if others else self.got
        last = len(self.masks) - 1
        if self.step < last:
            self.terms = self.terms + [got]
        elif self.step == last:
            self.value = (wide(self.value) + wide(got)).astype(LOW)
        elif self.step < 2 * last:
            side = side_of(self.dp, self.masks[2 * last - self.step])
            self.value = jnp.where(side == 1, jnp.concatenate([got, self.value]), jnp.concatenate([self.value, got]))
        self.step += 1
        self.got = got

    @property
    def done(self):
        return self.step == 2 * len(self.masks) - 1


def per_device(
    inputs, upstream, lengths, query_weight, key_weight, value_weight, query_bias, value_bias, mix_weight, mix_bias,
    mid_gain, mid_shift, up_weight, up_bias, down_weight, down_bias, end_gain, end_shift,
):
    dp = lax.axis_index("dp").astype(jnp.int32)
    side = lax.axis_index("tensor").astype(jnp.int32).reshape(1)
    masks = dp_masks()
    core = dp & 1
    order = [(masks[1], masks[2]), (masks[2], masks[1])] + masks[3:]
    scal = jnp.stack([core] + [side_of(dp, mask) for mask in order[:-1]])
    tokens, width = inputs.shape
    part = query_weight.shape[1]
    own_hidden = up_weight.shape[1]
    hidden = own_hidden // 2
    row = lambda v: v.reshape(1, -1)
    across = lambda v: swap(v, "tensor", 1)

    x_got = across(inputs)
    pairs = tuple(range(part // PAIR))
    qkv_weight = jnp.concatenate([query_weight, key_weight, value_weight], axis=1)
    qkv_bias = jnp.concatenate([wide(query_bias), jnp.zeros((part,), F32), wide(value_bias)])
    bias_own = up_bias.reshape(2, hidden)
    quarter = 2 * core + side_of(dp, order[0])
    m_piece = jnp.concatenate([cut(mix_weight, quarter * (part // 4), part // 4), bias_own, jnp.zeros((14, width), LOW)])
    eighth = 4 * core + 2 * side_of(dp, order[0]) + side_of(dp, order[1])
    up_piece = cut(up_weight, eighth * (width // 8), width // 8)
    down_piece = cut(down_weight, eighth * (own_hidden // 8), own_hidden // 8)
    piece = jnp.concatenate([up_piece[:, :hidden], up_piece[:, hidden:], down_piece])

    def project(v):
        return (nn(v, qkv_weight) + qkv_bias).astype(LOW)

    own = project(inputs)
    x_got = after(x_got, own, m_piece, piece)
    piece_0 = across(after(piece, x_got))
    got = project(x_got)
    ctx_own, ctx_send, lse = attend(lengths, side, own, got, pairs)
    ctx_send, piece_0 = lax.optimization_barrier((ctx_send, piece_0))
    ctx_got = across(ctx_send)
    m_0 = across(after(m_piece, ctx_send))
    m_1 = swap(m_0, "dp", order[0])
    m_got = [m_0, m_1, swap(m_0, "dp", 1), swap(m_1, "dp", 1)]
    piece_1 = swap(piece_0, "dp", order[0])
    piece_2, piece_3 = swap(piece_0, "dp", order[1]), swap(piece_1, "dp", order[1])
    resid, low, branch, act, slope_own = first_part(
        scal, ctx_own, ctx_got, inputs, mix_weight, [row(v) for v in (mix_bias, mid_gain, mid_shift, down_bias)], bias_own,
        m_got, up_weight, down_weight,
    )
    low_got = across(low)
    pieces = [piece_0, piece_1, after(piece_2, low), after(piece_3, low)]
    pieces += [swap(v, "dp", 1) for v in pieces]
    outputs, g_second, g_branch, slope_got, end_sums = second_part(
        scal, low, row(end_gain), row(end_shift), m_0, branch, upstream, pieces
    )
    g_branch_got = across(g_branch)
    g_first, g_att, g_ctx_own, g_ctx_send, g_pre, mid_sums = back_part(
        scal, g_branch, row(mid_gain), mix_weight, g_second, resid, (slope_own, slope_got),
        m_got, up_weight, down_weight, pieces,
    )
    g_ctx_got = across(g_ctx_send)
    mix_own, mix_send = mix_grad(ctx_own, ctx_got, after(g_att, low_got), mid_sums, end_sums)
    shared = (low, low_got, g_branch, g_branch_got, up_weight, down_weight, bias_own)
    send, bias_send = weight_part((1 - core).reshape(1), act, after(g_pre, mix_own), *shared)
    mix_other = across(after(mix_send, g_ctx_got))
    send = after(send, g_ctx_got)
    keep, bias_keep = weight_part(after(core.reshape(1), send), act, g_pre, *shared)
    feed = Chain(dp, order, [keep, swap(send, "dp", 1)])
    feed.start()
    g_qkv = attend_back(
        lengths, side, own, got, g_ctx_own, after(g_ctx_got, feed.sent), ctx_own, ctx_send, lse, pairs,
    )
    feed.finish(g_qkv)
    mix_other = after(mix_other, g_qkv)
    g_qkv = after(g_qkv, mix_other, feed.got)
    feed.start()
    keep_mine, keep_away, send_mine, send_away = late_grads(
        scal, inputs, x_got, g_qkv, mix_own, mix_other, (mid_sums, end_sums, bias_keep, bias_send)
    )
    feed.finish(keep_mine)
    away_got, mine_got = swap(after(send_away, feed.got), "dp", 1), swap(after(send_mine, feed.got), "dp", 1)
    proj = Chain(dp, order, [keep_mine, mine_got], [keep_away, away_got])
    proj.start()
    feed.start(proj.sent)
    input_got = across(nt(after(g_qkv, feed.sent)[tokens:], qkv_weight).astype(LOW))
    proj.finish(feed.sent)
    proj.start()
    proj.finish()
    feed.finish(proj.got)
    input_got = after(input_got, proj.got)
    proj.start(feed.got, input_got)
    input_own = g_first + nt(after(g_qkv, proj.sent)[:tokens], qkv_weight)
    input_grad = (input_own + wide(input_got)).astype(LOW)
    feed.start()
    proj.finish(feed.sent, input_grad)
    while not feed.done:
        proj.start()
        feed.finish(proj.sent)
        if not feed.done:
            feed.start()
            proj.finish(feed.sent)
    feed_pieces = [feed.value, feed.got]
    feed_pieces += [swap(v, "dp", 1) for v in feed_pieces]
    up_grad, down_grad = finish_feed(scal, feed_pieces)
    proj.finish(up_grad)
    assert proj.done
    late_pieces = [proj.value, proj.got]
    late_pieces += [swap(v, "dp", 1) for v in late_pieces]
    q_grad, k_grad, v_grad, mix_grads, *norms, up_bias_grad, q_bias_grad, v_bias_grad = finish_late(scal, late_pieces)
    return (
        outputs,
        input_grad,
        q_grad,
        k_grad,
        v_grad,
        q_bias_grad,
        v_bias_grad,
        mix_grads,
        *norms[:3],
        up_grad,
        up_bias_grad,
        down_grad,
        *norms[3:],
    )


def solution(mesh):
    placed = (
        P(("dp", "tensor"), None),
        P(("dp", "tensor"), None),
        P("dp", None),
        P(None, "tensor"),
        P(None, "tensor"),
        P(None, "tensor"),
        P("tensor"),
        P("tensor"),
        P("tensor", None),
        P(),
        P(),
        P(),
        P(None, "tensor"),
        P("tensor"),
        P("tensor", None),
        P(),
        P(),
        P(),
    )
    return jax.shard_map(
        per_device,
        mesh=mesh,
        in_specs=placed,
        out_specs=(
            P(("dp", "tensor"), None),
            P(("dp", "tensor"), None),
            P(None, "tensor"),
            P(None, "tensor"),
            P(None, "tensor"),
            P("tensor"),
            P("tensor"),
            P("tensor", None),
            P(),
            P(),
            P(),
            P(None, "tensor"),
            P("tensor"),
            P("tensor", None),
            P(),
            P(),
            P(),
        ),
        check_vma=False,
    )
```

```python
from functools import partial

import jax
import jax.numpy as jnp
from jax import lax
from jax.experimental import pallas as pl
from jax.experimental.pallas import tpu as pltpu
from jax.sharding import PartitionSpec as P

HEAD_DIM = 64
PAIR = 128
SEQ = 1024
LOW = jnp.bfloat16
F32 = jnp.float32
FAR = -1e30


def nt(a, b):
    return lax.dot_general(a, b, (((1,), (1,)), ((), ())), preferred_element_type=F32)


def tn(a, b):
    return lax.dot_general(a, b, (((0,), (0,)), ((), ())), preferred_element_type=F32)


def nn(a, b):
    return lax.dot_general(a, b, (((1,), (0,)), ((), ())), preferred_element_type=F32)


def seg_ends(len_ref):
    ends, total = [], jnp.int32(0)
    for j in range(len_ref.shape[1]):
        total = total + len_ref[0, j]
        ends.append(total)
    return ends


def seg_marks(ends, shift):
    pos = (lax.broadcasted_iota(jnp.int32, (SEQ, PAIR), 0) + shift) & (SEQ - 1)
    lane = lax.broadcasted_iota(jnp.int32, (SEQ, PAIR), 1) & (HEAD_DIM - 1)
    seg = jnp.zeros((SEQ, PAIR), jnp.int32)
    for e in ends:
        seg = seg + (pos >= e).astype(jnp.int32)
    own = seg == lane
    used = lane < len(ends)
    key_mark = jnp.where(own, 1.0, 0.0)
    query_mark = jnp.where(used & jnp.logical_not(own), FAR, 0.0)
    return key_mark, query_mark


def key_range(ends, first, size, step):
    begin, stop = jnp.int32(0), jnp.int32(SEQ)
    for e in ends:
        begin = jnp.where(e <= first, e, begin)
    for e in reversed(ends):
        stop = jnp.where(e >= first + size, e, stop)
    return (begin // step) * step, stop


def head_mask(h):
    lane = lax.broadcasted_iota(jnp.int32, (1, PAIR), 1)
    return (lane >= h * HEAD_DIM) & (lane < (h + 1) * HEAD_DIM)


def over_queries(ends, shift, bq, bk, step, body):
    most = -(-SEQ // bk)

    def one(t, _):
        q_at = pl.multiple_of(t * bq, bq)
        q_pos = (q_at + shift) & (SEQ - 1)
        begin, stop = key_range(ends, q_pos, bq, step)
        count = (stop - begin + bk - 1) // bk
        begin = jnp.minimum(begin, SEQ - count * bk)
        begin = pl.multiple_of(begin, step)
        for n in range(1, most + 1):

            @pl.when(count == n)
            def _():
                body(q_at, begin, n)

        return 0

    lax.fori_loop(0, SEQ // bq, one, 0)


def true_order(dst, src, shift):
    half = SEQ // 2
    dst[pl.ds(pl.multiple_of(shift, half), half), :] = src[:half]
    dst[pl.ds(pl.multiple_of(half - shift, half), half), :] = src[half:]


def both(own_ref, got_ref, at, pair):
    cols = slice(at + pair * PAIR, at + (pair + 1) * PAIR)
    return jnp.concatenate([own_ref[:, cols], got_ref[:, cols]], axis=0)


def attend_kernel(bq, bk, step, ahead, pairs, len_ref, side_ref, own_ref, got_ref, ctx_own, ctx_send, lse_ref, qh, kh, vt, acc, tot):
    shift = side_ref[0] * (SEQ // 2)
    half = SEQ // 2
    ends = seg_ends(len_ref)
    key_mark, query_mark = seg_marks(ends, shift)
    width = own_ref.shape[1] // 3
    heads = 2 * len(pairs)
    for p, pair in enumerate(pairs):
        cols = slice(p * PAIR, (p + 1) * PAIR)
        q = both(own_ref, got_ref, 0, pair).astype(F32) * 0.125
        k = both(own_ref, got_ref, width, pair).astype(F32)
        for h in range(2):
            qh[2 * p + h] = jnp.where(head_mask(h), q, query_mark).astype(LOW)
            true_order(kh.at[2 * p + h], jnp.where(head_mask(h), k, key_mark).astype(LOW), shift)
        vals = jnp.transpose(both(own_ref, got_ref, 2 * width, pair).astype(F32)).astype(LOW)
        vt[cols, pl.ds(pl.multiple_of(shift, half), half)] = vals[:, :half]
        vt[cols, pl.ds(pl.multiple_of(half - shift, half), half)] = vals[:, half:]

    def body(q_at, begin, n):
        qs = pl.ds(q_at, bq)
        at = [pl.ds(pl.multiple_of(begin + i * bk, step), bk) for i in range(n)]

        def score(h):
            query = qh[h, qs, :]
            return [nt(kh[h, at[i], :], query) for i in range(n)]

        ready = [score(h) for h in range(ahead)]
        for h in range(heads):
            dims = slice(h * HEAD_DIM, (h + 1) * HEAD_DIM)
            if h + ahead < heads:
                ready.append(score(h + ahead))
            parts = ready[h]
            top = jnp.max(parts[0], axis=0, keepdims=True)
            for s in parts[1:]:
                top = jnp.maximum(top, jnp.max(s, axis=0, keepdims=True))
            total, out = 0.0, 0.0
            for i, s in enumerate(parts):
                p = jnp.exp(s - top)
                total = total + jnp.sum(p, axis=0, keepdims=True)
                out = out + nn(vt[dims, at[i]], p.astype(LOW))
            acc[dims, qs] = out * (1.0 / total)
            tot[h : h + 1, qs] = top + jnp.log(total)

    over_queries(ends, shift, bq, bk, step, body)
    context = jnp.transpose(acc[...]).astype(LOW)
    ctx_own[...] = context[:half]
    ctx_send[...] = context[half:]
    lse_ref[...] = tot[...]


def attend(lengths, side, own, got, pairs, bq=256, bk=256, step=128, ahead=2):
    heads = 2 * len(pairs)
    width = heads * HEAD_DIM
    assert heads <= 8
    smem = pl.BlockSpec(memory_space=pltpu.SMEM)
    vmem = pl.BlockSpec(memory_space=pltpu.VMEM)
    return pl.pallas_call(
        partial(attend_kernel, bq, bk, step, ahead, pairs),
        in_specs=[smem, smem, vmem, vmem],
        out_specs=[vmem, vmem, vmem],
        out_shape=[
            jax.ShapeDtypeStruct((SEQ // 2, width), LOW),
            jax.ShapeDtypeStruct((SEQ // 2, width), LOW),
            jax.ShapeDtypeStruct((8, SEQ), F32),
        ],
        scratch_shapes=[
            pltpu.VMEM((heads, SEQ, PAIR), LOW),
            pltpu.VMEM((heads, SEQ, PAIR), LOW),
            pltpu.VMEM((width, SEQ), LOW),
            pltpu.VMEM((width, SEQ), F32),
            pltpu.VMEM((8, SEQ), F32),
        ],
        compiler_params=pltpu.CompilerParams(vmem_limit_bytes=32 * 1024 * 1024),
        name="attend",
    )(lengths, side, own, got)


def attend_back_kernel(
    bq, bk, step, ahead, pairs, len_ref, side_ref, own_ref, got_ref, do_own_ref, do_got_ref,
    ctx_own, ctx_send, lse_ref, g_ref, qh, qz, dom, kh, vals, kt, inner, dqt, dk, dv,
):
    shift = side_ref[0] * (SEQ // 2)
    half = SEQ // 2
    ends = seg_ends(len_ref)
    key_mark, query_mark = seg_marks(ends, shift)
    width = own_ref.shape[1] // 3
    heads = 2 * len(pairs)
    first = pl.ds(pl.multiple_of(shift, half), half)
    second = pl.ds(pl.multiple_of(half - shift, half), half)
    for p, pair in enumerate(pairs):
        cols = slice(p * PAIR, (p + 1) * PAIR)
        q = both(own_ref, got_ref, 0, pair).astype(F32) * 0.125
        k = both(own_ref, got_ref, width, pair).astype(F32)
        do = both(do_own_ref, do_got_ref, 0, pair).astype(F32)
        for h in range(2):
            mask = head_mask(h)
            at = 2 * p + h
            qh[at] = jnp.where(mask, q, query_mark).astype(LOW)
            qz[at] = jnp.where(mask, q, 0.0).astype(LOW)
            dom[at] = jnp.where(mask, do, 0.0).astype(LOW)
            true_order(kh.at[at], jnp.where(mask, k, key_mark).astype(LOW), shift)
        true_order(vals.at[p], both(own_ref, got_ref, 2 * width, pair), shift)
        turned = jnp.transpose(k).astype(LOW)
        kt[cols, first] = turned[:, :half]
        kt[cols, second] = turned[:, half:]
        prod = jnp.transpose(do * both(ctx_own, ctx_send, 0, p).astype(F32))
        for h in range(2):
            inner[2 * p + h : 2 * p + h + 1, :] = jnp.sum(
                prod[h * HEAD_DIM : (h + 1) * HEAD_DIM], axis=0, keepdims=True
            )
    dk[...] = jnp.zeros_like(dk)
    dv[...] = jnp.zeros_like(dv)

    def body(q_at, begin, n):
        qs = pl.ds(q_at, bq)
        at = [pl.ds(pl.multiple_of(begin + i * bk, step), bk) for i in range(n)]

        def score(h):
            query, grad = qh[h, qs, :], dom[h, qs, :]
            return [(nt(kh[h, at[i], :], query), nt(vals[h // 2, at[i], :], grad)) for i in range(n)]

        ready = [score(h) for h in range(ahead)]
        for h in range(heads):
            if h + ahead < heads:
                ready.append(score(h + ahead))
            dims = slice(h * HEAD_DIM, (h + 1) * HEAD_DIM)
            plain, grad = qz[h, qs, :], dom[h, qs, :]
            lse, mean = lse_ref[h : h + 1, qs], inner[h : h + 1, qs]
            out = 0.0
            for i, (s, gp) in enumerate(ready[h]):
                p = jnp.exp(s - lse)
                ds = (p * (gp - mean)).astype(LOW)
                dv[h // 2, at[i], :] += nn(p.astype(LOW), grad)
                dk[h // 2, at[i], :] += nn(ds, plain)
                out = out + nn(kt[dims, at[i]], ds)
            dqt[dims, qs] = out

    over_queries(ends, shift, bq, bk, step, body)
    part = heads * HEAD_DIM
    g_ref[:, :part] = (jnp.transpose(dqt[...]) * 0.125).astype(LOW)
    for p in range(heads // 2):
        for at, src in ((part + p * PAIR, dk), (2 * part + p * PAIR, dv)):
            g_ref[:half, at : at + PAIR] = src[p, first, :].astype(LOW)
            g_ref[half:, at : at + PAIR] = src[p, second, :].astype(LOW)


def attend_back(lengths, side, own, got, g_own, g_got, ctx_own, ctx_send, lse, pairs, bq=256, bk=256, step=128, ahead=1):
    heads = 2 * len(pairs)
    width = heads * HEAD_DIM
    smem = pl.BlockSpec(memory_space=pltpu.SMEM)
    vmem = pl.BlockSpec(memory_space=pltpu.VMEM)
    return pl.pallas_call(
        partial(attend_back_kernel, bq, bk, step, ahead, pairs),
        in_specs=[smem, smem] + [vmem] * 7,
        out_specs=vmem,
        out_shape=jax.ShapeDtypeStruct((SEQ, 3 * width), LOW),
        scratch_shapes=[
            pltpu.VMEM((heads, SEQ, PAIR), LOW),
            pltpu.VMEM((heads, SEQ, PAIR), LOW),
            pltpu.VMEM((heads, SEQ, PAIR), LOW),
            pltpu.VMEM((heads, SEQ, PAIR), LOW),
            pltpu.VMEM((heads // 2, SEQ, PAIR), LOW),
            pltpu.VMEM((width, SEQ), LOW),
            pltpu.VMEM((8, SEQ), F32),
            pltpu.VMEM((width, SEQ), F32),
            pltpu.VMEM((heads // 2, SEQ, PAIR), F32),
            pltpu.VMEM((heads // 2, SEQ, PAIR), F32),
        ],
        compiler_params=pltpu.CompilerParams(vmem_limit_bytes=48 * 1024 * 1024),
        name="attend_back",
    )(lengths, side, *(pltpu.with_memory_space_constraint(v, pltpu.HBM) for v in (own, got, g_own, g_got, ctx_own, ctx_send)), lse)


MIB = 1024 * 1024


def unit_norm(resid):
    middle = jnp.mean(resid, axis=-1, keepdims=True)
    centered = resid - middle
    spread = jnp.mean(centered * centered, axis=-1, keepdims=True)
    scaled = lax.rsqrt(spread + 1e-06)
    return centered * scaled, scaled


def norm_back(grad, unit, scaled, gain):
    weighted = grad * gain
    first_mean = jnp.mean(weighted, axis=-1, keepdims=True)
    second_mean = jnp.mean(weighted * unit, axis=-1, keepdims=True)
    return scaled * (weighted - first_mean - unit * second_mean)


def gelu_pair(v):
    cdf = 0.5 + 0.5 * lax.erf(v * 0.7071067811865476)
    bell = jnp.exp(-0.5 * (v * v))
    return v * cdf, cdf + (v * 0.3989422804014327) * bell


def rows_sum(v):
    return jnp.sum(v, axis=0, keepdims=True)


def after(value, *others):
    return lax.optimization_barrier((value, *others))[0]


def vmem_specs(count):
    return [pl.BlockSpec(memory_space=pltpu.VMEM)] * count


def any_specs(count):
    return [pl.BlockSpec(memory_space=pl.ANY)] * count


SMEM = pl.BlockSpec(memory_space=pltpu.SMEM)


def hbm(*arrays):
    return [pltpu.with_memory_space_constraint(v, pltpu.HBM) for v in arrays]


def in_hbm(shape, dtype=LOW):
    return pltpu.HBM(shape, dtype)


class Copies:
    def __init__(self, sem):
        self.sem, self.count = sem, 0

    def start(self, src, dst):
        copy = pltpu.make_async_copy(src, dst, self.sem.at[self.count])
        copy.start()
        self.count += 1
        return copy


def wait_all(copies):
    for copy in copies:
        copy.wait()


def eighths(scal):
    core, one, two = scal[0], scal[1], scal[2]
    order = []
    for c, a, b in ((core, one, two), (1 - core, two, one)):
        order += [4 * c + 2 * (a ^ (k & 1)) + (b ^ (k >> 1)) for k in range(4)]
    return order


def place(at, rows):
    return pl.ds(pl.multiple_of(at * rows, rows), rows)


class Stages:
    def __init__(self, go, groups, depth):
        self.go, self.groups, self.depth, self.next = go, groups, depth, 0
        self.running = []
        for _ in range(depth):
            self.begin()

    def begin(self):
        if len(self.running) < len(self.groups):
            self.running.append([self.go.start(src, dst) for src, dst in self.groups[len(self.running)]])

    def need(self):
        wait_all(self.running[self.next])
        self.next += 1
        self.begin()


def mix_copies(scal, pieces, dst):
    rows = dst.shape[0] // 4
    order = [2 * core + (side ^ k) for core, side in ((scal[0], scal[1]), (1 - scal[0], scal[2])) for k in range(2)]
    return [(src.at[:rows, :], dst.at[place(at, rows), :]) for src, at in zip(pieces, order)]


def own_copies(up, down, ups, downs):
    size = ups.shape[2]
    cols = [slice(k * size, (k + 1) * size) for k in range(ups.shape[0])]
    return [([(up.at[:, c], ups.at[k])], [(down.at[c, :], downs.at[c, :])]) for k, c in enumerate(cols)]


def got_copies(scal, pieces, ups, downs):
    order = eighths(scal)
    rows = ups.shape[1] // 8
    copies = []
    for k in range(ups.shape[0]):
        part = slice(k * rows, (k + 1) * rows)
        copies.append(([(src.at[part, :], ups.at[k, place(at, rows), :]) for src, at in zip(pieces, order)], []))
    first, rows = 2 * rows, downs.shape[0] // 8
    for src, at in zip(pieces, order):
        copies[0][1].append((src.at[first : first + rows, :], downs.at[place(at, rows), :]))
    return copies


def row_loop(first, count, step, body, carry=0):
    for at in range(first, first + count, step):
        carry = body(slice(at, at + step), carry)
    return carry


def fold(v):
    return jnp.sum(v.reshape(-1, 8, v.shape[-1]), axis=0)


ROWS = 128


def feed_chunks(tile, low, bias, ups, downs, need, branch, act, slope, done):
    tiles = low.shape[0] // tile
    size = ups.shape[2]
    span = [slice(r * tile, (r + 1) * tile) for r in range(tiles)]
    order = [(j, r) for j in range(ups.shape[0]) for r in range(tiles)]

    def pre(j, r):
        if r == 0:
            need()
        return nn(low[span[r], :], ups[j]) + bias(j)

    ahead = pre(*order[0])
    for t, (j, r) in enumerate(order):
        value, ahead = ahead, (pre(*order[t + 1]) if t + 1 < len(order) else None)
        active, incline = gelu_pair(value)
        active = active.astype(LOW)
        if act is not None:
            act[j, span[r], :] = active
        slope[j, span[r], :] = incline.astype(LOW)
        if r == 0:
            need()
        branch[span[r], :] += nn(active, downs[j * size : (j + 1) * size, :])
        if r == tiles - 1:
            done(j)


def first_kernel(
    tile, scal, mix_bias, gain_ref, shift_ref, down_bias, bias_ref, own_in, got_in, x_in, mix_in, m_0, m_1, m_2, m_3, up_in, down_in,
    resid_out, low_out, branch_out, act_out, slope_out,
    ctx_own, ctx_got, x_ref, mix_own, mix_got, ups, downs, resid, low, branch, act, slope, sem,
):
    go = Copies(sem)
    groups = [[(own_in, ctx_own), (mix_in, mix_own)], [(got_in, ctx_got)] + mix_copies(scal, (m_0, m_1, m_2, m_3), mix_got), [(x_in, x_ref)]]
    for up, down in own_copies(up_in, down_in, ups, downs):
        groups += [up, down]
    stages = Stages(go, groups, 3)
    gain, shift, offset, more = (r[...].astype(F32) for r in (gain_ref, shift_ref, mix_bias, down_bias))
    pending = []
    for r in range(x_ref.shape[0] // tile):
        rows = slice(r * tile, (r + 1) * tile)
        if r == 0:
            stages.need()
        attended = nn(ctx_own[rows, :], mix_own[...])
        if r == 0:
            stages.need()
        attended += nn(ctx_got[rows, :], mix_got[...])
        if r == 0:
            stages.need()
        resid[rows, :] = attended

        def norm(at, _):
            value = resid[at, :] + x_ref[at, :].astype(F32) + offset
            resid[at, :] = value
            normed = unit_norm(value)[0] * gain + shift
            low[at, :] = normed.astype(LOW)
            branch[at, :] = normed + more
            return 0

        row_loop(r * tile, tile, ROWS, norm)
    pending += [go.start(resid, resid_out), go.start(low, low_out)]

    def done(j):
        pending.extend([go.start(act.at[j], act_out.at[j]), go.start(slope.at[j], slope_out.at[j])])

    feed_chunks(
        tile, low, lambda j: bias_ref[j : j + 1, :].astype(F32), ups, downs, stages.need, branch, act, slope, done
    )
    pending.append(go.start(branch, branch_out))
    wait_all(pending)


def first_part(scal, ctx_own, ctx_got, x, mix_own, vecs, bias, m_got, up, down, tile=128):
    tokens, width = x.shape
    hidden = up.shape[1] // 2
    both_chunks = (2, tokens, hidden)
    return pl.pallas_call(
        partial(first_kernel, tile),
        in_specs=[SMEM] + vmem_specs(5) + any_specs(10),
        out_specs=any_specs(5),
        out_shape=[
            in_hbm((tokens, width), F32), in_hbm((tokens, width)), in_hbm((tokens, width), F32),
            in_hbm(both_chunks), in_hbm(both_chunks),
        ],
        scratch_shapes=[
            pltpu.VMEM(ctx_own.shape, LOW), pltpu.VMEM(ctx_own.shape, LOW), pltpu.VMEM((tokens, width), LOW),
            pltpu.VMEM(mix_own.shape, LOW), pltpu.VMEM(mix_own.shape, LOW),
            pltpu.VMEM((2, width, hidden), LOW), pltpu.VMEM((2 * hidden, width), LOW),
            pltpu.VMEM((tokens, width), F32), pltpu.VMEM((tokens, width), LOW), pltpu.VMEM((tokens, width), F32),
            pltpu.VMEM(both_chunks, LOW), pltpu.VMEM(both_chunks, LOW), pltpu.SemaphoreType.DMA((24,)),
        ],
        compiler_params=pltpu.CompilerParams(vmem_limit_bytes=48 * MIB),
        cost_estimate=pl.CostEstimate(
            flops=2 * tokens * width * (width + 4 * hidden), bytes_accessed=16 * MIB, transcendentals=4 * tokens * hidden
        ),
        name="first_part",
    )(scal, *vecs, bias, *hbm(ctx_own, ctx_got, x, mix_own, *m_got, up, down))


def second_kernel(
    tile, scal, down_gain, end_shift, m_0, low_in, branch_in, e_in, *rest,
):
    pieces = rest[:8]
    out_out, g_second_out, g_branch_out, slope_out, sum_ref = rest[8:13]
    ups, downs, low, branch, e_ref, slope, out, g_second, g_branch, sem = rest[13:]
    go = Copies(sem)
    (up_0, down), (up_1, _) = got_copies(scal, pieces, ups, downs)
    stages = Stages(go, [[(low_in, low)] + up_0, down + [(branch_in, branch)], up_1, [], [(e_in, e_ref)]], 2)
    pending = []
    bias_at = m_0.shape[0] - 16

    def done(j):
        pending.append(go.start(slope.at[j], slope_out.at[j]))

    feed_chunks(
        tile, low, lambda j: m_0[bias_at + j : bias_at + j + 1, :].astype(F32), ups, downs, stages.need, branch, None, slope, done
    )
    stages.need()
    gain, shift = down_gain[...].astype(F32), end_shift[...].astype(F32)
    width = branch.shape[1]
    sums = tuple(jnp.zeros((8, width), F32) for _ in range(3))

    def norm(at, sums):
        unit, scaled = unit_norm(branch[at, :])
        out[at, :] = (unit * gain + shift).astype(LOW)
        e = e_ref[at, :].astype(F32)
        grad = norm_back(e, unit, scaled, gain)
        g_second[at, :] = grad
        g_branch[at, :] = grad.astype(LOW)
        return tuple(a + fold(b) for a, b in zip(sums, (grad, e * unit, e)))

    half = branch.shape[0] // 2
    for r in range(2):
        sums = row_loop(r * half, half, ROWS, norm, sums)
        at = pl.ds(r * half, half)
        for src, dst in ((g_branch, g_branch_out), (g_second, g_second_out), (out, out_out)):
            pending.append(go.start(src.at[at, :], dst.at[at, :]))
    sum_ref[...] = jnp.concatenate([rows_sum(v) for v in sums] + [jnp.zeros((5, width), F32)], axis=0)
    wait_all(pending)


def second_part(scal, low, end_gain, end_shift, m_0, branch, e, pieces, tile=256):
    tokens, width = low.shape
    hidden = width
    sds = jax.ShapeDtypeStruct
    return pl.pallas_call(
        partial(second_kernel, tile),
        in_specs=[SMEM] + vmem_specs(3) + any_specs(11),
        out_specs=any_specs(4) + vmem_specs(1),
        out_shape=[
            in_hbm((tokens, width)), in_hbm((tokens, width), F32), in_hbm((tokens, width)),
            in_hbm((2, tokens, hidden)), sds((8, width), F32),
        ],
        scratch_shapes=[
            pltpu.VMEM((2, width, hidden), LOW), pltpu.VMEM((2 * hidden, width), LOW), pltpu.VMEM((tokens, width), LOW),
            pltpu.VMEM((tokens, width), F32),
            pltpu.VMEM((tokens, width), LOW), pltpu.VMEM((2, tokens, hidden), LOW), pltpu.VMEM((tokens, width), LOW),
            pltpu.VMEM((tokens, width), F32), pltpu.VMEM((tokens, width), LOW), pltpu.SemaphoreType.DMA((40,)),
        ],
        compiler_params=pltpu.CompilerParams(vmem_limit_bytes=48 * MIB),
        cost_estimate=pl.CostEstimate(
            flops=8 * tokens * width * hidden, bytes_accessed=14 * MIB, transcendentals=4 * tokens * hidden
        ),
        name="second_part",
    )(scal, end_gain, end_shift, *hbm(m_0, low, branch, e, *pieces))


def back_kernel(
    tile, scal, gain_ref, g_branch_in, mix_in, g_second_in, resid_in, slope_a, slope_b, m_0, m_1, m_2, m_3, up_in, down_in, *rest
):
    pieces = rest[:8]
    g_first_out, g_att_out, ctx_a_out, ctx_b_out, g_pre_out, sum_ref = rest[8:14]
    ups, downs, g_branch, mix_own, mix_got, slope, grad, resid, g_pre, g_att, g_ctx, sem = rest[14:]
    half = ups.shape[0] // 2
    size = ups.shape[2]
    go = Copies(sem)
    copies = own_copies(up_in, down_in, ups.at[:half], downs.at[: half * size])
    copies += got_copies(scal, pieces, ups.at[half:], downs.at[half * size :])
    slopes = [(s.at[j], slope.at[k * half + j]) for k, s in enumerate((slope_a, slope_b)) for j in range(half)]
    groups = []
    for k, (up, down) in enumerate(copies):
        groups += [down + [slopes[k]], up]
    groups[0] = [(g_branch_in, g_branch)] + groups[0]
    groups[1] = groups[1] + [(g_second_in, grad)]
    groups += [[(resid_in, resid), (mix_in, mix_own)] + mix_copies(scal, (m_0, m_1, m_2, m_3), mix_got)]
    stages = Stages(go, groups, 3)
    tokens = grad.shape[0]
    tiles = tokens // tile
    span = [slice(r * tile, (r + 1) * tile) for r in range(tiles)]
    order = [(j, r) for j in range(2 * half) for r in range(tiles)]
    pending = []

    def g_active(j, r):
        if r == 0:
            stages.need()
        return nt(g_branch[span[r], :], downs[j * size : (j + 1) * size, :])

    ahead = g_active(*order[0])
    for t, (j, r) in enumerate(order):
        value, ahead = ahead, (g_active(*order[t + 1]) if t + 1 < len(order) else None)
        if r == 0:
            stages.need()
        low = (value * slope[j, span[r], :].astype(F32)).astype(LOW)
        if j < half:
            g_pre[j, span[r], :] = low
            if r == tiles - 1:
                pending.append(go.start(g_pre.at[j], g_pre_out.at[j]))
        grad[span[r], :] += nt(low, ups[j])
    stages.need()
    gain = gain_ref[...].astype(F32)
    width = grad.shape[1]
    sums = tuple(jnp.zeros((8, width), F32) for _ in range(3))

    def norm(at, sums):
        unit, scaled = unit_norm(resid[at, :])
        e = grad[at, :]
        first = norm_back(e, unit, scaled, gain)
        grad[at, :] = first
        g_att[at, :] = first.astype(LOW)
        return tuple(a + fold(b) for a, b in zip(sums, (first, e * unit, e)))

    for r in range(tiles):
        sums = row_loop(r * tile, tile, ROWS, norm, sums)
        g_ctx[1, span[r], :] = nt(g_att[span[r], :], mix_got[...]).astype(LOW)
        g_ctx[0, span[r], :] = nt(g_att[span[r], :], mix_own[...]).astype(LOW)
        at = pl.ds(r * tile, tile)
        for src, dst in ((g_ctx.at[1], ctx_b_out), (g_ctx.at[0], ctx_a_out), (g_att, g_att_out), (grad, g_first_out)):
            pending.append(go.start(src.at[at, :], dst.at[at, :]))
    sum_ref[...] = jnp.concatenate([rows_sum(v) for v in sums] + [jnp.zeros((5, width), F32)], axis=0)
    wait_all(pending)


def back_part(scal, g_branch, gain, mix_own, g_second, resid, slopes, m_got, up, down, pieces, tile=256):
    tokens, width = g_branch.shape
    part = mix_own.shape[0]
    hidden = up.shape[1] // 2
    sds = jax.ShapeDtypeStruct
    return pl.pallas_call(
        partial(back_kernel, tile),
        in_specs=[SMEM] + vmem_specs(1) + any_specs(20),
        out_specs=any_specs(5) + vmem_specs(1),
        out_shape=[
            in_hbm((tokens, width), F32), in_hbm((tokens, width)), in_hbm((tokens, part)), in_hbm((tokens, part)),
            in_hbm((2, tokens, hidden)), sds((8, width), F32),
        ],
        scratch_shapes=[
            pltpu.VMEM((4, width, hidden), LOW), pltpu.VMEM((4 * hidden, width), LOW), pltpu.VMEM((tokens, width), LOW),
            pltpu.VMEM((part, width), LOW), pltpu.VMEM((part, width), LOW),
            pltpu.VMEM((4, tokens, hidden), LOW), pltpu.VMEM((tokens, width), F32), pltpu.VMEM((tokens, width), F32),
            pltpu.VMEM((2, tokens, hidden), LOW), pltpu.VMEM((tokens, width), LOW), pltpu.VMEM((2, tokens, part), LOW),
            pltpu.SemaphoreType.DMA((60,)),
        ],
        compiler_params=pltpu.CompilerParams(vmem_limit_bytes=50 * MIB),
        cost_estimate=pl.CostEstimate(flops=16 * tokens * width * hidden, bytes_accessed=24 * MIB, transcendentals=0),
        name="back_part",
    )(scal, gain, *hbm(g_branch, mix_own, g_second, resid, *slopes, *m_got, up, down, *pieces))


def weight_kernel(
    pick, bias_ref, act_in, g_pre_in, low_in, low_got_in, g_branch_in, g_branch_got_in, up_in, down_in, out, bias_out,
    act, g_pre, low, low_got, g_branch, g_branch_got, up, down, grads, sem,
):
    go = Copies(sem)
    width, hidden = up.shape
    at = pl.multiple_of(pick[0] * hidden, hidden)
    groups = [
        [(low_in, low), (g_pre_in.at[pick[0]], g_pre)],
        [(low_got_in, low_got), (up_in.at[:, pl.ds(at, hidden)], up)],
        [(g_branch_got_in, g_branch_got), (down_in.at[pl.ds(at, hidden), :], down)],
        [(act_in.at[pick[0]], act), (g_branch_in, g_branch)],
    ]
    stages = Stages(go, groups, 2)
    bias = bias_ref[...].astype(F32)
    stages.need()
    up_own = tn(low[...], g_pre[...])
    stages.need()
    pre = nn(low_got[...], up[...]) + jnp.where(pick[0] == 0, bias[0:1], bias[1:2])
    stages.need()
    g_active = nt(g_branch_got[...], down[...])
    active, incline = gelu_pair(pre)
    g_pre_got = g_active * incline
    bias_out[...] = rows_sum(g_pre_got) + rows_sum(g_pre[...].astype(F32))
    grads[:width, :] = (up_own + tn(low_got[...], g_pre_got.astype(LOW))).astype(LOW)
    first = go.start(grads.at[:width, :], out.at[:width, :])
    stages.need()
    grads[width:, :] = (tn(act[...], g_branch[...]) + tn(active.astype(LOW), g_branch_got[...])).astype(LOW)
    wait_all([go.start(grads.at[width:, :], out.at[width:, :]), first])


def weight_part(pick, act, g_pre, low, low_got, g_branch, g_branch_got, up, down, bias):
    _, tokens, hidden = act.shape
    width = low.shape[1]
    assert hidden == width
    token, square = pltpu.VMEM((tokens, width), LOW), pltpu.VMEM((width, hidden), LOW)
    return pl.pallas_call(
        weight_kernel,
        in_specs=[SMEM] + vmem_specs(1) + any_specs(8),
        out_specs=any_specs(1) + vmem_specs(1),
        out_shape=[in_hbm((width + hidden, width)), jax.ShapeDtypeStruct((1, hidden), F32)],
        scratch_shapes=[token] * 6 + [square] * 2 + [pltpu.VMEM((width + hidden, width), LOW), pltpu.SemaphoreType.DMA((10,))],
        compiler_params=pltpu.CompilerParams(vmem_limit_bytes=50 * MIB),
        cost_estimate=pl.CostEstimate(
            flops=12 * tokens * width * hidden, bytes_accessed=10 * MIB, transcendentals=2 * tokens * hidden
        ),
        name="weight_part",
    )(pick, bias, *hbm(act, g_pre, low, low_got, g_branch, g_branch_got, up, down))


def mix_grad_kernel(ctx_own, ctx_got, g_att, mid_sums, end_sums, own_out, got_out):
    own_out[...] = tn(ctx_own[...], g_att[...]).astype(LOW)
    part, width = own_out.shape
    got_out[:part, :] = tn(ctx_got[...], g_att[...]).astype(LOW)
    small = jnp.concatenate([mid_sums[:3, :], end_sums[:3, :], jnp.zeros((10, width), F32)], axis=0)
    got_out[part:, :] = small.astype(LOW)


def mix_grad(ctx_own, ctx_got, g_att, mid_sums, end_sums):
    tokens, width = g_att.shape
    part = ctx_own.shape[1]
    return pl.pallas_call(
        mix_grad_kernel,
        in_specs=vmem_specs(5),
        out_specs=vmem_specs(2),
        out_shape=[in_hbm((part, width)), in_hbm((part + 16, width))],
        compiler_params=pltpu.CompilerParams(vmem_limit_bytes=24 * MIB),
        cost_estimate=pl.CostEstimate(flops=4 * tokens * width * part, bytes_accessed=4 * MIB, transcendentals=0),
        name="mix_grad",
    )(*hbm(ctx_own, ctx_got, g_att), mid_sums, end_sums)


def late_kernel(
    scal, own_ref, got_ref, g_ref, mix_own, mix_other, mid_sums, end_sums, bias_keep, bias_send,
    keep_mine, keep_away, send_mine, send_away, out,
):
    half, width = own_ref.shape
    cols = g_ref.shape[1]
    out[:, :cols] = (tn(own_ref[...], g_ref[:half, :]) + tn(got_ref[...], g_ref[half:, :])).astype(LOW)
    part = mix_own.shape[0]
    for k in range(2):
        side = slice(k * part, (k + 1) * part)
        total = mix_own[:, side].astype(F32) + mix_other[:part, side].astype(F32)
        out[side, cols : cols + part] = total.astype(LOW)
    sums = nn(jnp.ones((8, 2 * half), LOW), g_ref[...])[:1]
    sums = jnp.concatenate([sums[:, :part], sums[:, 2 * part :]], axis=1)
    small = jnp.concatenate([mid_sums[:3, :], end_sums[:3, :]], axis=0) + mix_other[part : part + 6, :].astype(F32)
    first = scal[0] == 0
    ups = [jnp.where(first, bias_keep[...], bias_send[...]), jnp.where(first, bias_send[...], bias_keep[...])]
    rows = jnp.concatenate([small, *ups, sums, jnp.zeros((PAIR - 9, width), F32)], axis=0)
    out[:, cols + part :] = jnp.transpose(rows).astype(LOW)
    rows = part // 2
    for core, side, mine, away in ((scal[0], scal[1], keep_mine, keep_away), (1 - scal[0], scal[2], send_mine, send_away)):
        mine[...] = out[place(2 * core + side, rows), :]
        away[...] = out[place(2 * core + 1 - side, rows), :]


def late_grads(scal, own, got, g, mix_own, mix_other, sums):
    tokens, width = own.shape
    part = mix_own.shape[0]
    assert 2 * part == width
    cols = g.shape[1] + part + PAIR
    return pl.pallas_call(
        late_kernel,
        in_specs=[SMEM] + vmem_specs(9),
        out_specs=vmem_specs(4),
        out_shape=[in_hbm((part // 2, cols))] * 4,
        scratch_shapes=[pltpu.VMEM((width, cols), LOW)],
        compiler_params=pltpu.CompilerParams(vmem_limit_bytes=40 * MIB),
        cost_estimate=pl.CostEstimate(flops=4 * tokens * width * g.shape[1], bytes_accessed=8 * MIB, transcendentals=0),
        name="late_grads",
    )(scal, *hbm(own, got, g, mix_own, mix_other), *sums)


def finish_feed_kernel(scal, *refs):
    up_out, down_out = refs[4:]
    width = down_out.shape[2]
    for k in range(2):
        core, side = scal[0] ^ k, scal[1 + k]
        for n in range(2):
            piece = refs[2 * k + n][...].astype(F32)

            @pl.when(side == n)
            def _():
                up_out[:, pl.ds(pl.multiple_of(core * width, width), width)] = piece

            @pl.when(side != n)
            def _():
                down_out[core] = piece


def finish_feed(scal, pieces, steps=4):
    width = pieces[0].shape[1]
    rows = width // steps
    block = pl.BlockSpec((rows, width), lambda i, scal: (i, 0))
    up, down = pl.pallas_call(
        finish_feed_kernel,
        grid_spec=pltpu.PrefetchScalarGridSpec(
            num_scalar_prefetch=1,
            grid=(steps,),
            in_specs=[block] * 4,
            out_specs=[
                pl.BlockSpec((rows, 2 * width), lambda i, scal: (i, 0)),
                pl.BlockSpec((2, rows, width), lambda i, scal: (0, i, 0)),
            ],
        ),
        out_shape=[in_hbm((width, 2 * width), F32), in_hbm((2, width, width), F32)],
        compiler_params=pltpu.CompilerParams(vmem_limit_bytes=32 * MIB),
        cost_estimate=pl.CostEstimate(flops=0, bytes_accessed=14 * MIB, transcendentals=0),
        name="finish_feed",
    )(scal, *pieces)
    return up, down.reshape(2 * width, width)


def finish_late_kernel(scal, *refs):
    q_out, k_out, v_out, mix_out, *lines, small_out = refs[4:]
    part = q_out.shape[1]
    half = part // 2
    for k in range(2):
        core = scal[0] ^ k
        for n in range(2):
            side = scal[1 + k] ^ n
            piece = refs[2 * k + n]
            rows = pl.ds(pl.multiple_of(core * part + side * half, half), half)
            for m, out in enumerate((q_out, k_out, v_out)):
                out[rows, :] = piece[:, m * part : (m + 1) * part].astype(F32)
            some = pl.ds(pl.multiple_of(side * half, half), half)
            mix_out[some, pl.ds(pl.multiple_of(core * part, part), part)] = piece[:, 3 * part : 4 * part].astype(F32)
            small = jnp.transpose(piece[:, 4 * part :].astype(F32))[:16]
            for at in range(4):

                @pl.when(2 * core + side == at)
                def _():
                    small_out[:, at * half : (at + 1) * half] = small
    *norms, ups, q_bias, v_bias = lines
    for r, out in enumerate(norms):
        out[...] = small_out[r, :]
    width = 2 * part
    for k in range(2):
        ups[k * width : (k + 1) * width] = small_out[6 + k, :]
    q_bias[...] = small_out[8, :part]
    v_bias[...] = small_out[8, part:]


def finish_late(scal, pieces):
    part = 2 * pieces[0].shape[0]
    sds = jax.ShapeDtypeStruct
    return pl.pallas_call(
        finish_late_kernel,
        in_specs=[SMEM] + vmem_specs(4),
        out_specs=vmem_specs(13),
        out_shape=[in_hbm((2 * part, part), F32)] * 3
        + [in_hbm((part, 2 * part), F32)]
        + [sds((n,), F32) for n in [2 * part] * 6 + [4 * part, part, part]],
        scratch_shapes=[pltpu.VMEM((16, 2 * part), F32)],
        compiler_params=pltpu.CompilerParams(vmem_limit_bytes=32 * MIB),
        cost_estimate=pl.CostEstimate(flops=0, bytes_accessed=8 * MIB, transcendentals=0),
        name="finish_late",
    )(scal, *pieces)


def swap(value, axis, bit):
    even, odd = bit if isinstance(bit, tuple) else (bit, bit)
    return lax.ppermute(value, axis, [(i, i ^ (odd if i & 1 else even)) for i in range(lax.axis_size(axis))])


def wide(value):
    return value.astype(F32)


def cut(value, at, size):
    return lax.dynamic_slice_in_dim(value, at, size, 0)


def side_of(dp, mask):
    if isinstance(mask, tuple):
        mask = jnp.where(dp & 1, mask[1], mask[0])
    return ((dp & mask) != 0).astype(jnp.int32)


def dp_masks():
    return [1 << i for i in range(lax.axis_size("dp").bit_length() - 1)]


def total(terms):
    return sum(wide(t) for t in terms).astype(LOW)


class Chain:
    def __init__(self, dp, masks, terms, away=None):
        self.dp, self.masks, self.terms, self.away = dp, masks, terms, away
        self.step, self.value, self.sent, self.got = 0, None, None, None

    def start(self, *others):
        last = len(self.masks) - 1
        if self.step == 0 and self.away:
            mask = self.masks[0]
            self.sent = total(self.away)
        elif self.step < last:
            mask = self.masks[self.step]
            half, mine = self.terms[0].shape[0] // 2, side_of(self.dp, mask)
            self.sent = total([cut(t, (1 - mine) * half, half) for t in self.terms])
            self.terms = [cut(t, mine * half, half) for t in self.terms]
        elif self.step == last:
            mask = self.masks[last]
            self.sent = self.value = total(self.terms)
        else:
            mask = self.masks[2 * last - self.step]
            self.sent = self.value
        if others:
            self.sent = after(self.sent, *others)
        self.got = swap(self.sent, "dp", mask)

    def finish(self, *others):
        got = after(self.got, *others) if others else self.got
        last = len(self.masks) - 1
        if self.step < last:
            self.terms = self.terms + [got]
        elif self.step == last:
            self.value = (wide(self.value) + wide(got)).astype(LOW)
        elif self.step < 2 * last:
            side = side_of(self.dp, self.masks[2 * last - self.step])
            self.value = jnp.where(side == 1, jnp.concatenate([got, self.value]), jnp.concatenate([self.value, got]))
        self.step += 1
        self.got = got

    @property
    def done(self):
        return self.step == 2 * len(self.masks) - 1


def per_device(
    inputs, upstream, lengths, query_weight, key_weight, value_weight, query_bias, value_bias, mix_weight, mix_bias,
    mid_gain, mid_shift, up_weight, up_bias, down_weight, down_bias, end_gain, end_shift,
):
    dp = lax.axis_index("dp").astype(jnp.int32)
    side = lax.axis_index("tensor").astype(jnp.int32).reshape(1)
    masks = dp_masks()
    core = dp & 1
    order = [(masks[1], masks[2]), (masks[2], masks[1])] + masks[3:]
    scal = jnp.stack([core] + [side_of(dp, mask) for mask in order[:-1]])
    tokens, width = inputs.shape
    part = query_weight.shape[1]
    own_hidden = up_weight.shape[1]
    hidden = own_hidden // 2
    row = lambda v: v.reshape(1, -1)
    across = lambda v: swap(v, "tensor", 1)

    x_got = across(inputs)
    pairs = tuple(range(part // PAIR))
    qkv_weight = jnp.concatenate([query_weight, key_weight, value_weight], axis=1)
    qkv_bias = jnp.concatenate([wide(query_bias), jnp.zeros((part,), F32), wide(value_bias)])
    bias_own = up_bias.reshape(2, hidden)
    quarter = 2 * core + side_of(dp, order[0])
    m_piece = jnp.concatenate([cut(mix_weight, quarter * (part // 4), part // 4), bias_own, jnp.zeros((14, width), LOW)])
    eighth = 4 * core + 2 * side_of(dp, order[0]) + side_of(dp, order[1])
    up_piece = cut(up_weight, eighth * (width // 8), width // 8)
    down_piece = cut(down_weight, eighth * (own_hidden // 8), own_hidden // 8)
    piece = jnp.concatenate([up_piece[:, :hidden], up_piece[:, hidden:], down_piece])

    def project(v):
        return (nn(v, qkv_weight) + qkv_bias).astype(LOW)

    own = project(inputs)
    x_got = after(x_got, own, m_piece, piece)
    piece_0 = across(after(piece, x_got))
    got = project(x_got)
    ctx_own, ctx_send, lse = attend(lengths, side, own, got, pairs)
    ctx_send, piece_0 = lax.optimization_barrier((ctx_send, piece_0))
    ctx_got = across(ctx_send)
    m_0 = across(after(m_piece, ctx_send))
    m_1 = swap(m_0, "dp", order[0])
    m_got = [m_0, m_1, swap(m_0, "dp", 1), swap(m_1, "dp", 1)]
    piece_1 = swap(piece_0, "dp", order[0])
    piece_2, piece_3 = (swap(after(v, m_1), "dp", order[1]) for v in (piece_0, piece_1))
    resid, low, branch, act, slope_own = first_part(
        scal, ctx_own, ctx_got, inputs, mix_weight, [row(v) for v in (mix_bias, mid_gain, mid_shift, down_bias)], bias_own,
        m_got, up_weight, down_weight,
    )
    low_got = across(low)
    pieces = [piece_0, piece_1, after(piece_2, low), after(piece_3, low)]
    pieces += [swap(v, "dp", 1) for v in pieces]
    outputs, g_second, g_branch, slope_got, end_sums = second_part(
        scal, low, row(end_gain), row(end_shift), m_0, branch, upstream, pieces
    )
    g_branch_got = across(g_branch)
    g_first, g_att, g_ctx_own, g_ctx_send, g_pre, mid_sums = back_part(
        scal, g_branch, row(mid_gain), mix_weight, g_second, resid, (slope_own, slope_got),
        m_got, up_weight, down_weight, pieces,
    )
    g_ctx_got = across(g_ctx_send)
    mix_own, mix_send = mix_grad(ctx_own, ctx_got, after(g_att, low_got), mid_sums, end_sums)
    shared = (low, low_got, g_branch, g_branch_got, up_weight, down_weight, bias_own)
    send, bias_send = weight_part((1 - core).reshape(1), act, after(g_pre, mix_own), *shared)
    mix_other = across(after(mix_send, g_ctx_got))
    send = after(send, g_ctx_got)
    keep, bias_keep = weight_part(after(core.reshape(1), send), act, g_pre, *shared)
    feed = Chain(dp, order, [keep, swap(send, "dp", 1)])
    feed.start()
    g_qkv = attend_back(
        lengths, side, own, got, g_ctx_own, after(g_ctx_got, feed.sent), ctx_own, ctx_send, lse, pairs,
    )
    feed.finish(g_qkv)
    mix_other = after(mix_other, g_qkv)
    g_qkv = after(g_qkv, mix_other, feed.got)
    feed.start()
    keep_mine, keep_away, send_mine, send_away = late_grads(
        scal, inputs, x_got, g_qkv, mix_own, mix_other, (mid_sums, end_sums, bias_keep, bias_send)
    )
    feed.finish(keep_mine)
    away_got, mine_got = swap(after(send_away, feed.got), "dp", 1), swap(after(send_mine, feed.got), "dp", 1)
    proj = Chain(dp, order, [keep_mine, mine_got], [keep_away, away_got])
    proj.start()
    feed.start(proj.sent)
    input_got = across(nt(after(g_qkv, feed.sent)[tokens:], qkv_weight).astype(LOW))
    proj.finish(feed.sent)
    proj.start()
    proj.finish()
    feed.finish(proj.got)
    input_got = after(input_got, proj.got)
    proj.start(feed.got, input_got)
    input_own = g_first + nt(after(g_qkv, proj.sent)[:tokens], qkv_weight)
    input_grad = (input_own + wide(input_got)).astype(LOW)
    feed.start()
    proj.finish(feed.sent, input_grad)
    while not feed.done:
        proj.start()
        feed.finish(proj.sent)
        if not feed.done:
            feed.start()
            proj.finish(feed.sent)
    feed_pieces = [feed.value, feed.got]
    feed_pieces += [swap(v, "dp", 1) for v in feed_pieces]
    up_grad, down_grad = finish_feed(scal, feed_pieces)
    proj.finish(up_grad)
    assert proj.done
    late_pieces = [proj.value, proj.got]
    late_pieces += [swap(v, "dp", 1) for v in late_pieces]
    q_grad, k_grad, v_grad, mix_grads, *norms, up_bias_grad, q_bias_grad, v_bias_grad = finish_late(scal, late_pieces)
    return (
        outputs,
        input_grad,
        q_grad,
        k_grad,
        v_grad,
        q_bias_grad,
        v_bias_grad,
        mix_grads,
        *norms[:3],
        up_grad,
        up_bias_grad,
        down_grad,
        *norms[3:],
    )


def solution(mesh):
    placed = (
        P(("dp", "tensor"), None),
        P(("dp", "tensor"), None),
        P("dp", None),
        P(None, "tensor"),
        P(None, "tensor"),
        P(None, "tensor"),
        P("tensor"),
        P("tensor"),
        P("tensor", None),
        P(),
        P(),
        P(),
        P(None, "tensor"),
        P("tensor"),
        P("tensor", None),
        P(),
        P(),
        P(),
    )
    return jax.shard_map(
        per_device,
        mesh=mesh,
        in_specs=placed,
        out_specs=(
            P(("dp", "tensor"), None),
            P(("dp", "tensor"), None),
            P(None, "tensor"),
            P(None, "tensor"),
            P(None, "tensor"),
            P("tensor"),
            P("tensor"),
            P("tensor", None),
            P(),
            P(),
            P(),
            P(None, "tensor"),
            P("tensor"),
            P("tensor", None),
            P(),
            P(),
            P(),
        ),
        check_vma=False,
    )
```
